128 devices in a mesh: tok: 8 (over y_lo, x), chan: 16 (over z, y_hi, core).
Axes of the slice: x: 4, y: 4 (y_hi: 2, y_lo: 2; y = y_hi * 2 + y_lo), z: 4, core: 2. Of those that a mesh axis runs over, the one named last changes fastest.
Arguments:
- acts: bfloat16 [4096, 28672], P('tok', 'chan'), may hold values from -6 to 6
- target: bfloat16 [4096, 8192], P('tok', 'chan'), may hold values from -6 to 6
- proj_b: bfloat16 [2048, 28672], P(None, 'chan'), may hold values from -0.03125 to 0.03125
- proj_a: bfloat16 [8192, 2048], P('chan'), may hold values from -0.125 to 0.125
Outputs:
- grad_a: float32 [8192, 2048], P('chan', 'tok')
- grad_b: float32 [2048, 28672], P('tok', 'chan')
The draws below stay inside these ranges and needn't reach their ends.
All inputs are finite; a program needn't handle non-finite values.
Results may differ from the reference program's by a relative error of at most 0.004.
Values may be sent and summed in bfloat16 or wider, within the bound.
No kernel may reach another device: no remote copies, remote signals or barrier semaphores. Data moves between devices by JAX's collectives and lax.ppermute only.
A program may use at most 192 MiB of HBM per device.

```python
import jax
import jax.numpy as jnp
from jax import lax

IN = 28672
OUT = 8192
RANK = 2048
TOKENS = 4096


def block_levels(key, shape, pieces, least, largest):
    level, own = 1.0, jax.random.fold_in(key, 6)
    for position, shards_of in pieces:
        draws = jnp.exp(jax.random.uniform(jax.random.fold_in(own, position), (shards_of,), jnp.float32, least / len(pieces), largest / len(pieces)))
        level = level * jnp.repeat(draws, shape[position] // shards_of).reshape([-1 if axis == position else 1 for axis in range(len(shape))])
    return level


def bell_draw(stream_key, extent, spread, bound, cuts=(), dtype=jnp.bfloat16):
    factor_of = block_levels(stream_key, extent, cuts, -0.22, 0.18) if cuts else 1.0
    values = jax.random.normal(stream_key, extent, jnp.float32) * spread * factor_of
    return jnp.minimum(jnp.maximum(values, -bound), bound).astype(dtype)


def setup_inputs(seed: int = 0) -> dict:
    seeds = jax.random.split(jax.random.key(seed), 5)
    acts = bell_draw(seeds[0], (TOKENS, IN), 1.0, 6.0, ((0, 8), (1, 16)))
    target = bell_draw(seeds[1], (TOKENS, OUT), 1.0, 6.0, ((0, 8), (1, 16)))
    proj_b = bell_draw(seeds[2], (RANK, IN), IN ** -0.5, 0.03125, ((1, 16),))
    proj_a = bell_draw(seeds[3], (OUT, RANK), RANK ** -0.5, 0.125, ((0, 16),))
    return {"acts": acts, "target": target, "proj_b": proj_b, "proj_a": proj_a}


def reference(acts, target, proj_b, proj_a):
    codes = lax.dot_general(acts, proj_b, (((1,), (1,)), ((), ())), preferred_element_type=jnp.float32).astype(jnp.bfloat16)
    predicted = lax.dot_general(codes, proj_a, (((1,), (1,)), ((), ())), preferred_element_type=jnp.float32)
    residual = (target.astype(jnp.float32) - predicted).astype(jnp.bfloat16)
    grad_codes = jnp.dot(residual, proj_a, preferred_element_type=jnp.float32).astype(jnp.bfloat16)
    factor_scale = -2.0 / TOKENS
    grad_a = lax.dot_general(residual, codes, (((0,), (0,)), ((), ())), preferred_element_type=jnp.float32) * factor_scale
    grad_b = lax.dot_general(grad_codes, acts, (((0,), (0,)), ((), ())), preferred_element_type=jnp.float32) * factor_scale
    return grad_a, grad_b
```

```python
import jax
import jax.numpy as jnp
import numpy as np
from jax import lax
from jax.sharding import Mesh, PartitionSpec as P

BF, F32 = jnp.bfloat16, jnp.float32
TOK, CHAN, ZY = ("y_lo", "x"), ("z", "y_hi", "core"), ("z", "y_hi")


def shift(array, axis, size, step):
    return lax.ppermute(array, axis, [(i, (i + step) % size) for i in range(size)])


def swap(array, axis):
    return shift(array, axis, 2, 1)


def rows_dot(left, right):
    return lax.dot_general(left, right, (((1,), (1,)), ((), ())), preferred_element_type=F32)


def cols_dot(left, right):
    return lax.dot_general(left, right, (((0,), (0,)), ((), ())), preferred_element_type=F32)


def scatter_sum(partial, axes, parts):
    blocks = partial.astype(BF).reshape(parts, partial.shape[0] // parts, partial.shape[1])
    blocks = lax.all_to_all(blocks, axes, 0, 0)
    total = blocks[0].astype(F32)
    for i in range(1, parts):
        total = total + blocks[i].astype(F32)
    return total


def local(acts, target, proj_b, proj_a):
    core, y_lo, x = lax.axis_index("core"), lax.axis_index("y_lo"), lax.axis_index("x")
    tokens, rank = acts.shape[0], proj_b.shape[0]
    half = tokens // 2
    sub = half // 8
    width = rank // 8
    scale = -2.0 / (tokens * 8)

    def half_of(array, which):
        return lax.dynamic_slice_in_dim(array, which * half, half, 0)

    far = [shift(acts, "x", 4, k) for k in (1, 2, 3)]

    both_a = jnp.concatenate([proj_a, swap(proj_a, "core")], 0)
    both_t = jnp.concatenate([half_of(target, core), swap(half_of(target, 1 - core), "core")], 1)

    theirs = rows_dot(half_of(acts, 1 - core), proj_b)
    arrived = swap(theirs, "core")
    mine = rows_dot(half_of(acts, core), proj_b)
    mine = lax.optimization_barrier(mine) + arrived
    codes_sub = scatter_sum(mine, ZY, 8).astype(BF)
    codes = lax.all_to_all(jnp.broadcast_to(codes_sub[None], (8, sub, rank)), ZY, 0, 0).reshape(half, rank)

    residual = (both_t.astype(F32) - rows_dot(codes, both_a)).astype(BF)
    partial = jnp.dot(residual, both_a, preferred_element_type=F32)
    grad_sub = scatter_sum(partial, ZY, 8).astype(BF)

    split = grad_sub.reshape(sub, 2, 4, width)
    own = lax.dynamic_index_in_dim(split, y_lo, 1, False)
    other = lax.dynamic_index_in_dim(split, 1 - y_lo, 1, False)
    split = jnp.concatenate([own, other], 2).transpose(1, 0, 2)
    split = jnp.broadcast_to(split[:, None], (4, 8, sub, 2 * width)).reshape(32, sub, 2 * width)
    gathered = lax.all_to_all(split, ("x", "z", "y_hi"), 0, 0).reshape(4, half, 2 * width)
    gathered_o = swap(gathered, "core")
    first = core == 0
    grad_codes = jnp.stack(
        [jnp.where(first, gathered, gathered_o), jnp.where(first, gathered_o, gathered)], 1
    ).reshape(4, tokens, 2 * width)
    acts_all = jnp.concatenate([acts] + far, 0)
    grad_codes = jnp.concatenate(
        [lax.dynamic_index_in_dim(grad_codes, (x + 4 - k) % 4, 0, False) for k in range(4)], 0
    )
    away = cols_dot(grad_codes[:, width:], acts_all).astype(BF)
    away = swap(away, "y_lo")
    here = lax.optimization_barrier(cols_dot(grad_codes[:, :width], acts_all))
    grad_b = (here + away.astype(F32)) * scale

    outs = target.shape[1]
    codes_all = jnp.concatenate([codes, swap(codes, "core")], 0)
    residual_all = jnp.concatenate([residual[:, :outs], swap(residual[:, outs:], "core")], 0)
    term = cols_dot(codes_all, residual_all)
    grad_a = (scatter_sum(term, TOK, 8) * scale).T
    return (grad_a, grad_b)


def solution(mesh):
    fine = Mesh(np.reshape(mesh.devices, (2, 4, 4, 2, 2)), ("y_lo", "x", "z", "y_hi", "core"))
    return jax.shard_map(
        local,
        mesh=fine,
        in_specs=(P(TOK, CHAN), P(TOK, CHAN), P(None, CHAN), P(CHAN, None)),
        out_specs=(P(CHAN, TOK), P(TOK, CHAN)),
        check_vma=False,
    )
```

```python
import jax
import jax.numpy as jnp
import numpy as np
from jax import lax
from jax.sharding import Mesh, PartitionSpec as P

BF, F32 = jnp.bfloat16, jnp.float32
TOK, CHAN, ZY = ("y_lo", "x"), ("z", "y_hi", "core"), ("z", "y_hi")


def shift(array, axis, size, step):
    return lax.ppermute(array, axis, [(i, (i + step) % size) for i in range(size)])


def swap(array, axis):
    return shift(array, axis, 2, 1)


def rows_dot(left, right):
    return lax.dot_general(left, right, (((1,), (1,)), ((), ())), preferred_element_type=F32)


def cols_dot(left, right):
    return lax.dot_general(left, right, (((0,), (0,)), ((), ())), preferred_element_type=F32)


def pick(array, index, axis=0):
    return lax.dynamic_index_in_dim(array, index, axis, False)


def total(blocks):
    out = blocks[0].astype(F32)
    for i in range(1, blocks.shape[0]):
        out = out + blocks[i].astype(F32)
    return out


def local(acts, target, proj_b, proj_a):
    core, y_lo, x = lax.axis_index("core"), lax.axis_index("y_lo"), lax.axis_index("x")
    y_hi = lax.axis_index("y_hi")
    tokens, rank = acts.shape[0], proj_b.shape[0]
    outs = target.shape[1]
    half, sub, width = tokens // 2, tokens // 16, rank // 8
    scale = -2.0 / (tokens * 8)

    def half_of(array, which):
        return lax.dynamic_slice_in_dim(array, which * half, half, 0)

    cut = 1280
    mid = cut // 2
    near_a, near_b = acts[:, :cut], acts[:, cut:]
    plus_a, minus_a = shift(near_a, "x", 4, 1), shift(near_a, "x", 4, 3)

    def across(array):
        return lax.ppermute(array, ("y_lo", "y_hi"), [(0, 3), (3, 0), (1, 2), (2, 1)])

    across_a = across(proj_a)
    both_a = [proj_a, swap(proj_a, "core"), across_a, swap(across_a, "core")]
    both_a = jnp.concatenate(both_a, 0)
    wide_t = jnp.concatenate([half_of(target, core), swap(half_of(target, 1 - core), "core")], 1)
    wide_t = wide_t.reshape(4, 2, sub, 2 * outs)
    quarter_t = jnp.concatenate([pick(wide_t, y_hi, 1), swap(pick(wide_t, 1 - y_hi, 1), "y_hi")], 2)
    quarter_t = quarter_t.reshape(4 * sub, 4 * outs)

    theirs = rows_dot(half_of(acts, 1 - core), proj_b)
    arrived = swap(theirs, "core")
    mine = rows_dot(half_of(acts, core), proj_b)
    mine = lax.optimization_barrier(mine) + arrived
    blocks = lax.all_to_all(mine.astype(BF).reshape(8, sub, rank), ZY, 0, 0)
    blocks, plus_a, minus_a = lax.optimization_barrier((blocks, plus_a, minus_a))
    plus_b, minus_b = shift(near_b, "x", 4, 1), shift(near_b, "x", 4, 3)
    far_a = shift(plus_a[:, :mid], "x", 4, 1), shift(minus_a[:, mid:], "x", 4, 3)
    codes_sub = total(blocks).astype(BF)
    codes = lax.all_to_all(jnp.broadcast_to(codes_sub[None], (4, sub, rank)), "z", 0, 0)
    codes = codes.reshape(4 * sub, rank)

    residual = (quarter_t.astype(F32) - rows_dot(codes, both_a)).astype(BF)
    partial = jnp.dot(residual, both_a, preferred_element_type=F32)
    blocks = lax.all_to_all(partial.astype(BF).reshape(4, sub, rank), "z", 0, 0)
    blocks, plus_b, minus_b, far_a = lax.optimization_barrier((blocks, plus_b, minus_b, far_a))
    far_b = shift(plus_b[:, : plus_b.shape[1] // 2], "x", 4, 1), shift(minus_b[:, plus_b.shape[1] // 2 :], "x", 4, 3)
    grad_sub = total(blocks).astype(BF)

    far = jnp.concatenate(list(far_a) + list(far_b), 1)
    row = [acts, jnp.concatenate([plus_a, plus_b], 1), far, jnp.concatenate([minus_a, minus_b], 1)]
    acts_m = jnp.zeros((4, half, acts.shape[1]), BF)
    acts_o = acts_m
    for k in range(4):
        at = ((x + 4 - k) % 4, 0, 0)
        acts_m = lax.dynamic_update_slice(acts_m, half_of(row[k], core)[None], at)
        acts_o = lax.dynamic_update_slice(acts_o, half_of(row[k], 1 - core)[None], at)
    acts_m = acts_m.reshape(4 * half, -1)
    acts_o = acts_o.reshape(4 * half, -1)

    split = grad_sub.reshape(sub, 2, 4, width)
    split = jnp.stack([pick(split, y_lo, 1), pick(split, 1 - y_lo, 1)], 2).reshape(sub, 4, 2 * width)
    split = split.transpose(1, 0, 2)
    split = jnp.broadcast_to(split[:, None], (4, 8, sub, 2 * width)).reshape(32, sub, 2 * width)
    grad_m = lax.all_to_all(split, ("x", "z", "y_hi"), 0, 0).reshape(4 * half, 2 * width)
    grad_o = swap(grad_m, "core")
    away = lax.optimization_barrier(cols_dot(grad_m[:, width:], acts_m))
    away = (away + cols_dot(grad_o[:, width:], acts_o)).astype(BF)
    away = swap(away, "y_lo")
    here = lax.optimization_barrier(cols_dot(grad_m[:, :width], acts_m))
    here = lax.optimization_barrier(here + cols_dot(grad_o[:, :width], acts_o))
    grad_b = (here + away.astype(F32)) * scale

    codes_all = jnp.concatenate([codes, swap(codes, "y_hi")], 0)
    codes_all = jnp.concatenate([codes_all, swap(codes_all, "core")], 0)
    resid = jnp.concatenate([residual[:, : 2 * outs], swap(residual[:, 2 * outs :], "y_hi")], 0)
    resid = jnp.concatenate([resid[:, :outs], swap(resid[:, outs:], "core")], 0)
    term = cols_dot(codes_all, resid).reshape(2, 4 * width, outs)
    term_o = swap(pick(term, 1 - y_lo).astype(BF), "y_lo")
    term = (pick(term, y_lo) + term_o.astype(F32)).astype(BF).reshape(4, width, outs)
    grad_a = (total(lax.all_to_all(term, "x", 0, 0)) * scale).T
    return (grad_a, grad_b)


def solution(mesh):
    fine = Mesh(np.reshape(mesh.devices, (2, 4, 4, 2, 2)), ("y_lo", "x", "z", "y_hi", "core"))
    return jax.shard_map(
        local,
        mesh=fine,
        in_specs=(P(TOK, CHAN), P(TOK, CHAN), P(None, CHAN), P(CHAN, None)),
        out_specs=(P(CHAN, TOK), P(TOK, CHAN)),
        check_vma=False,
    )
```

```python
import functools

import jax
import jax.numpy as jnp
import numpy as np
from jax import lax
from jax.experimental import pallas as pl
from jax.experimental.pallas import tpu as pltpu
from jax.sharding import Mesh, PartitionSpec as P

BF, F32 = jnp.bfloat16, jnp.float32
TOK, CHAN, YZ, QUAD = ("y_lo", "x"), ("z", "y_hi", "core"), ("y_hi", "z"), ("y_hi", "core")
VMEM = pl.BlockSpec(memory_space=pltpu.VMEM)


def dot(left, right, left_dim=1, right_dim=0):
    return lax.dot_general(
        left, right, (((left_dim,), (right_dim,)), ((), ())), preferred_element_type=F32
    )


def shift(array, axis, size, step):
    return lax.ppermute(array, axis, [(i, (i + step) % size) for i in range(size)])


def swap(array, axis):
    return shift(array, axis, 2, 1)


def call(body, outs, *args, scratch=(), flops=0):
    moved = sum(a.size * a.dtype.itemsize for a in list(args) + list(outs))
    return pl.pallas_call(
        body,
        out_shape=outs if len(outs) > 1 else outs[0],
        in_specs=[VMEM] * len(args),
        out_specs=[VMEM] * len(outs) if len(outs) > 1 else VMEM,
        scratch_shapes=scratch,
        compiler_params=pltpu.CompilerParams(vmem_limit_bytes=48 * 1024 * 1024),
        cost_estimate=pl.CostEstimate(flops=flops, bytes_accessed=moved, transcendentals=0),
    )(*args)


def like(shape, dtype=BF):
    return jax.ShapeDtypeStruct(shape, dtype)


def total(ref, at=slice(None)):
    out = ref[0, at].astype(F32)
    for i in range(1, ref.shape[0]):
        out = out + ref[i, at].astype(F32)
    return out


def sum_and_copy(blocks, out):
    value = total(blocks).astype(BF)
    for i in range(out.shape[0]):
        out[i] = value


def residual_kernel(codes, near, far, a0, a1, a2, a3, message, partial, acc):
    y_hi, core = lax.axis_index("y_hi"), lax.axis_index("core")
    rank, outs = codes.shape[0], a0.shape[0]
    step = 256
    owners = (
        2 * y_hi + core,
        2 * y_hi + 1 - core,
        2 * (1 - y_hi) + core,
        2 * (1 - y_hi) + 1 - core,
    )
    for j, a in enumerate((a0, a1, a2, a3)):
        owner = owners[j]
        message[owner, :rank] = codes[...]
        for at in range(0, outs, step):
            rows = slice(at, at + step)
            target = (near if j < 2 else far)[j % 2, rows].astype(F32)
            left = target - dot(a[rows], codes[...])
            left = left.astype(BF)
            message[owner, rank + at : rank + at + step] = left
            term = dot(left, a[rows], 0, 0)
            if j == 0 and at == 0:
                acc[...] = term
            else:
                acc[...] += term
    sub = partial.shape[1]
    for z in range(partial.shape[0]):
        partial[z] = acc[z * sub : (z + 1) * sub].astype(BF)


def spread_kernel(blocks, out, held):
    y_lo = lax.axis_index("y_lo")
    held[...] = total(blocks).astype(BF)
    rank = held.shape[1]
    width = rank // 8
    for x in range(4):
        for side in range(2):
            start = (y_lo if side == 0 else 1 - y_lo) * (rank // 2) + x * width
            piece = held[:, pl.ds(pl.multiple_of(start, width), width)]
            for i in range(out.shape[1]):
                out[x, i, :, side * width : (side + 1) * width] = piece


def last_kernel(side, grad_m, grad_o, r0, r1, r2, r3, out, turned):
    core, x = lax.axis_index("core"), lax.axis_index("x")
    half, width = grad_m.shape[1], out.shape[0]
    at = slice(side * width, (side + 1) * width)
    tokens = 2 * half
    for k in range(4):
        row = lax.rem(x + 4 - k, 4)
        first = pl.multiple_of(core * half, half)
        other = pl.multiple_of((1 - core) * half, half)
        turned[k, :, pl.ds(first, half)] = grad_m[row, :, at].T
        turned[k, :, pl.ds(other, half)] = grad_o[row, :, at].T
    step = 256
    for c in range(0, out.shape[1], step):
        cols = slice(c, c + step)
        acc = dot(turned[0], r0[:, cols])
        for k, r in ((1, r1), (2, r2), (3, r3)):
            acc = acc + dot(turned[k], r[:, cols])
        out[:, cols] = acc.astype(out.dtype)


def term_kernel(message, out):
    rank = out.shape[0]
    outs = out.shape[1]
    step = 512
    for at in range(0, rank, step):
        acc = dot(message[0, at : at + step], message[0, rank:], 1, 1)
        for q in range(1, 4):
            acc = acc + dot(message[q, at : at + step], message[q, rank:], 1, 1)
        out[at : at + step] = acc.astype(BF)


def local(acts, target, proj_b, proj_a):
    core, y_hi = lax.axis_index("core"), lax.axis_index("y_hi")
    tokens, rank = acts.shape[0], proj_b.shape[0]
    outs, wide = target.shape[1], acts.shape[1]
    half, quarter, sub, width = tokens // 2, tokens // 4, tokens // 16, rank // 8
    scale = -2.0 / (tokens * 8)
    barrier = lax.optimization_barrier

    def part_of(array, which, size, axis):
        return lax.dynamic_slice_in_dim(array, which * size, size, axis)

    plus, minus = shift(acts, "x", 4, 1), shift(acts, "x", 4, 3)
    across_a = lax.ppermute(proj_a, ("y_lo", "y_hi"), [(0, 3), (3, 0), (1, 2), (2, 1)])
    pair_a = swap(proj_a, "core")
    target_t = target.T
    pair_t = swap(part_of(target_t, 1 - core, half, 1), "core")
    both_t = jnp.stack([part_of(target_t, core, half, 1), pair_t])
    near_t = part_of(both_t, y_hi, quarter, 2)
    far_t = swap(part_of(both_t, 1 - y_hi, quarter, 2), "y_hi")

    theirs = dot(proj_b, part_of(acts, 1 - core, half, 0), 1, 1)
    arrived = swap(theirs, "core")
    mine = barrier(dot(proj_b, part_of(acts, core, half, 0), 1, 1))
    mine = (mine + arrived).astype(BF).reshape(rank, 2, quarter).transpose(1, 0, 2).reshape(8, rank // 4, quarter)
    blocks = lax.all_to_all(mine, YZ, 0, 0)
    blocks, plus, minus, across_a, acts_2, far_t = barrier((blocks, plus, minus, across_a, acts, far_t))
    far = shift(acts_2, "x", 4, 2)
    pair_across = swap(across_a, "core")
    codes = call(sum_and_copy, [like((4, rank // 4, quarter))], blocks)
    codes = lax.all_to_all(codes, "z", 0, 0).reshape(rank, quarter)

    message, partial = call(
        residual_kernel,
        [like((4, rank + outs, quarter)), like((4, sub, rank))],
        codes, near_t, far_t, proj_a, pair_a, across_a, pair_across,
        scratch=[pltpu.VMEM((quarter, rank), F32)],
        flops=16 * quarter * rank * outs,
    )
    blocks = lax.all_to_all(partial, "z", 0, 0)
    blocks, far = barrier((blocks, far))
    message = lax.all_to_all(message, QUAD, 0, 0)

    split = call(spread_kernel, [like((4, 8, sub, 2 * width))], blocks, scratch=[pltpu.VMEM((sub, rank), BF)])
    split = split.reshape(32, sub, 2 * width)
    grad_m = lax.all_to_all(split, ("x", "y_hi", "z"), 0, 0).reshape(4, half, 2 * width)
    grad_o = swap(grad_m, "core")

    def last(side, dtype):
        return call(
            functools.partial(last_kernel, side),
            [like((width, wide), dtype)],
            grad_m, grad_o, acts, plus, far, minus,
            scratch=[pltpu.VMEM((4, width, tokens), BF)],
            flops=8 * tokens * width * wide,
        )

    away = swap(last(1, BF), "y_lo")
    grad_b = (last(0, F32) + away.astype(F32)) * scale

    term = call(term_kernel, [like((rank, outs))], message, flops=2 * tokens * rank * outs)
    term = lax.all_to_all(term.reshape(8, width, outs), TOK, 0, 0)
    sums = term[0].astype(F32)
    for i in range(1, 8):
        sums = sums + term[i].astype(F32)
    grad_a = (sums * scale).T
    return (grad_a, grad_b)


def solution(mesh):
    fine = Mesh(np.reshape(mesh.devices, (2, 4, 4, 2, 2)), ("y_lo", "x", "z", "y_hi", "core"))
    return jax.shard_map(
        local,
        mesh=fine,
        in_specs=(P(TOK, CHAN), P(TOK, CHAN), P(None, CHAN), P(CHAN, None)),
        out_specs=(P(CHAN, TOK), P(TOK, CHAN)),
        check_vma=False,
    )
```

```python
import functools

import jax
import jax.numpy as jnp
import numpy as np
from jax import lax
from jax.experimental import pallas as pl
from jax.experimental.pallas import tpu as pltpu
from jax.sharding import Mesh, PartitionSpec as P

BF, F32 = jnp.bfloat16, jnp.float32
TOK, CHAN, ZY = ("y_lo", "x"), ("z", "y_hi", "core"), ("z", "y_hi")
VMEM = pl.BlockSpec(memory_space=pltpu.VMEM)


def dot(left, right, left_dim=1, right_dim=0):
    return lax.dot_general(
        left, right, (((left_dim,), (right_dim,)), ((), ())), preferred_element_type=F32
    )


def shift(array, axis, size, step):
    return lax.ppermute(array, axis, [(i, (i + step) % size) for i in range(size)])


def swap(array, axis):
    return shift(array, axis, 2, 1)


def call(body, outs, *args, scratch=(), flops=0):
    moved = sum(a.size * a.dtype.itemsize for a in list(args) + list(outs))
    return pl.pallas_call(
        body,
        out_shape=outs if len(outs) > 1 else outs[0],
        in_specs=[VMEM] * len(args),
        out_specs=[VMEM] * len(outs) if len(outs) > 1 else VMEM,
        scratch_shapes=scratch,
        compiler_params=pltpu.CompilerParams(vmem_limit_bytes=48 * 1024 * 1024),
        cost_estimate=pl.CostEstimate(flops=flops, bytes_accessed=moved, transcendentals=0),
    )(*args)


def like(shape, dtype=BF):
    return jax.ShapeDtypeStruct(shape, dtype)


def total(ref, at=slice(None)):
    out = ref[0, at].astype(F32)
    for i in range(1, ref.shape[0]):
        out = out + ref[i, at].astype(F32)
    return out


def codes_kernel(other, acts, b, out, turned):
    core, half = lax.axis_index("core"), turned.shape[1]

    @pl.when(pl.program_id(0) == 0)
    def _():
        which = 1 - core if other else core
        turned[...] = acts[pl.ds(pl.multiple_of(which * half, half), half), :].T

    out[...] = dot(b[...], turned[...])


def codes_call(other, acts, proj_b):
    (tokens, wide), rank = acts.shape, proj_b.shape[0]
    half, step = tokens // 2, 512
    return pl.pallas_call(
        functools.partial(codes_kernel, other),
        grid=(rank // step,),
        out_shape=like((rank, half), F32),
        in_specs=[
            pl.BlockSpec((tokens, wide), lambda i: (0, 0)),
            pl.BlockSpec((step, wide), lambda i: (i, 0)),
        ],
        out_specs=pl.BlockSpec((step, half), lambda i: (i, 0)),
        scratch_shapes=[pltpu.VMEM((wide, half), BF)],
        compiler_params=pltpu.CompilerParams(vmem_limit_bytes=32 * 1024 * 1024),
        cost_estimate=pl.CostEstimate(
            flops=2 * rank * wide * half, bytes_accessed=2 * rank * wide, transcendentals=0
        ),
    )(acts, proj_b)


def sum_and_copy(blocks, out):
    value = total(blocks).astype(BF)
    for i in range(out.shape[0]):
        out[i] = value


def residual_kernel(codes, near, far, a0, a1, own, message, partial, held):
    rank, outs = codes.shape[0], a0.shape[0]
    step = 256
    for j, (target, a) in enumerate(((near, a0), (far, a1))):
        for at in range(0, outs, step):
            rows = slice(at, at + step)
            left = target[rows].astype(F32) - dot(a[rows], codes[...])
            left = left.astype(BF).T
            held[:, j * outs + at : j * outs + at + step] = left
            if j == 0:
                own[:, rows] = left
            else:
                message[rank + at : rank + at + step] = left
    message[:rank] = codes[...]
    sub = partial.shape[1]
    for at in range(0, rank, 512):
        cols = slice(at, at + 512)
        term = dot(held[:, :outs], a0[:, cols]) + dot(held[:, outs:], a1[:, cols])
        for i in range(partial.shape[0]):
            partial[i, :, cols] = term[i * sub : (i + 1) * sub].astype(BF)


def spread_kernel(blocks, out, held):
    y_lo = lax.axis_index("y_lo")
    held[...] = total(blocks).astype(BF)
    rank = held.shape[1]
    width = rank // 8
    for x in range(4):
        for side in range(2):
            start = (y_lo if side == 0 else 1 - y_lo) * (rank // 2) + x * width
            piece = held[:, pl.ds(pl.multiple_of(start, width), width)]
            for i in range(out.shape[1]):
                out[x, i, :, side * width : (side + 1) * width] = piece


def last_kernel(side, cuts, grad_m, grad_o, *refs):
    parts, out, turned = refs[:-2], refs[-2], refs[-1]
    core, x = lax.axis_index("core"), lax.axis_index("x")
    half, width = grad_m.shape[1], out.shape[0]
    at = slice(side * width, (side + 1) * width)
    for k in range(4):
        row = lax.rem(x + 4 - k, 4)
        first = pl.multiple_of(core * half, half)
        other = pl.multiple_of((1 - core) * half, half)
        turned[k, :, pl.ds(first, half)] = grad_m[row, :, at].T
        turned[k, :, pl.ds(other, half)] = grad_o[row, :, at].T
    step = 256
    for c in range(0, out.shape[1], step):
        acc = None
        for ref, (k, start) in zip(parts, cuts):
            if start <= c < start + ref.shape[1]:
                term = dot(turned[k], ref[:, c - start : c - start + step])
                acc = term if acc is None else acc + term
        out[:, c : c + step] = acc.astype(out.dtype)


def term_kernel(codes, own, message, out):
    rank, outs = out.shape
    for at in range(0, rank, 512):
        rows = slice(at, at + 512)
        for c in range(0, outs, 256):
            acc = dot(codes[rows], own[:, c : c + 256])
            acc = acc + dot(message[rows], message[rank + c : rank + c + 256])
            out[rows, c : c + 256] = acc.astype(BF)


def local(acts, target, proj_b, proj_a):
    core = lax.axis_index("core")
    tokens, rank = acts.shape[0], proj_b.shape[0]
    outs, wide = target.shape[1], acts.shape[1]
    half, sub, width = tokens // 2, tokens // 16, rank // 8
    scale = -2.0 / (tokens * 8)
    barrier = lax.optimization_barrier

    def part_of(array, which, size, axis):
        return lax.dynamic_slice_in_dim(array, which * size, size, axis)

    cut, low = 1280, 512
    plus_a, minus_a = shift(acts[:, :cut], "x", 4, 1), shift(acts[:, :cut], "x", 4, 3)
    pair_a = swap(proj_a, "core")
    target_t = target.T
    near_t = part_of(target_t, core, half, 1)
    pair_t = swap(part_of(target_t, 1 - core, half, 1), "core")

    theirs = codes_call(True, acts, proj_b)
    arrived = swap(theirs, "core")
    mine = codes_call(False, acts, proj_b)
    mine = (mine + arrived).astype(BF).reshape(8, width, half)
    blocks = lax.all_to_all(mine, ZY, 0, 0)
    blocks, plus_a, minus_a, acts_2 = barrier((blocks, plus_a, minus_a, acts))
    plus_b, minus_b = shift(acts_2[:, cut:], "x", 4, 1), shift(acts_2[:, cut:], "x", 4, 3)
    far_a = shift(acts_2[:, :low], "x", 4, 2)
    codes = call(sum_and_copy, [like((8, width, half))], blocks)
    codes = lax.all_to_all(codes, ZY, 0, 0).reshape(rank, half)

    own, message, partial = call(
        residual_kernel,
        [like((half, outs)), like((rank + outs, half)), like((8, sub, rank))],
        codes, near_t, pair_t, proj_a, pair_a,
        scratch=[pltpu.VMEM((half, 2 * outs), BF)],
        flops=8 * half * rank * outs,
    )
    partial, plus_b, minus_b, far_a, acts_3 = barrier((partial, plus_b, minus_b, far_a, acts_2))
    far_b = shift(acts_3[:, low:], "x", 4, 2)
    blocks = lax.all_to_all(partial, ZY, 0, 0)

    term = call(
        term_kernel, [like((rank, outs))], codes, own, swap(message, "core"), flops=2 * tokens * rank * outs
    )
    term = lax.all_to_all(term.reshape(8, width, outs), TOK, 0, 0)

    split = call(spread_kernel, [like((4, 8, sub, 2 * width))], blocks, scratch=[pltpu.VMEM((sub, rank), BF)])
    split = split.reshape(32, sub, 2 * width)
    grad_m = lax.all_to_all(split, ("x", "z", "y_hi"), 0, 0).reshape(4, half, 2 * width)
    grad_m, far_b, term = barrier((grad_m, far_b, term))
    grad_o = swap(grad_m, "core")
    parts = [acts, plus_a, plus_b, far_a, far_b, minus_a, minus_b]
    cuts = ((0, 0), (1, 0), (1, cut), (2, 0), (2, low), (3, 0), (3, cut))

    def last(side, dtype):
        return call(
            functools.partial(last_kernel, side, cuts),
            [like((width, wide), dtype)],
            grad_m, grad_o, *parts,
            scratch=[pltpu.VMEM((4, width, tokens), BF)],
            flops=8 * tokens * width * wide,
        )

    away = swap(last(1, BF), "y_lo")
    grad_b = (last(0, F32) + away.astype(F32)) * scale

    sums = term[0].astype(F32)
    for i in range(1, 8):
        sums = sums + term[i].astype(F32)
    grad_a = (sums * scale).T
    return (grad_a, grad_b)


def solution(mesh):
    fine = Mesh(np.reshape(mesh.devices, (2, 4, 4, 2, 2)), ("y_lo", "x", "z", "y_hi", "core"))
    return jax.shard_map(
        local,
        mesh=fine,
        in_specs=(P(TOK, CHAN), P(TOK, CHAN), P(None, CHAN), P(CHAN, None)),
        out_specs=(P(CHAN, TOK), P(TOK, CHAN)),
        check_vma=False,
    )
```

```python
import functools

import jax
import jax.numpy as jnp
import numpy as np
from jax import lax
from jax.experimental import pallas as pl
from jax.experimental.pallas import tpu as pltpu
from jax.sharding import Mesh, PartitionSpec as P

BF, F32 = jnp.bfloat16, jnp.float32
TOK, CHAN, ZY = ("y_lo", "x"), ("z", "y_hi", "core"), ("z", "y_hi")
VMEM = pl.BlockSpec(memory_space=pltpu.VMEM)


def dot(left, right, left_dim=1, right_dim=0):
    return lax.dot_general(
        left, right, (((left_dim,), (right_dim,)), ((), ())), preferred_element_type=F32
    )


def shift(array, axis, size, step):
    return lax.ppermute(array, axis, [(i, (i + step) % size) for i in range(size)])


def swap(array, axis):
    return shift(array, axis, 2, 1)


def call(body, outs, *args, scratch=(), flops=0):
    moved = sum(a.size * a.dtype.itemsize for a in list(args) + list(outs))
    return pl.pallas_call(
        body,
        out_shape=outs if len(outs) > 1 else outs[0],
        in_specs=[VMEM] * len(args),
        out_specs=[VMEM] * len(outs) if len(outs) > 1 else VMEM,
        scratch_shapes=scratch,
        compiler_params=pltpu.CompilerParams(vmem_limit_bytes=16 * 1024 * 1024),
        cost_estimate=pl.CostEstimate(flops=flops, bytes_accessed=moved, transcendentals=0),
    )(*args)


def like(shape, dtype=BF):
    return jax.ShapeDtypeStruct(shape, dtype)


def total(ref, at=slice(None)):
    out = ref[0, at].astype(F32)
    for i in range(1, ref.shape[0]):
        out = out + ref[i, at].astype(F32)
    return out


def codes_kernel(other, acts, b, out, turned):
    core, half = lax.axis_index("core"), turned.shape[1]

    @pl.when(pl.program_id(0) == 0)
    def _():
        which = 1 - core if other else core
        turned[...] = acts[pl.ds(pl.multiple_of(which * half, half), half), :].T

    out[...] = dot(b[...], turned[...])


def codes_call(other, acts, proj_b):
    (tokens, wide), rank = acts.shape, proj_b.shape[0]
    half, step = tokens // 2, 512
    return pl.pallas_call(
        functools.partial(codes_kernel, other),
        grid=(rank // step,),
        out_shape=like((rank, half), F32),
        in_specs=[
            pl.BlockSpec((tokens, wide), lambda i: (0, 0)),
            pl.BlockSpec((step, wide), lambda i: (i, 0)),
        ],
        out_specs=pl.BlockSpec((step, half), lambda i: (i, 0)),
        scratch_shapes=[pltpu.VMEM((wide, half), BF)],
        compiler_params=pltpu.CompilerParams(vmem_limit_bytes=60 * 1024 * 1024),
        cost_estimate=pl.CostEstimate(
            flops=2 * rank * wide * half, bytes_accessed=2 * rank * wide, transcendentals=0
        ),
    )(acts, proj_b)


def sum_and_copy(blocks, out):
    value = total(blocks).astype(BF)
    for i in range(out.shape[0]):
        out[i] = value


def residual_kernel(codes, near, far, a0, a1, own, message, partial, held):
    rank, outs = codes.shape[0], a0.shape[0]
    step = 256
    for j, (target, a) in enumerate(((near, a0), (far, a1))):
        for at in range(0, outs, step):
            rows = slice(at, at + step)
            left = target[rows].astype(F32) - dot(a[rows], codes[...])
            left = left.astype(BF).T
            held[:, j * outs + at : j * outs + at + step] = left
            if j == 0:
                own[:, rows] = left
            else:
                message[rank + at : rank + at + step] = left
    message[:rank] = codes[...]
    sub = partial.shape[1]
    for at in range(0, rank, 512):
        cols = slice(at, at + 512)
        term = dot(held[:, :outs], a0[:, cols]) + dot(held[:, outs:], a1[:, cols])
        for i in range(partial.shape[0]):
            partial[i, :, cols] = term[i * sub : (i + 1) * sub].astype(BF)


def spread_kernel(blocks, out, held):
    y_lo = lax.axis_index("y_lo")
    held[...] = total(blocks).astype(BF)
    rank = held.shape[1]
    width = rank // 8
    for x in range(4):
        for side in range(2):
            start = (y_lo if side == 0 else 1 - y_lo) * (rank // 2) + x * width
            piece = held[:, pl.ds(pl.multiple_of(start, width), width)]
            for i in range(out.shape[1]):
                out[x, i, :, side * width : (side + 1) * width] = piece


def last_kernel(side, cuts, other, more, grad, *refs):
    parts = refs[: len(cuts)]
    before = refs[len(cuts) : len(cuts) + more]
    out, turned = refs[-2:]
    core, x = lax.axis_index("core"), lax.axis_index("x")
    half, width = grad.shape[1], out.shape[0]
    which = 1 - core if other else core
    rows = pl.ds(pl.multiple_of(which * half, half), half)
    for k in range(4):
        turned[k] = grad[lax.rem(x + 4 - k, 4), :, side * width : (side + 1) * width].T
    step = 256
    for c in range(0, out.shape[1], step):
        acc = before[0][:, c : c + step] if more else None
        for ref, (k, start) in zip(parts, cuts):
            if start <= c < start + ref.shape[1]:
                term = dot(turned[k], ref[rows, c - start : c - start + step])
                acc = term if acc is None else acc + term
        out[:, c : c + step] = acc.astype(out.dtype)


def term_kernel(codes, own, message, keep, send):
    y_lo = lax.axis_index("y_lo")
    rank, outs = codes.shape[0], keep.shape[1]
    for out, which in ((send, 1 - y_lo), (keep, y_lo)):
        for at in range(0, rank // 2, 512):
            rows = pl.ds(pl.multiple_of(which * (rank // 2) + at, 512), 512)
            left, right = codes[rows, :], message[rows, :]
            for c in range(0, outs, 256):
                acc = dot(left, own[:, c : c + 256])
                acc = acc + dot(right, message[rank + c : rank + c + 256])
                out[at : at + 512, c : c + 256] = acc.astype(out.dtype)


def local(acts, target, proj_b, proj_a):
    core = lax.axis_index("core")
    tokens, rank = acts.shape[0], proj_b.shape[0]
    outs, wide = target.shape[1], acts.shape[1]
    half, sub, width = tokens // 2, tokens // 16, rank // 8
    scale = -2.0 / (tokens * 8)
    barrier = lax.optimization_barrier

    def part_of(array, which, size, axis):
        return lax.dynamic_slice_in_dim(array, which * size, size, axis)

    cut, low = 1024, 1024
    plus_a, minus_a = shift(acts[:, :cut], "x", 4, 1), shift(acts[:, :cut], "x", 4, 3)
    pair_a = swap(proj_a, "core")
    target_t = target.T
    near_t = part_of(target_t, core, half, 1)
    pair_t = swap(part_of(target_t, 1 - core, half, 1), "core")

    theirs = codes_call(True, acts, proj_b)
    arrived = swap(theirs, "core")
    mine = codes_call(False, acts, proj_b)
    mine = (mine + arrived).astype(BF).reshape(8, width, half)
    blocks = lax.all_to_all(mine, ZY, 0, 0)
    blocks, plus_a, minus_a, acts_2 = barrier((blocks, plus_a, minus_a, acts))
    plus_b, minus_b = shift(acts_2[:, cut:], "x", 4, 1), shift(acts_2[:, cut:], "x", 4, 3)
    far_a = shift(acts_2[:, :low], "x", 4, 2)
    codes = call(sum_and_copy, [like((8, width, half))], blocks)
    codes = lax.all_to_all(codes, ZY, 0, 0).reshape(rank, half)

    own, message, partial = call(
        residual_kernel,
        [like((half, outs)), like((rank + outs, half)), like((8, sub, rank))],
        codes, near_t, pair_t, proj_a, pair_a,
        scratch=[pltpu.VMEM((half, 2 * outs), BF)],
        flops=8 * half * rank * outs,
    )
    partial, plus_b, minus_b, far_a, acts_3 = barrier((partial, plus_b, minus_b, far_a, acts_2))
    far_b = shift(acts_3[:, low:], "x", 4, 2)
    blocks = lax.all_to_all(partial, ZY, 0, 0)

    keep, send = call(
        term_kernel,
        [like((rank // 2, outs), F32), like((rank // 2, outs))],
        codes, own, swap(message, "core"),
        flops=2 * tokens * rank * outs,
    )
    blocks, far_b, keep, send = barrier((blocks, far_b, keep, send))
    send = swap(send, "y_lo")

    split = call(spread_kernel, [like((4, 8, sub, 2 * width))], blocks, scratch=[pltpu.VMEM((sub, rank), BF)])
    split = split.reshape(32, sub, 2 * width)
    grad_m = lax.all_to_all(split, ("x", "z", "y_hi"), 0, 0).reshape(4, half, 2 * width)
    grad_m, send = barrier((grad_m, send))
    term = (keep + send.astype(F32)).astype(BF).reshape(4, width, outs)
    grad_o = swap(grad_m, "core")
    parts = [acts, plus_a, plus_b, far_a, far_b, minus_a, minus_b]
    cuts = ((0, 0), (1, 0), (1, cut), (2, 0), (2, low), (3, 0), (3, cut))

    def last(side, other, dtype, *before):
        return call(
            functools.partial(last_kernel, side, cuts, other, len(before)),
            [like((width, wide), dtype)],
            grad_o if other else grad_m, *parts, *before,
            scratch=[pltpu.VMEM((4, width, half), BF)],
            flops=8 * half * width * wide,
        )

    away = swap(last(1, True, BF, last(1, False, F32)), "y_lo")
    here = last(0, True, F32, last(0, False, F32))
    grad_b = (here + away.astype(F32)) * scale

    term = lax.all_to_all(term, "x", 0, 0)
    sums = term[0].astype(F32)
    for i in range(1, 4):
        sums = sums + term[i].astype(F32)
    grad_a = (sums * scale).T
    return (grad_a, grad_b)


def solution(mesh):
    fine = Mesh(np.reshape(mesh.devices, (2, 4, 4, 2, 2)), ("y_lo", "x", "z", "y_hi", "core"))
    return jax.shard_map(
        local,
        mesh=fine,
        in_specs=(P(TOK, CHAN), P(TOK, CHAN), P(None, CHAN), P(CHAN, None)),
        out_specs=(P(CHAN, TOK), P(TOK, CHAN)),
        check_vma=False,
    )
```

```python
import functools

import jax
import jax.numpy as jnp
import numpy as np
from jax import lax
from jax.experimental import pallas as pl
from jax.experimental.pallas import tpu as pltpu
from jax.sharding import Mesh, PartitionSpec as P

BF, F32 = jnp.bfloat16, jnp.float32
TOK, CHAN, ZY = ("y_lo", "x"), ("z", "y_hi", "core"), ("z", "y_hi")
VMEM = pl.BlockSpec(memory_space=pltpu.VMEM)


def dot(left, right, left_dim=1, right_dim=0):
    return lax.dot_general(
        left, right, (((left_dim,), (right_dim,)), ((), ())), preferred_element_type=F32
    )


def shift(array, axis, size, step):
    return lax.ppermute(array, axis, [(i, (i + step) % size) for i in range(size)])


def swap(array, axis):
    return shift(array, axis, 2, 1)


def call(body, outs, *args, scratch=(), flops=0):
    moved = sum(a.size * a.dtype.itemsize for a in list(args) + list(outs))
    return pl.pallas_call(
        body,
        out_shape=outs if len(outs) > 1 else outs[0],
        in_specs=[VMEM] * len(args),
        out_specs=[VMEM] * len(outs) if len(outs) > 1 else VMEM,
        scratch_shapes=scratch,
        compiler_params=pltpu.CompilerParams(vmem_limit_bytes=16 * 1024 * 1024),
        cost_estimate=pl.CostEstimate(flops=flops, bytes_accessed=moved, transcendentals=0),
    )(*args)


def like(shape, dtype=BF):
    return jax.ShapeDtypeStruct(shape, dtype)


def total(ref, at=slice(None)):
    out = ref[0, at].astype(F32)
    for i in range(1, ref.shape[0]):
        out = out + ref[i, at].astype(F32)
    return out


def codes_kernel(other, acts, b, out, turned):
    core, half = lax.axis_index("core"), turned.shape[1]

    @pl.when(pl.program_id(0) == 0)
    def _():
        which = 1 - core if other else core
        turned[...] = acts[pl.ds(pl.multiple_of(which * half, half), half), :].T

    out[...] = dot(b[...], turned[...])


def codes_call(other, acts, proj_b):
    (tokens, wide), rank = acts.shape, proj_b.shape[0]
    half, step = tokens // 2, 512
    return pl.pallas_call(
        functools.partial(codes_kernel, other),
        grid=(rank // step,),
        out_shape=like((rank, half), F32),
        in_specs=[
            pl.BlockSpec((tokens, wide), lambda i: (0, 0)),
            pl.BlockSpec((step, wide), lambda i: (i, 0)),
        ],
        out_specs=pl.BlockSpec((step, half), lambda i: (i, 0)),
        scratch_shapes=[pltpu.VMEM((wide, half), BF)],
        compiler_params=pltpu.CompilerParams(vmem_limit_bytes=32 * 1024 * 1024),
        cost_estimate=pl.CostEstimate(
            flops=2 * rank * wide * half, bytes_accessed=2 * rank * wide, transcendentals=0
        ),
    )(acts, proj_b)


def sum_and_copy(blocks, out):
    value = total(blocks).astype(BF)
    for i in range(out.shape[0]):
        out[i] = value


def residual_kernel(codes, near, far, a0, a1, own, message, partial, held):
    rank, outs = codes.shape[0], a0.shape[0]
    step = 256
    for j, (target, a) in enumerate(((near, a0), (far, a1))):
        for at in range(0, outs, step):
            rows = slice(at, at + step)
            left = target[rows].astype(F32) - dot(a[rows], codes[...])
            left = left.astype(BF).T
            held[:, j * outs + at : j * outs + at + step] = left
            if j == 0:
                own[:, rows] = left
            else:
                message[rank + at : rank + at + step] = left
    message[:rank] = codes[...]
    sub = partial.shape[1]
    for at in range(0, rank, 512):
        cols = slice(at, at + 512)
        term = dot(held[:, :outs], a0[:, cols]) + dot(held[:, outs:], a1[:, cols])
        for i in range(partial.shape[0]):
            partial[i, :, cols] = term[i * sub : (i + 1) * sub].astype(BF)


def spread_kernel(blocks, out, held):
    y_lo = lax.axis_index("y_lo")
    held[...] = total(blocks).astype(BF)
    rank = held.shape[1]
    width = rank // 8
    for x in range(4):
        for side in range(2):
            start = (y_lo if side == 0 else 1 - y_lo) * (rank // 2) + x * width
            piece = held[:, pl.ds(pl.multiple_of(start, width), width)]
            for i in range(out.shape[1]):
                out[x, i, :, side * width : (side + 1) * width] = piece


def last_kernel(side, other, more, grad, acts, *refs):
    out, turned = refs[-2:]
    core = lax.axis_index("core")
    half, width = grad.shape[1], out.shape[0]
    which = 1 - core if other else core
    rows = pl.ds(pl.multiple_of(which * half, half), half)
    for k in range(4):
        turned[k] = grad[k, :, side * width : (side + 1) * width].T
    for c in range(0, out.shape[1], 256):
        cols = slice(c, c + 256)
        acc = dot(turned[0], acts[0, rows, cols])
        for k in range(1, 4):
            acc = acc + dot(turned[k], acts[k, rows, cols])
        if more:
            acc = acc + refs[0][:, cols]
        out[:, cols] = acc.astype(out.dtype)


def term_kernel(codes, own, message, out):
    rank, outs = out.shape
    for at in range(0, rank, 512):
        rows = slice(at, at + 512)
        for c in range(0, outs, 256):
            acc = dot(codes[rows], own[:, c : c + 256])
            out[rows, c : c + 256] = acc + dot(message[rows], message[rank + c : rank + c + 256])


def local(acts, target, proj_b, proj_a):
    core = lax.axis_index("core")
    tokens, rank = acts.shape[0], proj_b.shape[0]
    outs, wide = target.shape[1], acts.shape[1]
    half, sub, width = tokens // 2, tokens // 16, rank // 8
    scale = -2.0 / (tokens * 8)

    def part_of(array, which, size, axis):
        return lax.dynamic_slice_in_dim(array, which * size, size, axis)

    row = lax.all_gather(acts, "x")
    pair_a = swap(proj_a, "core")
    target_t = target.T
    near_t = part_of(target_t, core, half, 1)
    pair_t = swap(part_of(target_t, 1 - core, half, 1), "core")

    arrived = swap(codes_call(True, acts, proj_b), "core")
    mine = (codes_call(False, acts, proj_b) + arrived).astype(BF).reshape(8, width, half)
    blocks = lax.all_to_all(mine, ZY, 0, 0)
    codes = call(sum_and_copy, [like((8, width, half))], blocks)
    codes = lax.all_to_all(codes, ZY, 0, 0).reshape(rank, half)

    own, message, partial = call(
        residual_kernel,
        [like((half, outs)), like((rank + outs, half)), like((8, sub, rank))],
        codes, near_t, pair_t, proj_a, pair_a,
        scratch=[pltpu.VMEM((half, 2 * outs), BF)],
        flops=8 * half * rank * outs,
    )
    blocks = lax.all_to_all(partial, ZY, 0, 0)

    term = call(
        term_kernel, [like((rank, outs), F32)], codes, own, swap(message, "core"), flops=2 * tokens * rank * outs
    )
    blocks, term = lax.optimization_barrier((blocks, term))
    grad_a = (lax.psum_scatter(term, TOK, scatter_dimension=0, tiled=True) * scale).T

    split = call(spread_kernel, [like((4, 8, sub, 2 * width))], blocks, scratch=[pltpu.VMEM((sub, rank), BF)])
    split = split.reshape(32, sub, 2 * width)
    grad_m = lax.all_to_all(split, ("x", "z", "y_hi"), 0, 0).reshape(4, half, 2 * width)
    grad_o = swap(grad_m, "core")

    def last(side, other, dtype, *before):
        return call(
            functools.partial(last_kernel, side, other, len(before)),
            [like((width, wide), dtype)],
            grad_o if other else grad_m, row, *before,
            scratch=[pltpu.VMEM((4, width, half), BF)],
            flops=8 * half * width * wide,
        )

    away = swap(last(1, True, BF, last(1, False, F32)), "y_lo")
    here = last(0, True, F32, last(0, False, F32))
    grad_b = (here + away.astype(F32)) * scale
    return (grad_a, grad_b)


def solution(mesh):
    fine = Mesh(np.reshape(mesh.devices, (2, 4, 4, 2, 2)), ("y_lo", "x", "z", "y_hi", "core"))
    return jax.shard_map(
        local,
        mesh=fine,
        in_specs=(P(TOK, CHAN), P(TOK, CHAN), P(None, CHAN), P(CHAN, None)),
        out_specs=(P(CHAN, TOK), P(TOK, CHAN)),
        check_vma=False,
    )
```

```python
import functools

import jax
import jax.numpy as jnp
import numpy as np
from jax import lax
from jax.experimental import pallas as pl
from jax.experimental.pallas import tpu as pltpu
from jax.sharding import Mesh, PartitionSpec as P

BF, F32 = jnp.bfloat16, jnp.float32
TOK, CHAN, ZY = ("y_lo", "x"), ("z", "y_hi", "core"), ("z", "y_hi")
VMEM = pl.BlockSpec(memory_space=pltpu.VMEM)


def dot(left, right, left_dim=1, right_dim=0):
    return lax.dot_general(
        left, right, (((left_dim,), (right_dim,)), ((), ())), preferred_element_type=F32
    )


def shift(array, axis, size, step):
    return lax.ppermute(array, axis, [(i, (i + step) % size) for i in range(size)])


def swap(array, axis):
    return shift(array, axis, 2, 1)


def call(body, outs, *args, scratch=(), flops=0):
    moved = sum(a.size * a.dtype.itemsize for a in list(args) + list(outs))
    return pl.pallas_call(
        body,
        out_shape=outs if len(outs) > 1 else outs[0],
        in_specs=[VMEM] * len(args),
        out_specs=[VMEM] * len(outs) if len(outs) > 1 else VMEM,
        scratch_shapes=scratch,
        compiler_params=pltpu.CompilerParams(vmem_limit_bytes=16 * 1024 * 1024),
        cost_estimate=pl.CostEstimate(flops=flops, bytes_accessed=moved, transcendentals=0),
    )(*args)


def like(shape, dtype=BF):
    return jax.ShapeDtypeStruct(shape, dtype)


def total(ref, at=slice(None)):
    out = ref[0, at].astype(F32)
    for i in range(1, ref.shape[0]):
        out = out + ref[i, at].astype(F32)
    return out


def codes_kernel(other, acts, b, out, turned):
    core, half = lax.axis_index("core"), turned.shape[1]

    @pl.when(pl.program_id(0) == 0)
    def _():
        which = 1 - core if other else core
        turned[...] = acts[pl.ds(pl.multiple_of(which * half, half), half), :].T

    out[...] = dot(b[...], turned[...])


def codes_call(other, acts, proj_b):
    (tokens, wide), rank = acts.shape, proj_b.shape[0]
    half, step = tokens // 2, 512
    return pl.pallas_call(
        functools.partial(codes_kernel, other),
        grid=(rank // step,),
        out_shape=like((rank, half), F32),
        in_specs=[
            pl.BlockSpec((tokens, wide), lambda i: (0, 0)),
            pl.BlockSpec((step, wide), lambda i: (i, 0)),
        ],
        out_specs=pl.BlockSpec((step, half), lambda i: (i, 0)),
        scratch_shapes=[pltpu.VMEM((wide, half), BF)],
        compiler_params=pltpu.CompilerParams(vmem_limit_bytes=32 * 1024 * 1024),
        cost_estimate=pl.CostEstimate(
            flops=2 * rank * wide * half, bytes_accessed=2 * rank * wide, transcendentals=0
        ),
    )(acts, proj_b)


def sum_and_copy(blocks, out):
    value = total(blocks).astype(BF)
    for i in range(out.shape[0]):
        out[i] = value


def residual_kernel(codes, near, far, a0, a1, own, message, partial, held):
    rank, outs = codes.shape[0], a0.shape[0]
    step = 512
    for j, (target, a) in enumerate(((near, a0), (far, a1))):
        for at in range(0, outs, step):
            rows = slice(at, at + step)
            left = target[rows].astype(F32) - dot(a[rows], codes[...])
            left = left.astype(BF).T
            held[:, j * outs + at : j * outs + at + step] = left
            if j == 0:
                own[:, rows] = left
            else:
                for c in range(0, step, 256):
                    message[rank + at + c : rank + at + c + 256] = left[:, c : c + 256]
    message[:rank] = codes[...]
    sub = partial.shape[1]
    for at in range(0, rank, 512):
        cols = slice(at, at + 512)
        term = dot(held[:, :outs], a0[:, cols]) + dot(held[:, outs:], a1[:, cols])
        for i in range(partial.shape[0]):
            partial[i, :, cols] = term[i * sub : (i + 1) * sub].astype(BF)


def spread_kernel(blocks, away, own, held):
    y_lo = lax.axis_index("y_lo")
    held[...] = total(blocks).astype(BF)
    rank = held.shape[1]
    width = rank // 8
    for out, side in ((away, 1 - y_lo), (own, y_lo)):
        for x in range(4):
            start = pl.multiple_of(side * (rank // 2) + x * width, width)
            piece = held[:, pl.ds(start, width)]
            for i in range(out.shape[1]):
                out[x, i] = piece


def last_kernel(other, more, grad, acts, *refs):
    out, turned = refs[-2:]
    core = lax.axis_index("core")
    half, width = grad.shape[1], out.shape[0]
    which = 1 - core if other else core
    rows = pl.ds(pl.multiple_of(which * half, half), half)
    for k in range(4):
        turned[k] = grad[k].T
    for c in range(0, out.shape[1], 256):
        cols = slice(c, c + 256)
        acc = dot(turned[0], acts[0, rows, cols])
        for k in range(1, 4):
            acc = acc + dot(turned[k], acts[k, rows, cols])
        if more:
            acc = acc + refs[0][:, cols]
        out[:, cols] = acc.astype(out.dtype)


def term_kernel(codes, own, message, out):
    rank, outs = out.shape
    for at in range(0, rank, 512):
        rows = slice(at, at + 512)
        for c in range(0, outs, 256):
            acc = dot(codes[rows], own[:, c : c + 256])
            acc = acc + dot(message[rows], message[rank + c : rank + c + 256])
            out[rows, c : c + 256] = acc.astype(BF)


def local(acts, target, proj_b, proj_a):
    core = lax.axis_index("core")
    tokens, rank = acts.shape[0], proj_b.shape[0]
    outs, wide = target.shape[1], acts.shape[1]
    half, sub, width = tokens // 2, tokens // 16, rank // 8
    scale = -2.0 / (tokens * 8)

    def part_of(array, which, size, axis):
        return lax.dynamic_slice_in_dim(array, which * size, size, axis)

    row = lax.all_gather(acts, "x")
    pair_a = swap(proj_a, "core")
    target_t = target.T
    near_t = part_of(target_t, core, half, 1)
    pair_t = swap(part_of(target_t, 1 - core, half, 1), "core")

    arrived = swap(codes_call(True, acts, proj_b), "core")
    mine = (codes_call(False, acts, proj_b) + arrived).astype(BF).reshape(8, width, half)
    blocks = lax.all_to_all(mine, ZY, 0, 0)
    codes = call(sum_and_copy, [like((8, width, half))], blocks)
    codes = lax.all_to_all(codes, ZY, 0, 0).reshape(rank, half)

    own, message, partial = call(
        residual_kernel,
        [like((half, outs)), like((rank + outs, half)), like((8, sub, rank))],
        codes, near_t, pair_t, proj_a, pair_a,
        scratch=[pltpu.VMEM((half, 2 * outs), BF)],
        flops=8 * half * rank * outs,
    )
    blocks = lax.all_to_all(partial, ZY, 0, 0)

    term = call(
        term_kernel, [like((rank, outs))], codes, own, swap(message, "core"), flops=2 * tokens * rank * outs
    )
    term = term.reshape(2, 4, width, outs).transpose(1, 0, 2, 3)
    term = lax.all_to_all(term, "x", 0, 0)

    blocks, row = lax.optimization_barrier((blocks, row))
    spread = like((4, 8, sub, width))
    split_a, split_o = call(spread_kernel, [spread, spread], blocks, scratch=[pltpu.VMEM((sub, rank), BF)])

    def gather(split):
        split = lax.all_to_all(split.reshape(32, sub, width), ("x", "z", "y_hi"), 0, 0)
        return split.reshape(4, half, width)

    def last(grad, other, dtype, *before):
        return call(
            functools.partial(last_kernel, other, len(before)),
            [like((width, wide), dtype)],
            grad, row, *before,
            scratch=[pltpu.VMEM((4, width, half), BF)],
            flops=8 * half * width * wide,
        )

    grad = gather(split_a)
    grad, split_o, term = lax.optimization_barrier((grad, split_o, term))
    away = last(swap(grad, "core"), True, BF, last(grad, False, F32))
    away = swap(away, "y_lo")
    grad = gather(split_o)
    here = last(swap(grad, "core"), True, F32, last(grad, False, F32))
    grad_b = (here + away.astype(F32)) * scale

    sums = term[0].astype(F32)
    for i in range(1, 4):
        sums = sums + term[i].astype(F32)
    y_lo = lax.axis_index("y_lo")
    pick = functools.partial(lax.dynamic_index_in_dim, sums, axis=0, keepdims=False)
    grad_a = pick(y_lo) + swap(pick(1 - y_lo).astype(BF), "y_lo").astype(F32)
    return ((grad_a * scale).T, grad_b)


def solution(mesh):
    fine = Mesh(np.reshape(mesh.devices, (2, 4, 4, 2, 2)), ("y_lo", "x", "z", "y_hi", "core"))
    return jax.shard_map(
        local,
        mesh=fine,
        in_specs=(P(TOK, CHAN), P(TOK, CHAN), P(None, CHAN), P(CHAN, None)),
        out_specs=(P(CHAN, TOK), P(TOK, CHAN)),
        check_vma=False,
    )
```

```python
import functools

import jax
import jax.numpy as jnp
import numpy as np
from jax import lax
from jax.experimental import pallas as pl
from jax.experimental.pallas import tpu as pltpu
from jax.sharding import Mesh, PartitionSpec as P

BF, F32 = jnp.bfloat16, jnp.float32
TOK, CHAN, ZY = ("y_lo", "x"), ("z", "y_hi", "core"), ("z", "y_hi")
VMEM = pl.BlockSpec(memory_space=pltpu.VMEM)


def dot(left, right, left_dim=1, right_dim=0):
    return lax.dot_general(
        left, right, (((left_dim,), (right_dim,)), ((), ())), preferred_element_type=F32
    )


def shift(array, axis, size, step):
    return lax.ppermute(array, axis, [(i, (i + step) % size) for i in range(size)])


def swap(array, axis):
    return shift(array, axis, 2, 1)


def call(body, outs, *args, scratch=(), flops=0):
    moved = sum(a.size * a.dtype.itemsize for a in list(args) + list(outs))
    return pl.pallas_call(
        body,
        out_shape=outs if len(outs) > 1 else outs[0],
        in_specs=[VMEM] * len(args),
        out_specs=[VMEM] * len(outs) if len(outs) > 1 else VMEM,
        scratch_shapes=scratch,
        compiler_params=pltpu.CompilerParams(vmem_limit_bytes=16 * 1024 * 1024),
        cost_estimate=pl.CostEstimate(flops=flops, bytes_accessed=moved, transcendentals=0),
    )(*args)


def like(shape, dtype=BF):
    return jax.ShapeDtypeStruct(shape, dtype)


def total(ref, at=slice(None)):
    out = ref[0, at].astype(F32)
    for i in range(1, ref.shape[0]):
        out = out + ref[i, at].astype(F32)
    return out


def codes_kernel(other, acts, b, out, turned):
    core, half = lax.axis_index("core"), turned.shape[1]

    @pl.when(pl.program_id(0) == 0)
    def _():
        which = 1 - core if other else core
        turned[...] = acts[pl.ds(pl.multiple_of(which * half, half), half), :].T

    out[...] = dot(b[...], turned[...])


def codes_call(other, acts, proj_b):
    (tokens, wide), rank = acts.shape, proj_b.shape[0]
    half, step = tokens // 2, 512
    return pl.pallas_call(
        functools.partial(codes_kernel, other),
        grid=(rank // step,),
        out_shape=like((rank, half), F32),
        in_specs=[
            pl.BlockSpec((tokens, wide), lambda i: (0, 0)),
            pl.BlockSpec((step, wide), lambda i: (i, 0)),
        ],
        out_specs=pl.BlockSpec((step, half), lambda i: (i, 0)),
        scratch_shapes=[pltpu.VMEM((wide, half), BF)],
        compiler_params=pltpu.CompilerParams(vmem_limit_bytes=32 * 1024 * 1024),
        cost_estimate=pl.CostEstimate(
            flops=2 * rank * wide * half, bytes_accessed=2 * rank * wide, transcendentals=0
        ),
    )(acts, proj_b)


def sum_and_copy(blocks, out):
    value = total(blocks).astype(BF)
    for i in range(out.shape[0]):
        out[i] = value


def residual_kernel(codes, near, far, a0, a1, own, message, partial, held):
    rank, outs = codes.shape[0], a0.shape[0]
    step = 256
    for j, (target, a) in enumerate(((near, a0), (far, a1))):
        for at in range(0, outs, step):
            rows = slice(at, at + step)
            left = target[rows].astype(F32) - dot(a[rows], codes[...])
            left = left.astype(BF).T
            held[:, j * outs + at : j * outs + at + step] = left
            if j == 0:
                own[:, rows] = left
            else:
                for c in range(0, step, 256):
                    message[rank + at + c : rank + at + c + 256] = left[:, c : c + 256]
    message[:rank] = codes[...]
    sub = partial.shape[1]
    for at in range(0, rank, 512):
        cols = slice(at, at + 512)
        term = dot(held[:, :outs], a0[:, cols]) + dot(held[:, outs:], a1[:, cols])
        for i in range(partial.shape[0]):
            partial[i, :, cols] = term[i * sub : (i + 1) * sub].astype(BF)


def spread_kernel(blocks, away, own, held):
    y_lo = lax.axis_index("y_lo")
    held[...] = total(blocks).astype(BF)
    rank = held.shape[1]
    width = rank // 8
    for out, side in ((away, 1 - y_lo), (own, y_lo)):
        for x in range(4):
            start = pl.multiple_of(side * (rank // 2) + x * width, width)
            piece = held[:, pl.ds(start, width)]
            for i in range(out.shape[1]):
                out[x, i] = piece


def last_kernel(joined, grad_m, grad_o, acts, *refs):
    out, turned = refs[-2:]
    core, step = lax.axis_index("core"), pl.program_id(0)
    half = grad_m.shape[1]
    steps = pl.num_programs(0) - (2 if joined else 0)

    @pl.when(step == 0)
    def _():
        for k in range(4):
            turned[k, :, pl.ds(pl.multiple_of(core * half, half), half)] = grad_m[k].T
            turned[k, :, pl.ds(pl.multiple_of((1 - core) * half, half), half)] = grad_o[k].T

    @pl.when(step < steps)
    def _():
        acc = dot(turned[0], acts[0])
        for k in range(1, 4):
            acc = acc + dot(turned[k], acts[k])
        out[...] = acc.astype(out.dtype)

    if joined:

        @pl.when(step >= steps)
        def _():
            out[...] = refs[0][...]


def last_call(grad_m, grad_o, row, dtype, *joined):
    _, tokens, wide = row.shape
    half, width = grad_m.shape[1:]
    block = 256
    steps = wide // block
    more = 2 if joined else 0
    whole = pl.BlockSpec((4, half, width), lambda i: (0, 0, 0))
    return pl.pallas_call(
        functools.partial(last_kernel, bool(joined)),
        grid=(steps + more,),
        out_shape=like((width, wide + more * block), dtype),
        in_specs=[
            whole,
            whole,
            pl.BlockSpec((4, tokens, block), lambda i: (0, 0, jnp.minimum(i, steps - 1))),
        ]
        + [pl.BlockSpec((width, block), lambda i: (0, jnp.maximum(i - steps, 0)))] * len(joined),
        out_specs=pl.BlockSpec((width, block), lambda i: (0, i)),
        scratch_shapes=[pltpu.VMEM((4, width, tokens), BF)],
        compiler_params=pltpu.CompilerParams(vmem_limit_bytes=48 * 1024 * 1024),
        cost_estimate=pl.CostEstimate(
            flops=8 * tokens * width * wide, bytes_accessed=8 * tokens * wide, transcendentals=0
        ),
    )(grad_m, grad_o, row, *joined)


def term_kernel(codes, own, message, keep, s1, s2, s3):
    x = lax.axis_index("x")
    rank, outs = codes.shape[0], own.shape[1]
    width = rank // 8
    for k, out in enumerate((keep, s1, s2, s3)):
        for side in range(2):
            start = side * (rank // 2) + lax.rem(x + k, 4) * width
            rows = pl.ds(pl.multiple_of(start, width), width)
            left, right = codes[rows, :], message[rows, :]
            for c in range(0, outs, 256):
                acc = dot(left, own[:, c : c + 256])
                acc = acc + dot(right, message[rank + c : rank + c + 256])
                out[side, :, c : c + 256] = acc.astype(out.dtype)


def term_sum_kernel(keep, r1, r2, r3, own, away):
    y_lo = lax.axis_index("y_lo")
    for out, side in ((own, y_lo), (away, 1 - y_lo)):
        value = keep[side]
        for r in (r1, r2, r3):
            value = value + r[side].astype(F32)
        out[...] = value.astype(out.dtype)


def local(acts, target, proj_b, proj_a):
    core = lax.axis_index("core")
    tokens, rank = acts.shape[0], proj_b.shape[0]
    outs, wide = target.shape[1], acts.shape[1]
    half, sub, width = tokens // 2, tokens // 16, rank // 8
    scale = -2.0 / (tokens * 8)

    def part_of(array, which, size, axis):
        return lax.dynamic_slice_in_dim(array, which * size, size, axis)

    row = lax.all_gather(acts, "x")
    pair_a = swap(proj_a, "core")
    target_t = target.T
    near_t = part_of(target_t, core, half, 1)
    pair_t = swap(part_of(target_t, 1 - core, half, 1), "core")

    arrived = swap(codes_call(True, acts, proj_b), "core")
    mine = (codes_call(False, acts, proj_b) + arrived).astype(BF).reshape(8, width, half)
    blocks = lax.all_to_all(mine, ZY, 0, 0)
    codes = call(sum_and_copy, [like((8, width, half))], blocks)
    codes = lax.all_to_all(codes, ZY, 0, 0).reshape(rank, half)

    own, message, partial = call(
        residual_kernel,
        [like((half, outs)), like((rank + outs, half)), like((8, sub, rank))],
        codes, near_t, pair_t, proj_a, pair_a,
        scratch=[pltpu.VMEM((half, 2 * outs), BF)],
        flops=8 * half * rank * outs,
    )
    blocks = lax.all_to_all(partial, ZY, 0, 0)

    piece = like((2, width, outs))
    terms = call(
        term_kernel,
        [like(piece.shape, F32), piece, piece, piece],
        codes, own, swap(message, "core"),
        flops=2 * tokens * rank * outs,
    )
    terms = [terms[0]] + [shift(terms[k], "x", 4, k) for k in (1, 2, 3)]

    blocks, row, *terms = lax.optimization_barrier((blocks, row, *terms))
    spread = like((4, 8, sub, width))
    split_a, split_o = call(spread_kernel, [spread, spread], blocks, scratch=[pltpu.VMEM((sub, rank), BF)])
    term_o, term_a = call(term_sum_kernel, [like((width, outs), F32), like((width, outs))], *terms)

    def gather(split):
        split = lax.all_to_all(split.reshape(32, sub, width), ("x", "z", "y_hi"), 0, 0)
        return split.reshape(4, half, width)

    grad = gather(split_a)
    grad, split_o = lax.optimization_barrier((grad, split_o))
    away = swap(last_call(grad, swap(grad, "core"), row, BF, term_a), "y_lo").astype(F32)
    grad = gather(split_o)
    here = last_call(grad, swap(grad, "core"), row, F32)
    here, term_o = lax.optimization_barrier((here, term_o))
    return (((term_o + away[:, wide:]) * scale).T, (here + away[:, :wide]) * scale)


def solution(mesh):
    fine = Mesh(np.reshape(mesh.devices, (2, 4, 4, 2, 2)), ("y_lo", "x", "z", "y_hi", "core"))
    return jax.shard_map(
        local,
        mesh=fine,
        in_specs=(P(TOK, CHAN), P(TOK, CHAN), P(None, CHAN), P(CHAN, None)),
        out_specs=(P(CHAN, TOK), P(TOK, CHAN)),
        check_vma=False,
    )
```

```python
import functools

import jax
import jax.numpy as jnp
import numpy as np
from jax import lax
from jax.experimental import pallas as pl
from jax.experimental.pallas import tpu as pltpu
from jax.sharding import Mesh, PartitionSpec as P

BF, F32 = jnp.bfloat16, jnp.float32
TOK, CHAN, ZY = ("y_lo", "x"), ("z", "y_hi", "core"), ("z", "y_hi")
VMEM = pl.BlockSpec(memory_space=pltpu.VMEM)
ANY = pl.BlockSpec(memory_space=pl.ANY)


def dot(left, right, left_dim=1, right_dim=0):
    return lax.dot_general(
        left, right, (((left_dim,), (right_dim,)), ((), ())), preferred_element_type=F32
    )


def shift(array, axis, size, step):
    return lax.ppermute(array, axis, [(i, (i + step) % size) for i in range(size)])


def swap(array, axis):
    return shift(array, axis, 2, 1)


def call(body, outs, *args, scratch=(), flops=0):
    moved = sum(a.size * a.dtype.itemsize for a in list(args) + list(outs))
    return pl.pallas_call(
        body,
        out_shape=outs if len(outs) > 1 else outs[0],
        in_specs=[VMEM] * len(args),
        out_specs=[VMEM] * len(outs) if len(outs) > 1 else VMEM,
        scratch_shapes=scratch,
        compiler_params=pltpu.CompilerParams(vmem_limit_bytes=16 * 1024 * 1024),
        cost_estimate=pl.CostEstimate(flops=flops, bytes_accessed=moved, transcendentals=0),
    )(*args)


def like(shape, dtype=BF):
    return jax.ShapeDtypeStruct(shape, dtype)


def total(ref, at=slice(None)):
    out = ref[0, at].astype(F32)
    for i in range(1, ref.shape[0]):
        out = out + ref[i, at].astype(F32)
    return out


def codes_kernel(other, acts, b, out, rows, turned, held, sems):
    core, (parts, step), half = lax.axis_index("core"), held.shape[:2], rows.shape[0]
    start = pl.multiple_of((1 - core if other else core) * half, half)
    first = pltpu.make_async_copy(acts.at[pl.ds(start, half), :], rows, sems.at[parts])
    first.start()
    copies = [
        pltpu.make_async_copy(b.at[pl.ds(i * step, step), :], held.at[i], sems.at[i])
        for i in range(parts)
    ]
    for copy in copies:
        copy.start()
    first.wait()
    turned[...] = rows[...].T
    for i in range(parts):
        copies[i].wait()
        out[i * step : (i + 1) * step] = dot(held[i], turned[...])


def codes_call(other, acts, proj_b):
    (tokens, wide), rank = acts.shape, proj_b.shape[0]
    half, step = tokens // 2, 512
    return pl.pallas_call(
        functools.partial(codes_kernel, other),
        out_shape=like((rank, half), F32),
        in_specs=[ANY, ANY],
        out_specs=VMEM,
        scratch_shapes=[
            pltpu.VMEM((half, wide), BF),
            pltpu.VMEM((wide, half), BF),
            pltpu.VMEM((rank // step, step, wide), BF),
            pltpu.SemaphoreType.DMA((rank // step + 1,)),
        ],
        compiler_params=pltpu.CompilerParams(vmem_limit_bytes=58 * 1024 * 1024),
        cost_estimate=pl.CostEstimate(
            flops=2 * rank * wide * half, bytes_accessed=2 * rank * wide, transcendentals=0
        ),
    )(acts, proj_b)


def sum_and_copy(blocks, out):
    value = total(blocks).astype(BF)
    for i in range(out.shape[0]):
        out[i] = value


def residual_kernel(codes, near, far, a0, a1, own, message, partial, held):
    rank, outs = codes.shape[0], a0.shape[0]
    step = 256
    for j, (target, a) in enumerate(((near, a0), (far, a1))):
        for at in range(0, outs, step):
            rows = slice(at, at + step)
            left = target[rows].astype(F32) - dot(a[rows], codes[...])
            left = left.astype(BF).T
            held[:, j * outs + at : j * outs + at + step] = left
            if j == 0:
                own[:, rows] = left
            else:
                for c in range(0, step, 256):
                    message[rank + at + c : rank + at + c + 256] = left[:, c : c + 256]
    message[:rank] = codes[...]
    sub = partial.shape[1]
    for at in range(0, rank, 512):
        cols = slice(at, at + 512)
        term = dot(held[:, :outs], a0[:, cols]) + dot(held[:, outs:], a1[:, cols])
        for i in range(partial.shape[0]):
            partial[i, :, cols] = term[i * sub : (i + 1) * sub].astype(BF)


def spread_kernel(blocks, away, own, held):
    y_lo = lax.axis_index("y_lo")
    held[...] = total(blocks).astype(BF)
    rank = held.shape[1]
    width = rank // 8
    for out, side in ((away, 1 - y_lo), (own, y_lo)):
        for x in range(4):
            start = pl.multiple_of(side * (rank // 2) + x * width, width)
            piece = held[:, pl.ds(start, width)]
            for i in range(out.shape[1]):
                out[x, i] = piece


def last_kernel(grad_m, grad_o, acts, *refs):
    joined, (out, turned, held, sems) = refs[:-4], refs[-4:]
    core = lax.axis_index("core")
    half, wide, step = grad_m.shape[1], acts.shape[2], held.shape[3]
    copies = [
        pltpu.make_async_copy(acts.at[:, :, pl.ds(i * step, step)], held.at[i], sems.at[i])
        for i in range(wide // step)
    ]
    for copy in copies:
        copy.start()
    for k in range(4):
        turned[k, :, pl.ds(pl.multiple_of(core * half, half), half)] = grad_m[k].T
        turned[k, :, pl.ds(pl.multiple_of((1 - core) * half, half), half)] = grad_o[k].T
    for ref in joined:
        out[:, wide:] = ref[...]
    for i, copy in enumerate(copies):
        copy.wait()
        acc = dot(turned[0], held[i, 0])
        for k in range(1, 4):
            acc = acc + dot(turned[k], held[i, k])
        out[:, i * step : (i + 1) * step] = acc.astype(out.dtype)


def last_call(grad_m, grad_o, row, dtype, *joined):
    _, tokens, wide = row.shape
    width, step = grad_m.shape[2], 256
    return pl.pallas_call(
        last_kernel,
        out_shape=like((width, wide + sum(j.shape[1] for j in joined)), dtype),
        in_specs=[VMEM, VMEM, ANY] + [VMEM] * len(joined),
        out_specs=VMEM,
        scratch_shapes=[
            pltpu.VMEM((4, width, tokens), BF),
            pltpu.VMEM((wide // step, 4, tokens, step), BF),
            pltpu.SemaphoreType.DMA((wide // step,)),
        ],
        compiler_params=pltpu.CompilerParams(vmem_limit_bytes=48 * 1024 * 1024),
        cost_estimate=pl.CostEstimate(
            flops=8 * tokens * width * wide, bytes_accessed=8 * tokens * wide, transcendentals=0
        ),
    )(grad_m, grad_o, row, *joined)


def term_kernel(codes, own, message, keep, s1, s2, s3):
    x = lax.axis_index("x")
    rank, outs = codes.shape[0], own.shape[1]
    width = rank // 8
    for k, out in enumerate((keep, s1, s2, s3)):
        for side in range(2):
            start = side * (rank // 2) + lax.rem(x + k, 4) * width
            rows = pl.ds(pl.multiple_of(start, width), width)
            left, right = codes[rows, :], message[rows, :]
            for c in range(0, outs, 256):
                acc = dot(left, own[:, c : c + 256])
                acc = acc + dot(right, message[rank + c : rank + c + 256])
                out[side, :, c : c + 256] = acc.astype(out.dtype)


def term_sum_kernel(keep, r1, r2, r3, own, away):
    y_lo = lax.axis_index("y_lo")
    for out, side in ((own, y_lo), (away, 1 - y_lo)):
        value = keep[side]
        for r in (r1, r2, r3):
            value = value + r[side].astype(F32)
        out[...] = value.astype(out.dtype)


def local(acts, target, proj_b, proj_a):
    core = lax.axis_index("core")
    tokens, rank = acts.shape[0], proj_b.shape[0]
    outs, wide = target.shape[1], acts.shape[1]
    half, sub, width = tokens // 2, tokens // 16, rank // 8
    scale = -2.0 / (tokens * 8)

    def part_of(array, which, size, axis):
        return lax.dynamic_slice_in_dim(array, which * size, size, axis)

    row = lax.all_gather(acts, "x")
    pair_a = swap(proj_a, "core")
    target_t = target.T
    near_t = part_of(target_t, core, half, 1)
    pair_t = swap(part_of(target_t, 1 - core, half, 1), "core")

    arrived = swap(codes_call(True, acts, proj_b), "core")
    mine = (codes_call(False, acts, proj_b) + arrived).astype(BF).reshape(8, width, half)
    blocks = lax.all_to_all(mine, ZY, 0, 0)
    codes = call(sum_and_copy, [like((8, width, half))], blocks)
    codes = lax.all_to_all(codes, ZY, 0, 0).reshape(rank, half)

    own, message, partial = call(
        residual_kernel,
        [like((half, outs)), like((rank + outs, half)), like((8, sub, rank))],
        codes, near_t, pair_t, proj_a, pair_a,
        scratch=[pltpu.VMEM((half, 2 * outs), BF)],
        flops=8 * half * rank * outs,
    )
    blocks = lax.all_to_all(partial, ZY, 0, 0)

    piece = like((2, width, outs))
    terms = call(
        term_kernel,
        [like(piece.shape, F32), piece, piece, piece],
        codes, own, swap(message, "core"),
        flops=2 * tokens * rank * outs,
    )
    terms = [terms[0]] + [shift(terms[k], "x", 4, k) for k in (1, 2, 3)]

    blocks, row, terms[1], terms[3] = lax.optimization_barrier((blocks, row, terms[1], terms[3]))
    spread = like((4, 8, sub, width))
    split_a, split_o = call(spread_kernel, [spread, spread], blocks, scratch=[pltpu.VMEM((sub, rank), BF)])

    def gather(split):
        split = lax.all_to_all(split.reshape(32, sub, width), ("x", "z", "y_hi"), 0, 0)
        return split.reshape(4, half, width)

    grad = gather(split_a)
    grad, terms[2] = lax.optimization_barrier((grad, terms[2]))
    term_o, term_a = call(term_sum_kernel, [like((width, outs), F32), like((width, outs))], *terms)
    away = last_call(grad, swap(grad, "core"), row, BF, term_a)
    away, split_o = lax.optimization_barrier((away, split_o))
    away = swap(away, "y_lo").astype(F32)
    grad = gather(split_o)
    here = last_call(grad, swap(grad, "core"), row, F32)
    here, term_o = lax.optimization_barrier((here, term_o))
    return (((term_o + away[:, wide:]) * scale).T, (here + away[:, :wide]) * scale)


def solution(mesh):
    fine = Mesh(np.reshape(mesh.devices, (2, 4, 4, 2, 2)), ("y_lo", "x", "z", "y_hi", "core"))
    return jax.shard_map(
        local,
        mesh=fine,
        in_specs=(P(TOK, CHAN), P(TOK, CHAN), P(None, CHAN), P(CHAN, None)),
        out_specs=(P(CHAN, TOK), P(TOK, CHAN)),
        check_vma=False,
    )
```

```python
import functools

import jax
import jax.numpy as jnp
import numpy as np
from jax import lax
from jax.experimental import pallas as pl
from jax.experimental.pallas import tpu as pltpu
from jax.sharding import Mesh, PartitionSpec as P

BF, F32 = jnp.bfloat16, jnp.float32
TOK, CHAN, ZY = ("y_lo", "x"), ("z", "y_hi", "core"), ("z", "y_hi")
VMEM = pl.BlockSpec(memory_space=pltpu.VMEM)
ANY = pl.BlockSpec(memory_space=pl.ANY)


def dot(left, right, left_dim=1, right_dim=0):
    return lax.dot_general(
        left, right, (((left_dim,), (right_dim,)), ((), ())), preferred_element_type=F32
    )


def shift(array, axis, size, step):
    return lax.ppermute(array, axis, [(i, (i + step) % size) for i in range(size)])


def swap(array, axis):
    return shift(array, axis, 2, 1)


def call(body, outs, *args, scratch=(), flops=0):
    moved = sum(a.size * a.dtype.itemsize for a in list(args) + list(outs))
    return pl.pallas_call(
        body,
        out_shape=outs if len(outs) > 1 else outs[0],
        in_specs=[VMEM] * len(args),
        out_specs=[VMEM] * len(outs) if len(outs) > 1 else VMEM,
        scratch_shapes=scratch,
        compiler_params=pltpu.CompilerParams(vmem_limit_bytes=16 * 1024 * 1024),
        cost_estimate=pl.CostEstimate(flops=flops, bytes_accessed=moved, transcendentals=0),
    )(*args)


def like(shape, dtype=BF):
    return jax.ShapeDtypeStruct(shape, dtype)


def total(ref, at=slice(None)):
    out = ref[0, at].astype(F32)
    for i in range(1, ref.shape[0]):
        out = out + ref[i, at].astype(F32)
    return out


def codes_kernel(other, acts, b, out, turned):
    core, half = lax.axis_index("core"), turned.shape[1]

    @pl.when(pl.program_id(0) == 0)
    def _():
        which = 1 - core if other else core
        turned[...] = acts[pl.ds(pl.multiple_of(which * half, half), half), :].T

    out[...] = dot(b[...], turned[...])


def codes_call(other, acts, proj_b):
    (tokens, wide), rank = acts.shape, proj_b.shape[0]
    half, step = tokens // 2, 512
    return pl.pallas_call(
        functools.partial(codes_kernel, other),
        grid=(rank // step,),
        out_shape=like((rank, half), F32),
        in_specs=[
            pl.BlockSpec((tokens, wide), lambda i: (0, 0)),
            pl.BlockSpec((step, wide), lambda i: (i, 0)),
        ],
        out_specs=pl.BlockSpec((step, half), lambda i: (i, 0)),
        scratch_shapes=[pltpu.VMEM((wide, half), BF)],
        compiler_params=pltpu.CompilerParams(vmem_limit_bytes=32 * 1024 * 1024),
        cost_estimate=pl.CostEstimate(
            flops=2 * rank * wide * half, bytes_accessed=2 * rank * wide, transcendentals=0
        ),
    )(acts, proj_b)


def sum_and_copy(blocks, out):
    value = total(blocks).astype(BF)
    for i in range(out.shape[0]):
        out[i] = value


def residual_kernel(codes, near, far, a0, a1, own, message, partial, held):
    rank, outs = codes.shape[0], a0.shape[0]
    step = 256
    for j, (target, a) in enumerate(((near, a0), (far, a1))):
        for at in range(0, outs, step):
            rows = slice(at, at + step)
            left = target[rows].astype(F32) - dot(a[rows], codes[...])
            left = left.astype(BF).T
            held[:, j * outs + at : j * outs + at + step] = left
            if j == 0:
                own[:, rows] = left
            else:
                for c in range(0, step, 256):
                    message[rank + at + c : rank + at + c + 256] = left[:, c : c + 256]
    message[:rank] = codes[...]
    sub = partial.shape[1]
    for at in range(0, rank, 512):
        cols = slice(at, at + 512)
        term = dot(held[:, :outs], a0[:, cols]) + dot(held[:, outs:], a1[:, cols])
        for i in range(partial.shape[0]):
            partial[i, :, cols] = term[i * sub : (i + 1) * sub].astype(BF)


def spread_kernel(blocks, away, own, held):
    y_lo = lax.axis_index("y_lo")
    held[...] = total(blocks).astype(BF)
    rank = held.shape[1]
    width = rank // 8
    for out, side in ((away, 1 - y_lo), (own, y_lo)):
        for x in range(4):
            start = pl.multiple_of(side * (rank // 2) + x * width, width)
            piece = held[:, pl.ds(start, width)]
            for i in range(out.shape[1]):
                out[x, i] = piece


def last_kernel(grad_m, grad_o, acts, *refs):
    joined, (out, turned, held, sems) = refs[:-4], refs[-4:]
    core = lax.axis_index("core")
    half, wide, step = grad_m.shape[1], acts.shape[2], held.shape[3]
    copies = [
        pltpu.make_async_copy(acts.at[:, :, pl.ds(i * step, step)], held.at[i], sems.at[i])
        for i in range(wide // step)
    ]
    for copy in copies:
        copy.start()
    for k in range(4):
        turned[k, :, pl.ds(pl.multiple_of(core * half, half), half)] = grad_m[k].T
        turned[k, :, pl.ds(pl.multiple_of((1 - core) * half, half), half)] = grad_o[k].T
    for ref in joined:
        out[:, wide:] = ref[...]
    for i, copy in enumerate(copies):
        copy.wait()
        acc = dot(turned[0], held[i, 0])
        for k in range(1, 4):
            acc = acc + dot(turned[k], held[i, k])
        out[:, i * step : (i + 1) * step] = acc.astype(out.dtype)


def last_call(grad_m, grad_o, row, dtype, *joined):
    _, tokens, wide = row.shape
    width, step = grad_m.shape[2], 256
    return pl.pallas_call(
        last_kernel,
        out_shape=like((width, wide + sum(j.shape[1] for j in joined)), dtype),
        in_specs=[VMEM, VMEM, ANY] + [VMEM] * len(joined),
        out_specs=VMEM,
        scratch_shapes=[
            pltpu.VMEM((4, width, tokens), BF),
            pltpu.VMEM((wide // step, 4, tokens, step), BF),
            pltpu.SemaphoreType.DMA((wide // step,)),
        ],
        compiler_params=pltpu.CompilerParams(vmem_limit_bytes=48 * 1024 * 1024),
        cost_estimate=pl.CostEstimate(
            flops=8 * tokens * width * wide, bytes_accessed=8 * tokens * wide, transcendentals=0
        ),
    )(grad_m, grad_o, row, *joined)


def term_kernel(codes, own, message, keep, s1, s2, s3):
    x = lax.axis_index("x")
    rank, outs = codes.shape[0], own.shape[1]
    width = rank // 8
    for k, out in enumerate((keep, s1, s2, s3)):
        for side in range(2):
            start = side * (rank // 2) + lax.rem(x + k, 4) * width
            rows = pl.ds(pl.multiple_of(start, width), width)
            left, right = codes[rows, :], message[rows, :]
            for c in range(0, outs, 256):
                acc = dot(left, own[:, c : c + 256])
                acc = acc + dot(right, message[rank + c : rank + c + 256])
                out[side, :, c : c + 256] = acc.astype(out.dtype)


def term_sum_kernel(keep, r1, r2, r3, own, away):
    y_lo = lax.axis_index("y_lo")
    for out, side in ((own, y_lo), (away, 1 - y_lo)):
        value = keep[side]
        for r in (r1, r2, r3):
            value = value + r[side].astype(F32)
        out[...] = value.astype(out.dtype)


def local(acts, target, proj_b, proj_a):
    core = lax.axis_index("core")
    tokens, rank = acts.shape[0], proj_b.shape[0]
    outs, wide = target.shape[1], acts.shape[1]
    half, sub, width = tokens // 2, tokens // 16, rank // 8
    scale = -2.0 / (tokens * 8)

    def part_of(array, which, size, axis):
        return lax.dynamic_slice_in_dim(array, which * size, size, axis)

    row = lax.all_gather(acts, "x")
    pair_a = swap(proj_a, "core")
    target_t = target.T
    near_t = part_of(target_t, core, half, 1)
    pair_t = swap(part_of(target_t, 1 - core, half, 1), "core")

    arrived = swap(codes_call(True, acts, proj_b), "core")
    mine = (codes_call(False, acts, proj_b) + arrived).astype(BF).reshape(8, width, half)
    blocks = lax.all_to_all(mine, ZY, 0, 0)
    codes = call(sum_and_copy, [like((8, width, half))], blocks)
    codes = lax.all_to_all(codes, ZY, 0, 0).reshape(rank, half)

    own, message, partial = call(
        residual_kernel,
        [like((half, outs)), like((rank + outs, half)), like((8, sub, rank))],
        codes, near_t, pair_t, proj_a, pair_a,
        scratch=[pltpu.VMEM((half, 2 * outs), BF)],
        flops=8 * half * rank * outs,
    )
    blocks = lax.all_to_all(partial, ZY, 0, 0)

    piece = like((2, width, outs))
    terms = call(
        term_kernel,
        [like(piece.shape, F32), piece, piece, piece],
        codes, own, swap(message, "core"),
        flops=2 * tokens * rank * outs,
    )
    terms = [terms[0]] + [shift(terms[k], "x", 4, k) for k in (1, 2, 3)]

    blocks, row = lax.optimization_barrier((blocks, row))
    spread = like((4, 8, sub, width))
    split_a, split_o = call(spread_kernel, [spread, spread], blocks, scratch=[pltpu.VMEM((sub, rank), BF)])

    def gather(split):
        split = lax.all_to_all(split.reshape(32, sub, width), ("x", "z", "y_hi"), 0, 0)
        return split.reshape(4, half, width)

    grad = gather(split_a)
    grad, *terms = lax.optimization_barrier((grad, *terms))
    term_o, term_a = call(term_sum_kernel, [like((width, outs), F32), like((width, outs))], *terms)
    away = last_call(grad, swap(grad, "core"), row, BF, term_a)
    away, split_o = lax.optimization_barrier((away, split_o))
    away = swap(away, "y_lo").astype(F32)
    grad = gather(split_o)
    here = last_call(grad, swap(grad, "core"), row, F32)
    here, term_o = lax.optimization_barrier((here, term_o))
    return (((term_o + away[:, wide:]) * scale).T, (here + away[:, :wide]) * scale)


def solution(mesh):
    fine = Mesh(np.reshape(mesh.devices, (2, 4, 4, 2, 2)), ("y_lo", "x", "z", "y_hi", "core"))
    return jax.shard_map(
        local,
        mesh=fine,
        in_specs=(P(TOK, CHAN), P(TOK, CHAN), P(None, CHAN), P(CHAN, None)),
        out_specs=(P(CHAN, TOK), P(TOK, CHAN)),
        check_vma=False,
    )
```

```python
import functools

import jax
import jax.numpy as jnp
import numpy as np
from jax import lax
from jax.experimental import pallas as pl
from jax.experimental.pallas import tpu as pltpu
from jax.sharding import Mesh, PartitionSpec as P

BF, F32 = jnp.bfloat16, jnp.float32
TOK, CHAN, ZY = ("y_lo", "x"), ("z", "y_hi", "core"), ("z", "y_hi")
VMEM = pl.BlockSpec(memory_space=pltpu.VMEM)
ANY = pl.BlockSpec(memory_space=pl.ANY)


def dot(left, right, left_dim=1, right_dim=0):
    return lax.dot_general(
        left, right, (((left_dim,), (right_dim,)), ((), ())), preferred_element_type=F32
    )


def shift(array, axis, size, step):
    return lax.ppermute(array, axis, [(i, (i + step) % size) for i in range(size)])


def swap(array, axis):
    return shift(array, axis, 2, 1)


def call(body, outs, *args, scratch=(), flops=0):
    moved = sum(a.size * a.dtype.itemsize for a in list(args) + list(outs))
    return pl.pallas_call(
        body,
        out_shape=outs if len(outs) > 1 else outs[0],
        in_specs=[VMEM] * len(args),
        out_specs=[VMEM] * len(outs) if len(outs) > 1 else VMEM,
        scratch_shapes=scratch,
        compiler_params=pltpu.CompilerParams(vmem_limit_bytes=16 * 1024 * 1024),
        cost_estimate=pl.CostEstimate(flops=flops, bytes_accessed=moved, transcendentals=0),
    )(*args)


def like(shape, dtype=BF):
    return jax.ShapeDtypeStruct(shape, dtype)


def total(ref, at=slice(None)):
    out = ref[0, at].astype(F32)
    for i in range(1, ref.shape[0]):
        out = out + ref[i, at].astype(F32)
    return out


def codes_kernel(other, acts, b, out, turned):
    core, half = lax.axis_index("core"), turned.shape[1]

    @pl.when(pl.program_id(0) == 0)
    def _():
        which = 1 - core if other else core
        turned[...] = acts[pl.ds(pl.multiple_of(which * half, half), half), :].T

    out[...] = dot(b[...], turned[...])


def codes_call(other, acts, proj_b):
    (tokens, wide), rank = acts.shape, proj_b.shape[0]
    half, step = tokens // 2, 512
    return pl.pallas_call(
        functools.partial(codes_kernel, other),
        grid=(rank // step,),
        out_shape=like((rank, half), F32),
        in_specs=[
            pl.BlockSpec((tokens, wide), lambda i: (0, 0)),
            pl.BlockSpec((step, wide), lambda i: (i, 0)),
        ],
        out_specs=pl.BlockSpec((step, half), lambda i: (i, 0)),
        scratch_shapes=[pltpu.VMEM((wide, half), BF)],
        compiler_params=pltpu.CompilerParams(vmem_limit_bytes=32 * 1024 * 1024),
        cost_estimate=pl.CostEstimate(
            flops=2 * rank * wide * half, bytes_accessed=2 * rank * wide, transcendentals=0
        ),
    )(acts, proj_b)


def sum_and_copy(blocks, out):
    value = total(blocks).astype(BF)
    for i in range(out.shape[0]):
        out[i] = value


def residual_kernel(codes, near, far, a0, a1, own, message, partial, held):
    rank, outs = codes.shape[0], a0.shape[0]
    step = 256
    for j, (target, a) in enumerate(((near, a0), (far, a1))):
        for at in range(0, outs, step):
            rows = slice(at, at + step)
            left = target[rows].astype(F32) - dot(a[rows], codes[...])
            left = left.astype(BF).T
            held[:, j * outs + at : j * outs + at + step] = left
            if j == 0:
                own[:, rows] = left
            else:
                for c in range(0, step, 256):
                    message[rank + at + c : rank + at + c + 256] = left[:, c : c + 256]
    message[:rank] = codes[...]
    sub = partial.shape[1]
    for at in range(0, rank, 512):
        cols = slice(at, at + 512)
        term = dot(held[:, :outs], a0[:, cols]) + dot(held[:, outs:], a1[:, cols])
        for i in range(partial.shape[0]):
            partial[i, :, cols] = term[i * sub : (i + 1) * sub].astype(BF)


def spread_kernel(blocks, away, own, held):
    y_lo = lax.axis_index("y_lo")
    held[...] = total(blocks).astype(BF)
    rank = held.shape[1]
    width = rank // 8
    for out, side in ((away, 1 - y_lo), (own, y_lo)):
        for x in range(4):
            start = pl.multiple_of(side * (rank // 2) + x * width, width)
            piece = held[:, pl.ds(start, width)]
            for i in range(out.shape[1]):
                out[x, i] = piece


def last_kernel(cuts, joined, grad_m, grad_o, *refs):
    parts, more, (out, turned) = refs[: len(cuts)], refs[len(cuts) : -2], refs[-2:]
    core, x = lax.axis_index("core"), lax.axis_index("x")
    half = grad_m.shape[1]
    wide = max(start + ref.shape[1] for ref, (_, start) in zip(parts, cuts))
    for k in range(4):
        row = lax.rem(x + 4 - k, 4)
        turned[k, :, pl.ds(pl.multiple_of(core * half, half), half)] = grad_m[row].T
        turned[k, :, pl.ds(pl.multiple_of((1 - core) * half, half), half)] = grad_o[row].T
    for ref in more:
        out[:, wide:] = ref[...]
    edges = sorted({start for _, start in cuts} | {wide})
    for low, high in zip(edges, edges[1:]):
        acc = None
        for ref, (k, start) in zip(parts, cuts):
            if start <= low and high <= start + ref.shape[1]:
                term = dot(turned[k], ref[:, low - start : high - start])
                acc = term if acc is None else acc + term
        out[:, low:high] = acc.astype(out.dtype)


def last_call(grad_m, grad_o, cuts, parts, dtype, *joined):
    tokens, wide = parts[0].shape
    width = grad_m.shape[2]
    return call(
        functools.partial(last_kernel, cuts, bool(joined)),
        [like((width, wide + sum(j.shape[1] for j in joined)), dtype)],
        grad_m, grad_o, *parts, *joined,
        scratch=[pltpu.VMEM((4, width, tokens), BF)],
        flops=8 * tokens * width * wide if joined else 0,
    )


def term_kernel(codes, own, message, keep, s1, s2, s3):
    x = lax.axis_index("x")
    rank, outs = codes.shape[0], own.shape[1]
    width = rank // 8
    for k, out in enumerate((keep, s1, s2, s3)):
        for side in range(2):
            start = side * (rank // 2) + lax.rem(x + k, 4) * width
            rows = pl.ds(pl.multiple_of(start, width), width)
            left, right = codes[rows, :], message[rows, :]
            for c in range(0, outs, 256):
                acc = dot(left, own[:, c : c + 256])
                acc = acc + dot(right, message[rank + c : rank + c + 256])
                out[side, :, c : c + 256] = acc.astype(out.dtype)


def term_sum_kernel(keep, r1, r2, r3, own, away):
    y_lo = lax.axis_index("y_lo")
    for out, side in ((own, y_lo), (away, 1 - y_lo)):
        value = keep[side]
        for r in (r1, r2, r3):
            value = value + r[side].astype(F32)
        out[...] = value.astype(out.dtype)


def local(acts, target, proj_b, proj_a):
    core = lax.axis_index("core")
    tokens, rank = acts.shape[0], proj_b.shape[0]
    outs, wide = target.shape[1], acts.shape[1]
    half, sub, width = tokens // 2, tokens // 16, rank // 8
    scale = -2.0 / (tokens * 8)

    def part_of(array, which, size, axis):
        return lax.dynamic_slice_in_dim(array, which * size, size, axis)

    barrier = lax.optimization_barrier
    c1, c2, c3 = 1152, 384, 896
    plus_a = shift(acts[:, :c1], "x", 4, 1)
    minus_a = shift(acts[:, wide - c1 :], "x", 4, 3)
    pair_a = swap(proj_a, "core")
    target_t = target.T
    near_t = part_of(target_t, core, half, 1)
    pair_t = swap(part_of(target_t, 1 - core, half, 1), "core")

    arrived = swap(codes_call(True, acts, proj_b), "core")
    mine = (codes_call(False, acts, proj_b) + arrived).astype(BF).reshape(8, width, half)
    blocks = lax.all_to_all(mine, ZY, 0, 0)
    blocks, plus_a, minus_a, later = barrier((blocks, plus_a, minus_a, acts))
    plus_b = shift(later[:, c1:], "x", 4, 1)
    minus_b = shift(later[:, : wide - c1], "x", 4, 3)
    far_a = shift(plus_a[:, :c2], "x", 4, 1), shift(minus_a[:, c1 - c2 :], "x", 4, 3)
    codes = call(sum_and_copy, [like((8, width, half))], blocks)
    codes = lax.all_to_all(codes, ZY, 0, 0).reshape(rank, half)

    own, message, partial = call(
        residual_kernel,
        [like((half, outs)), like((rank + outs, half)), like((8, sub, rank))],
        codes, near_t, pair_t, proj_a, pair_a,
        scratch=[pltpu.VMEM((half, 2 * outs), BF)],
        flops=8 * half * rank * outs,
    )
    partial, plus_a, minus_a, plus_b, minus_b, far_a = barrier((partial, plus_a, minus_a, plus_b, minus_b, far_a))
    far_b = (
        shift(plus_a[:, c2:c3], "x", 4, 1),
        shift(minus_a[:, c1 - c3 : c1 - c2], "x", 4, 3),
    )
    blocks = lax.all_to_all(partial, ZY, 0, 0)

    piece = like((2, width, outs))
    terms = call(
        term_kernel,
        [like(piece.shape, F32), piece, piece, piece],
        codes, own, swap(message, "core"),
        flops=2 * tokens * rank * outs,
    )
    terms = [terms[0]] + [shift(terms[k], "x", 4, k) for k in (1, 2, 3)]

    spread = like((4, 8, sub, width))
    split_a, split_o = call(spread_kernel, [spread, spread], blocks, scratch=[pltpu.VMEM((sub, rank), BF)])

    def gather(split):
        split = lax.all_to_all(split.reshape(32, sub, width), ("x", "z", "y_hi"), 0, 0)
        return split.reshape(4, half, width)

    grad = gather(split_a)
    grad, far_b, *terms = barrier((grad, far_b, *terms))
    term_o, term_a = call(term_sum_kernel, [like((width, outs), F32), like((width, outs))], *terms)
    parts = [acts, plus_a, plus_b, far_a[0], far_b[0], far_b[1], far_a[1], minus_b, minus_a]
    cuts = ((0, 0), (1, 0), (1, c1), (2, 0), (2, c2), (2, c3), (2, wide - c2), (3, 0), (3, wide - c1))
    away = last_call(grad, swap(grad, "core"), cuts, parts, BF, term_a)
    away, split_o = barrier((away, split_o))
    away = swap(away, "y_lo").astype(F32)
    grad = gather(split_o)
    here = last_call(grad, swap(grad, "core"), cuts, parts, F32)
    here, term_o = barrier((here, term_o))
    return (((term_o + away[:, wide:]) * scale).T, (here + away[:, :wide]) * scale)


def solution(mesh):
    fine = Mesh(np.reshape(mesh.devices, (2, 4, 4, 2, 2)), ("y_lo", "x", "z", "y_hi", "core"))
    return jax.shard_map(
        local,
        mesh=fine,
        in_specs=(P(TOK, CHAN), P(TOK, CHAN), P(None, CHAN), P(CHAN, None)),
        out_specs=(P(CHAN, TOK), P(TOK, CHAN)),
        check_vma=False,
    )
```

```python
import functools

import jax
import jax.numpy as jnp
import numpy as np
from jax import lax
from jax.experimental import pallas as pl
from jax.experimental.pallas import tpu as pltpu
from jax.sharding import Mesh, PartitionSpec as P

BF, F32 = jnp.bfloat16, jnp.float32
TOK, CHAN, ZY = ("y_lo", "x"), ("z", "y_hi", "core"), ("z", "y_hi")
VMEM = pl.BlockSpec(memory_space=pltpu.VMEM)
ANY = pl.BlockSpec(memory_space=pl.ANY)


def dot(left, right, left_dim=1, right_dim=0):
    return lax.dot_general(
        left, right, (((left_dim,), (right_dim,)), ((), ())), preferred_element_type=F32
    )


def shift(array, axis, size, step):
    return lax.ppermute(array, axis, [(i, (i + step) % size) for i in range(size)])


def swap(array, axis):
    return shift(array, axis, 2, 1)


def call(body, outs, *args, scratch=(), flops=0):
    moved = sum(a.size * a.dtype.itemsize for a in list(args) + list(outs))
    return pl.pallas_call(
        body,
        out_shape=outs if len(outs) > 1 else outs[0],
        in_specs=[VMEM] * len(args),
        out_specs=[VMEM] * len(outs) if len(outs) > 1 else VMEM,
        scratch_shapes=scratch,
        compiler_params=pltpu.CompilerParams(vmem_limit_bytes=16 * 1024 * 1024),
        cost_estimate=pl.CostEstimate(flops=flops, bytes_accessed=moved, transcendentals=0),
    )(*args)


def like(shape, dtype=BF):
    return jax.ShapeDtypeStruct(shape, dtype)


def total(ref, at=slice(None)):
    out = ref[0, at].astype(F32)
    for i in range(1, ref.shape[0]):
        out = out + ref[i, at].astype(F32)
    return out


def codes_kernel(other, acts, b, out, turned):
    core, half = lax.axis_index("core"), turned.shape[1]

    @pl.when(pl.program_id(0) == 0)
    def _():
        which = 1 - core if other else core
        turned[...] = acts[pl.ds(pl.multiple_of(which * half, half), half), :].T

    out[...] = dot(b[...], turned[...])


def codes_call(other, acts, proj_b):
    (tokens, wide), rank = acts.shape, proj_b.shape[0]
    half, step = tokens // 2, 512
    return pl.pallas_call(
        functools.partial(codes_kernel, other),
        grid=(rank // step,),
        out_shape=like((rank, half), F32),
        in_specs=[
            pl.BlockSpec((tokens, wide), lambda i: (0, 0)),
            pl.BlockSpec((step, wide), lambda i: (i, 0)),
        ],
        out_specs=pl.BlockSpec((step, half), lambda i: (i, 0)),
        scratch_shapes=[pltpu.VMEM((wide, half), BF)],
        compiler_params=pltpu.CompilerParams(vmem_limit_bytes=32 * 1024 * 1024),
        cost_estimate=pl.CostEstimate(
            flops=2 * rank * wide * half, bytes_accessed=2 * rank * wide, transcendentals=0
        ),
    )(acts, proj_b)


def sum_and_copy(blocks, out):
    value = total(blocks).astype(BF)
    for i in range(out.shape[0]):
        out[i] = value


def residual_kernel(codes, near, far, a0, a1, own, message, partial, held):
    rank, outs = codes.shape[0], a0.shape[0]
    step = 256
    for j, (target, a) in enumerate(((near, a0), (far, a1))):
        for at in range(0, outs, step):
            rows = slice(at, at + step)
            left = target[rows].astype(F32) - dot(a[rows], codes[...])
            left = left.astype(BF).T
            held[:, j * outs + at : j * outs + at + step] = left
            if j == 0:
                own[:, rows] = left
            else:
                for c in range(0, step, 256):
                    message[rank + at + c : rank + at + c + 256] = left[:, c : c + 256]
    message[:rank] = codes[...]
    sub = partial.shape[1]
    for at in range(0, rank, 512):
        cols = slice(at, at + 512)
        term = dot(held[:, :outs], a0[:, cols]) + dot(held[:, outs:], a1[:, cols])
        for i in range(partial.shape[0]):
            partial[i, :, cols] = term[i * sub : (i + 1) * sub].astype(BF)


def spread_kernel(blocks, out, held):
    y_lo = lax.axis_index("y_lo")
    held[...] = total(blocks).astype(BF)
    rank = held.shape[1]
    width = rank // 8
    for at, side in ((0, 1 - y_lo), (width, y_lo)):
        for x in range(4):
            start = pl.multiple_of(side * (rank // 2) + x * width, width)
            piece = held[:, pl.ds(start, width)]
            for i in range(out.shape[1]):
                out[x, i, :, at : at + width] = piece


def last_kernel(cuts, side, other, more, grad, *refs):
    parts, before, (out, turned) = refs[: len(cuts)], refs[len(cuts) : -2], refs[-2:]
    core, x = lax.axis_index("core"), lax.axis_index("x")
    half, width = grad.shape[1], out.shape[0]
    wide = max(start + ref.shape[1] for ref, (_, start) in zip(parts, cuts))
    rows = pl.ds(pl.multiple_of((1 - core if other else core) * half, half), half)
    for k in range(4):
        turned[k] = grad[lax.rem(x + 4 - k, 4), :, side * width : (side + 1) * width].T
    for ref in before[1:]:
        out[:, wide:] = ref[...]
    edges = sorted({start for _, start in cuts} | {wide})
    for low, high in zip(edges, edges[1:]):
        acc = before[0][:, low:high] if other else None
        for ref, (k, start) in zip(parts, cuts):
            if start <= low and high <= start + ref.shape[1]:
                term = dot(turned[k], ref[rows, low - start : high - start])
                acc = term if acc is None else acc + term
        out[:, low:high] = acc.astype(out.dtype)


def last_call(grad_m, grad_o, cuts, parts, side, dtype, *joined):
    tokens, wide = parts[0].shape
    half, width = tokens // 2, grad_m.shape[2] // 2
    scratch = [pltpu.VMEM((4, width, half), BF)]
    flops = 4 * tokens * width * wide
    first = call(
        functools.partial(last_kernel, cuts, side, False, 0),
        [like((width, wide), F32)],
        grad_m, *parts, scratch=scratch, flops=flops,
    )
    return call(
        functools.partial(last_kernel, cuts, side, True, len(joined)),
        [like((width, wide + sum(j.shape[1] for j in joined)), dtype)],
        grad_o, *parts, first, *joined, scratch=scratch, flops=flops,
    )


def term_kernel(codes, own, message, keep, s1, s2, s3):
    x = lax.axis_index("x")
    rank, outs = codes.shape[0], own.shape[1]
    width = rank // 8
    for k, out in enumerate((keep, s1, s2, s3)):
        for side in range(2):
            start = side * (rank // 2) + lax.rem(x + k, 4) * width
            rows = pl.ds(pl.multiple_of(start, width), width)
            left, right = codes[rows, :], message[rows, :]
            for c in range(0, outs, 256):
                acc = dot(left, own[:, c : c + 256])
                acc = acc + dot(right, message[rank + c : rank + c + 256])
                out[side, :, c : c + 256] = acc.astype(out.dtype)


def term_sum_kernel(keep, r1, r2, r3, own, away):
    y_lo = lax.axis_index("y_lo")
    for out, side in ((own, y_lo), (away, 1 - y_lo)):
        value = keep[side]
        for r in (r1, r2, r3):
            value = value + r[side].astype(F32)
        out[...] = value.astype(out.dtype)


def local(acts, target, proj_b, proj_a):
    core = lax.axis_index("core")
    tokens, rank = acts.shape[0], proj_b.shape[0]
    outs, wide = target.shape[1], acts.shape[1]
    half, sub, width = tokens // 2, tokens // 16, rank // 8
    scale = -2.0 / (tokens * 8)

    def part_of(array, which, size, axis):
        return lax.dynamic_slice_in_dim(array, which * size, size, axis)

    barrier = lax.optimization_barrier
    c1, c2, c3 = 1152, 384, 896
    plus_a = shift(acts[:, :c1], "x", 4, 1)
    minus_a = shift(acts[:, wide - c1 :], "x", 4, 3)
    pair_a = swap(proj_a, "core")
    target_t = target.T
    near_t = part_of(target_t, core, half, 1)
    pair_t = swap(part_of(target_t, 1 - core, half, 1), "core")

    arrived = swap(codes_call(True, acts, proj_b), "core")
    mine = (codes_call(False, acts, proj_b) + arrived).astype(BF).reshape(8, width, half)
    blocks = lax.all_to_all(mine, ZY, 0, 0)
    blocks, plus_a, minus_a, later, pair_a, pair_t = barrier((blocks, plus_a, minus_a, acts, pair_a, pair_t))
    plus_b = shift(later[:, c1:], "x", 4, 1)
    minus_b = shift(later[:, : wide - c1], "x", 4, 3)
    far_a = shift(plus_a[:, :c2], "x", 4, 1), shift(minus_a[:, c1 - c2 :], "x", 4, 3)
    codes = call(sum_and_copy, [like((8, width, half))], blocks)
    codes = lax.all_to_all(codes, ZY, 0, 0).reshape(rank, half)

    own, message, partial = call(
        residual_kernel,
        [like((half, outs)), like((rank + outs, half)), like((8, sub, rank))],
        codes, near_t, pair_t, proj_a, pair_a,
        scratch=[pltpu.VMEM((half, 2 * outs), BF)],
        flops=8 * half * rank * outs,
    )
    partial, plus_a, minus_a, plus_b, minus_b, far_a = barrier((partial, plus_a, minus_a, plus_b, minus_b, far_a))
    far_b = (
        shift(plus_a[:, c2:c3], "x", 4, 1),
        shift(minus_a[:, c1 - c3 : c1 - c2], "x", 4, 3),
    )
    blocks = lax.all_to_all(partial, ZY, 0, 0)

    piece = like((2, width, outs))
    terms = call(
        term_kernel,
        [like(piece.shape, F32), piece, piece, piece],
        codes, own, swap(message, "core"),
        flops=2 * tokens * rank * outs,
    )
    terms = [terms[0]] + [shift(terms[k], "x", 4, k) for k in (1, 2, 3)]

    split = call(spread_kernel, [like((4, 8, sub, 2 * width))], blocks, scratch=[pltpu.VMEM((sub, rank), BF)])
    grad = lax.all_to_all(split.reshape(32, sub, 2 * width), ("x", "z", "y_hi"), 0, 0)
    grad = grad.reshape(4, half, 2 * width)
    grad, far_b, *terms = barrier((grad, far_b, *terms))
    grad_o = swap(grad, "core")
    term_o, term_a = call(term_sum_kernel, [like((width, outs), F32), like((width, outs))], *terms)
    parts = [acts, plus_a, plus_b, far_a[0], far_b[0], far_b[1], far_a[1], minus_b, minus_a]
    cuts = ((0, 0), (1, 0), (1, c1), (2, 0), (2, c2), (2, c3), (2, wide - c2), (3, 0), (3, wide - c1))
    away = last_call(grad, grad_o, cuts, parts, 0, BF, term_a)
    away = swap(away, "y_lo").astype(F32)
    here = last_call(grad, grad_o, cuts, parts, 1, F32)
    here, term_o = barrier((here, term_o))
    return (((term_o + away[:, wide:]) * scale).T, (here + away[:, :wide]) * scale)


def solution(mesh):
    fine = Mesh(np.reshape(mesh.devices, (2, 4, 4, 2, 2)), ("y_lo", "x", "z", "y_hi", "core"))
    return jax.shard_map(
        local,
        mesh=fine,
        in_specs=(P(TOK, CHAN), P(TOK, CHAN), P(None, CHAN), P(CHAN, None)),
        out_specs=(P(CHAN, TOK), P(TOK, CHAN)),
        check_vma=False,
    )
```

```python
import functools

import jax
import jax.numpy as jnp
import numpy as np
from jax import lax
from jax.experimental import pallas as pl
from jax.experimental.pallas import tpu as pltpu
from jax.sharding import Mesh, PartitionSpec as P

BF, F32 = jnp.bfloat16, jnp.float32
TOK, CHAN, ZY = ("y_lo", "x"), ("z", "y_hi", "core"), ("z", "y_hi")
VMEM = pl.BlockSpec(memory_space=pltpu.VMEM)
ANY = pl.BlockSpec(memory_space=pl.ANY)


def dot(left, right, left_dim=1, right_dim=0):
    return lax.dot_general(
        left, right, (((left_dim,), (right_dim,)), ((), ())), preferred_element_type=F32
    )


def shift(array, axis, size, step):
    return lax.ppermute(array, axis, [(i, (i + step) % size) for i in range(size)])


def swap(array, axis):
    return shift(array, axis, 2, 1)


def call(body, outs, *args, scratch=(), flops=0):
    moved = sum(a.size * a.dtype.itemsize for a in list(args) + list(outs))
    return pl.pallas_call(
        body,
        out_shape=outs if len(outs) > 1 else outs[0],
        in_specs=[VMEM] * len(args),
        out_specs=[VMEM] * len(outs) if len(outs) > 1 else VMEM,
        scratch_shapes=scratch,
        compiler_params=pltpu.CompilerParams(vmem_limit_bytes=16 * 1024 * 1024),
        cost_estimate=pl.CostEstimate(flops=flops, bytes_accessed=moved, transcendentals=0),
    )(*args)


def like(shape, dtype=BF):
    return jax.ShapeDtypeStruct(shape, dtype)


def total(ref, at=slice(None)):
    out = ref[0, at].astype(F32)
    for i in range(1, ref.shape[0]):
        out = out + ref[i, at].astype(F32)
    return out


def codes_kernel(other, acts, b, out, turned):
    core, half = lax.axis_index("core"), turned.shape[1]

    @pl.when(pl.program_id(0) == 0)
    def _():
        which = 1 - core if other else core
        turned[...] = acts[pl.ds(pl.multiple_of(which * half, half), half), :].T

    out[...] = dot(b[...], turned[...])


def codes_call(other, acts, proj_b):
    (tokens, wide), rank = acts.shape, proj_b.shape[0]
    half, step = tokens // 2, 512
    return pl.pallas_call(
        functools.partial(codes_kernel, other),
        grid=(rank // step,),
        out_shape=like((rank, half), F32),
        in_specs=[
            pl.BlockSpec((tokens, wide), lambda i: (0, 0)),
            pl.BlockSpec((step, wide), lambda i: (i, 0)),
        ],
        out_specs=pl.BlockSpec((step, half), lambda i: (i, 0)),
        scratch_shapes=[pltpu.VMEM((wide, half), BF)],
        compiler_params=pltpu.CompilerParams(vmem_limit_bytes=32 * 1024 * 1024),
        cost_estimate=pl.CostEstimate(
            flops=2 * rank * wide * half, bytes_accessed=2 * rank * wide, transcendentals=0
        ),
    )(acts, proj_b)


def sum_and_copy(blocks, out):
    value = total(blocks).astype(BF)
    for i in range(out.shape[0]):
        out[i] = value


def residual_kernel(codes, near, far, a0, a1, own, message, partial, held):
    rank, outs = codes.shape[0], a0.shape[0]
    step = 256
    for j, (target, a) in enumerate(((near, a0), (far, a1))):
        for at in range(0, outs, step):
            rows = slice(at, at + step)
            left = target[rows].astype(F32) - dot(a[rows], codes[...])
            left = left.astype(BF).T
            held[:, j * outs + at : j * outs + at + step] = left
            if j == 0:
                own[:, rows] = left
            else:
                for c in range(0, step, 256):
                    message[rank + at + c : rank + at + c + 256] = left[:, c : c + 256]
    message[:rank] = codes[...]
    sub = partial.shape[1]
    for at in range(0, rank, 512):
        cols = slice(at, at + 512)
        term = dot(held[:, :outs], a0[:, cols]) + dot(held[:, outs:], a1[:, cols])
        for i in range(partial.shape[0]):
            partial[i, :, cols] = term[i * sub : (i + 1) * sub].astype(BF)


def spread_kernel(blocks, out, held):
    y_lo = lax.axis_index("y_lo")
    held[...] = total(blocks).astype(BF)
    rank = held.shape[1]
    width = rank // 8
    for at, side in ((0, 1 - y_lo), (width, y_lo)):
        for x in range(4):
            start = pl.multiple_of(side * (rank // 2) + x * width, width)
            piece = held[:, pl.ds(start, width)]
            for i in range(out.shape[1]):
                out[x, i, :, at : at + width] = piece


def hold_kernel(row, out, sems):
    parts = sems.shape[0]
    copies = [pltpu.make_async_copy(row.at[i], out.at[i], sems.at[i]) for i in range(parts)]
    for copy in copies:
        copy.start()
    for copy in copies:
        copy.wait()


def hold(row):
    return pl.pallas_call(
        hold_kernel,
        out_shape=like(row.shape),
        in_specs=[ANY],
        out_specs=VMEM,
        scratch_shapes=[pltpu.SemaphoreType.DMA((row.shape[0],))],
        compiler_params=pltpu.CompilerParams(vmem_limit_bytes=16 * 1024 * 1024),
        cost_estimate=pl.CostEstimate(flops=0, bytes_accessed=4 * row.size, transcendentals=0),
    )(row)


def last_kernel(side, other, grad, acts, *refs):
    before, (out, turned) = refs[:-2], refs[-2:]
    core = lax.axis_index("core")
    half, wide, width = grad.shape[1], acts.shape[2], out.shape[0]
    rows = pl.ds(pl.multiple_of((1 - core if other else core) * half, half), half)
    for k in range(4):
        turned[k] = grad[k, :, side * width : (side + 1) * width].T
    for ref in before[1:]:
        out[:, wide:] = ref[...]
    for c in range(0, wide, 256):
        cols = slice(c, c + 256)
        acc = dot(turned[0], acts[0, rows, cols])
        for k in range(1, 4):
            acc = acc + dot(turned[k], acts[k, rows, cols])
        if other:
            acc = acc + before[0][:, cols]
        out[:, cols] = acc.astype(out.dtype)


def last_call(grad_m, grad_o, held, side, dtype, *joined):
    _, tokens, wide = held.shape
    half, width = tokens // 2, grad_m.shape[2] // 2
    scratch = [pltpu.VMEM((4, width, half), BF)]
    flops = 4 * tokens * width * wide
    first = call(
        functools.partial(last_kernel, side, False),
        [like((width, wide), F32)],
        grad_m, held, scratch=scratch, flops=flops,
    )
    return call(
        functools.partial(last_kernel, side, True),
        [like((width, wide + sum(j.shape[1] for j in joined)), dtype)],
        grad_o, held, first, *joined, scratch=scratch, flops=flops,
    )


def term_kernel(codes, own, message, keep, s1, s2, s3):
    x = lax.axis_index("x")
    rank, outs = codes.shape[0], own.shape[1]
    width = rank // 8
    for k, out in enumerate((keep, s1, s2, s3)):
        for side in range(2):
            start = side * (rank // 2) + lax.rem(x + k, 4) * width
            rows = pl.ds(pl.multiple_of(start, width), width)
            left, right = codes[rows, :], message[rows, :]
            for c in range(0, outs, 256):
                acc = dot(left, own[:, c : c + 256])
                acc = acc + dot(right, message[rank + c : rank + c + 256])
                out[side, :, c : c + 256] = acc.astype(out.dtype)


def term_sum_kernel(keep, r1, r2, r3, own, away):
    y_lo = lax.axis_index("y_lo")
    for out, side in ((own, y_lo), (away, 1 - y_lo)):
        value = keep[side]
        for r in (r1, r2, r3):
            value = value + r[side].astype(F32)
        out[...] = value.astype(out.dtype)


def local(acts, target, proj_b, proj_a):
    core = lax.axis_index("core")
    tokens, rank = acts.shape[0], proj_b.shape[0]
    outs, wide = target.shape[1], acts.shape[1]
    half, sub, width = tokens // 2, tokens // 16, rank // 8
    scale = -2.0 / (tokens * 8)

    def part_of(array, which, size, axis):
        return lax.dynamic_slice_in_dim(array, which * size, size, axis)

    row = lax.all_gather(acts, "x")
    pair_a = swap(proj_a, "core")
    target_t = target.T
    near_t = part_of(target_t, core, half, 1)
    pair_t = swap(part_of(target_t, 1 - core, half, 1), "core")

    arrived = swap(codes_call(True, acts, proj_b), "core")
    mine = (codes_call(False, acts, proj_b) + arrived).astype(BF).reshape(8, width, half)
    blocks = lax.all_to_all(mine, ZY, 0, 0)
    codes = call(sum_and_copy, [like((8, width, half))], blocks)
    codes = lax.all_to_all(codes, ZY, 0, 0).reshape(rank, half)

    own, message, partial = call(
        residual_kernel,
        [like((half, outs)), like((rank + outs, half)), like((8, sub, rank))],
        codes, near_t, pair_t, proj_a, pair_a,
        scratch=[pltpu.VMEM((half, 2 * outs), BF)],
        flops=8 * half * rank * outs,
    )
    blocks = lax.all_to_all(partial, ZY, 0, 0)

    piece = like((2, width, outs))
    terms = call(
        term_kernel,
        [like(piece.shape, F32), piece, piece, piece],
        codes, own, swap(message, "core"),
        flops=2 * tokens * rank * outs,
    )
    terms = [terms[0]] + [shift(terms[k], "x", 4, k) for k in (1, 2, 3)]

    barrier = lax.optimization_barrier
    blocks, row = barrier((blocks, row))
    split = call(spread_kernel, [like((4, 8, sub, 2 * width))], blocks, scratch=[pltpu.VMEM((sub, rank), BF)])
    split, row = barrier((split, row))
    held = hold(row)
    grad = lax.all_to_all(split.reshape(32, sub, 2 * width), ("x", "z", "y_hi"), 0, 0)
    grad = grad.reshape(4, half, 2 * width)
    grad, held, *terms = barrier((grad, held, *terms))
    grad_o = swap(grad, "core")
    term_o, term_a = call(term_sum_kernel, [like((width, outs), F32), like((width, outs))], *terms)
    away = swap(last_call(grad, grad_o, held, 0, BF, term_a), "y_lo").astype(F32)
    here = last_call(grad, grad_o, held, 1, F32)
    here, term_o = barrier((here, term_o))
    return (((term_o + away[:, wide:]) * scale).T, (here + away[:, :wide]) * scale)


def solution(mesh):
    fine = Mesh(np.reshape(mesh.devices, (2, 4, 4, 2, 2)), ("y_lo", "x", "z", "y_hi", "core"))
    return jax.shard_map(
        local,
        mesh=fine,
        in_specs=(P(TOK, CHAN), P(TOK, CHAN), P(None, CHAN), P(CHAN, None)),
        out_specs=(P(CHAN, TOK), P(TOK, CHAN)),
        check_vma=False,
    )
```

```python
import functools

import jax
import jax.numpy as jnp
import numpy as np
from jax import lax
from jax.experimental import pallas as pl
from jax.experimental.pallas import tpu as pltpu
from jax.sharding import Mesh, PartitionSpec as P

BF, F32 = jnp.bfloat16, jnp.float32
TOK, CHAN, ZY = ("y_lo", "x"), ("z", "y_hi", "core"), ("z", "y_hi")
VMEM = pl.BlockSpec(memory_space=pltpu.VMEM)
ANY = pl.BlockSpec(memory_space=pl.ANY)


def dot(left, right, left_dim=1, right_dim=0):
    return lax.dot_general(
        left, right, (((left_dim,), (right_dim,)), ((), ())), preferred_element_type=F32
    )


def shift(array, axis, size, step):
    return lax.ppermute(array, axis, [(i, (i + step) % size) for i in range(size)])


def swap(array, axis):
    return shift(array, axis, 2, 1)


def call(body, outs, *args, scratch=(), flops=0):
    moved = sum(a.size * a.dtype.itemsize for a in list(args) + list(outs))
    return pl.pallas_call(
        body,
        out_shape=outs if len(outs) > 1 else outs[0],
        in_specs=[VMEM] * len(args),
        out_specs=[VMEM] * len(outs) if len(outs) > 1 else VMEM,
        scratch_shapes=scratch,
        compiler_params=pltpu.CompilerParams(vmem_limit_bytes=16 * 1024 * 1024),
        cost_estimate=pl.CostEstimate(flops=flops, bytes_accessed=moved, transcendentals=0),
    )(*args)


def like(shape, dtype=BF):
    return jax.ShapeDtypeStruct(shape, dtype)


def total(ref, at=slice(None)):
    out = ref[0, at].astype(F32)
    for i in range(1, ref.shape[0]):
        out = out + ref[i, at].astype(F32)
    return out


def codes_kernel(other, acts, b, out, turned):
    core, half = lax.axis_index("core"), turned.shape[1]

    @pl.when(pl.program_id(0) == 0)
    def _():
        which = 1 - core if other else core
        turned[...] = acts[pl.ds(pl.multiple_of(which * half, half), half), :].T

    out[...] = dot(b[...], turned[...])


def codes_call(other, acts, proj_b):
    (tokens, wide), rank = acts.shape, proj_b.shape[0]
    half, step = tokens // 2, 512
    return pl.pallas_call(
        functools.partial(codes_kernel, other),
        grid=(rank // step,),
        out_shape=like((rank, half), F32),
        in_specs=[
            pl.BlockSpec((tokens, wide), lambda i: (0, 0)),
            pl.BlockSpec((step, wide), lambda i: (i, 0)),
        ],
        out_specs=pl.BlockSpec((step, half), lambda i: (i, 0)),
        scratch_shapes=[pltpu.VMEM((wide, half), BF)],
        compiler_params=pltpu.CompilerParams(vmem_limit_bytes=32 * 1024 * 1024),
        cost_estimate=pl.CostEstimate(
            flops=2 * rank * wide * half, bytes_accessed=2 * rank * wide, transcendentals=0
        ),
    )(acts, proj_b)


def sum_and_copy(blocks, out):
    value = total(blocks).astype(BF)
    for i in range(out.shape[0]):
        out[i] = value


def residual_kernel(codes, near, far, a0, a1, own, message, partial, held):
    rank, outs = codes.shape[0], a0.shape[0]
    step = 256
    for j, (target, a) in enumerate(((near, a0), (far, a1))):
        for at in range(0, outs, step):
            rows = slice(at, at + step)
            left = target[rows].astype(F32) - dot(a[rows], codes[...])
            left = left.astype(BF).T
            held[:, j * outs + at : j * outs + at + step] = left
            if j == 0:
                own[:, rows] = left
            else:
                for c in range(0, step, 256):
                    message[rank + at + c : rank + at + c + 256] = left[:, c : c + 256]
    message[:rank] = codes[...]
    sub = partial.shape[1]
    for at in range(0, rank, 512):
        cols = slice(at, at + 512)
        term = dot(held[:, :outs], a0[:, cols]) + dot(held[:, outs:], a1[:, cols])
        for i in range(partial.shape[0]):
            partial[i, :, cols] = term[i * sub : (i + 1) * sub].astype(BF)


def spread_kernel(blocks, out, held):
    y_lo = lax.axis_index("y_lo")
    held[...] = total(blocks).astype(BF)
    rank = held.shape[1]
    width = rank // 8
    for at, side in ((0, 1 - y_lo), (width, y_lo)):
        for x in range(4):
            start = pl.multiple_of(side * (rank // 2) + x * width, width)
            piece = held[:, pl.ds(start, width)]
            for i in range(out.shape[1]):
                out[x, i, :, at : at + width] = piece


def last_kernel(side, other, grad, acts, *refs):
    before, (out, turned, held, sems) = refs[:-4], refs[-4:]
    core = lax.axis_index("core")
    half, wide, width = grad.shape[1], acts.shape[2], out.shape[0]
    step, flight = held.shape[3], 4
    start = pl.multiple_of((1 - core if other else core) * half, half)
    copies = [
        pltpu.make_async_copy(
            acts.at[:, pl.ds(start, half), pl.ds(i * step, step)], held.at[i], sems.at[i]
        )
        for i in range(wide // step)
    ]
    for copy in copies[:flight]:
        copy.start()
    for k in range(4):
        turned[k] = grad[k, :, side * width : (side + 1) * width].T
    for ref in before[1:]:
        out[:, wide:] = ref[...]
    for i, copy in enumerate(copies):
        copy.wait()
        if i + flight < len(copies):
            copies[i + flight].start()
        cols = slice(i * step, (i + 1) * step)
        acc = dot(turned[0], held[i, 0])
        for k in range(1, 4):
            acc = acc + dot(turned[k], held[i, k])
        if other:
            acc = acc + before[0][:, cols]
        out[:, cols] = acc.astype(out.dtype)


def last_call(grad_m, grad_o, row, side, dtype, *joined):
    _, tokens, wide = row.shape
    half, width, step = tokens // 2, grad_m.shape[2] // 2, 256

    def part(other, out, grad, *more):
        return pl.pallas_call(
            functools.partial(last_kernel, side, other),
            out_shape=out,
            in_specs=[VMEM, ANY] + [VMEM] * len(more),
            out_specs=VMEM,
            scratch_shapes=[
                pltpu.VMEM((4, width, half), BF),
                pltpu.VMEM((wide // step, 4, half, step), BF),
                pltpu.SemaphoreType.DMA((wide // step,)),
            ],
            compiler_params=pltpu.CompilerParams(vmem_limit_bytes=32 * 1024 * 1024),
            cost_estimate=pl.CostEstimate(
                flops=4 * tokens * width * wide, bytes_accessed=4 * tokens * wide, transcendentals=0
            ),
        )(grad, row, *more)

    first = part(False, like((width, wide), F32), grad_m)
    shape = (width, wide + sum(j.shape[1] for j in joined))
    return part(True, like(shape, dtype), grad_o, first, *joined)


def term_kernel(codes, own, message, keep, s1, s2, s3):
    x = lax.axis_index("x")
    rank, outs = codes.shape[0], own.shape[1]
    width = rank // 8
    for k, out in enumerate((keep, s1, s2, s3)):
        for side in range(2):
            start = side * (rank // 2) + lax.rem(x + k, 4) * width
            rows = pl.ds(pl.multiple_of(start, width), width)
            left, right = codes[rows, :], message[rows, :]
            for c in range(0, outs, 256):
                acc = dot(left, own[:, c : c + 256])
                acc = acc + dot(right, message[rank + c : rank + c + 256])
                out[side, :, c : c + 256] = acc.astype(out.dtype)


def term_sum_kernel(keep, r1, r2, r3, own, away):
    y_lo = lax.axis_index("y_lo")
    for out, side in ((own, y_lo), (away, 1 - y_lo)):
        value = keep[side]
        for r in (r1, r2, r3):
            value = value + r[side].astype(F32)
        out[...] = value.astype(out.dtype)


def local(acts, target, proj_b, proj_a):
    core = lax.axis_index("core")
    tokens, rank = acts.shape[0], proj_b.shape[0]
    outs, wide = target.shape[1], acts.shape[1]
    half, sub, width = tokens // 2, tokens // 16, rank // 8
    scale = -2.0 / (tokens * 8)

    def part_of(array, which, size, axis):
        return lax.dynamic_slice_in_dim(array, which * size, size, axis)

    row = lax.all_gather(acts, "x")
    pair_a = swap(proj_a, "core")
    target_t = target.T
    near_t = part_of(target_t, core, half, 1)
    pair_t = swap(part_of(target_t, 1 - core, half, 1), "core")

    arrived = swap(codes_call(True, acts, proj_b), "core")
    mine = (codes_call(False, acts, proj_b) + arrived).astype(BF).reshape(8, width, half)
    blocks = lax.all_to_all(mine, ZY, 0, 0)
    codes = call(sum_and_copy, [like((8, width, half))], blocks)
    codes = lax.all_to_all(codes, ZY, 0, 0).reshape(rank, half)

    own, message, partial = call(
        residual_kernel,
        [like((half, outs)), like((rank + outs, half)), like((8, sub, rank))],
        codes, near_t, pair_t, proj_a, pair_a,
        scratch=[pltpu.VMEM((half, 2 * outs), BF)],
        flops=8 * half * rank * outs,
    )
    blocks = lax.all_to_all(partial, ZY, 0, 0)

    piece = like((2, width, outs))
    terms = call(
        term_kernel,
        [like(piece.shape, F32), piece, piece, piece],
        codes, own, swap(message, "core"),
        flops=2 * tokens * rank * outs,
    )
    terms = [terms[0]] + [shift(terms[k], "x", 4, k) for k in (1, 2, 3)]

    barrier = lax.optimization_barrier
    blocks, row, terms[0] = barrier((blocks, row, terms[0]))
    split = call(spread_kernel, [like((4, 8, sub, 2 * width))], blocks, scratch=[pltpu.VMEM((sub, rank), BF)])
    grad = lax.all_to_all(split.reshape(32, sub, 2 * width), ("x", "z", "y_hi"), 0, 0)
    grad = grad.reshape(4, half, 2 * width)
    grad, *terms = barrier((grad, *terms))
    grad_o = swap(grad, "core")
    term_o, term_a = call(term_sum_kernel, [like((width, outs), F32), like((width, outs))], *terms)
    away = swap(last_call(grad, grad_o, row, 0, BF, term_a), "y_lo").astype(F32)
    here = last_call(grad, grad_o, row, 1, F32)
    here, term_o = barrier((here, term_o))
    return (((term_o + away[:, wide:]) * scale).T, (here + away[:, :wide]) * scale)


def solution(mesh):
    fine = Mesh(np.reshape(mesh.devices, (2, 4, 4, 2, 2)), ("y_lo", "x", "z", "y_hi", "core"))
    return jax.shard_map(
        local,
        mesh=fine,
        in_specs=(P(TOK, CHAN), P(TOK, CHAN), P(None, CHAN), P(CHAN, None)),
        out_specs=(P(CHAN, TOK), P(TOK, CHAN)),
        check_vma=False,
    )
```

```python
import functools

import jax
import jax.numpy as jnp
import numpy as np
from jax import lax
from jax.experimental import pallas as pl
from jax.experimental.pallas import tpu as pltpu
from jax.sharding import Mesh, PartitionSpec as P

BF, F32 = jnp.bfloat16, jnp.float32
TOK, CHAN, ZY = ("y_lo", "x"), ("z", "y_hi", "core"), ("z", "y_hi")
VMEM = pl.BlockSpec(memory_space=pltpu.VMEM)
ANY = pl.BlockSpec(memory_space=pl.ANY)


def dot(left, right, left_dim=1, right_dim=0):
    return lax.dot_general(
        left, right, (((left_dim,), (right_dim,)), ((), ())), preferred_element_type=F32
    )


def shift(array, axis, size, step):
    return lax.ppermute(array, axis, [(i, (i + step) % size) for i in range(size)])


def swap(array, axis):
    return shift(array, axis, 2, 1)


def call(body, outs, *args, scratch=(), flops=0):
    moved = sum(a.size * a.dtype.itemsize for a in list(args) + list(outs))
    return pl.pallas_call(
        body,
        out_shape=outs if len(outs) > 1 else outs[0],
        in_specs=[VMEM] * len(args),
        out_specs=[VMEM] * len(outs) if len(outs) > 1 else VMEM,
        scratch_shapes=scratch,
        compiler_params=pltpu.CompilerParams(vmem_limit_bytes=16 * 1024 * 1024),
        cost_estimate=pl.CostEstimate(flops=flops, bytes_accessed=moved, transcendentals=0),
    )(*args)


def like(shape, dtype=BF):
    return jax.ShapeDtypeStruct(shape, dtype)


def total(ref, at=slice(None)):
    out = ref[0, at].astype(F32)
    for i in range(1, ref.shape[0]):
        out = out + ref[i, at].astype(F32)
    return out


def codes_kernel(other, acts, b, out, turned):
    core, half = lax.axis_index("core"), turned.shape[1]

    @pl.when(pl.program_id(0) == 0)
    def _():
        which = 1 - core if other else core
        turned[...] = acts[pl.ds(pl.multiple_of(which * half, half), half), :].T

    out[...] = dot(b[...], turned[...])


def codes_call(other, acts, proj_b):
    (tokens, wide), rank = acts.shape, proj_b.shape[0]
    half, step = tokens // 2, 512
    return pl.pallas_call(
        functools.partial(codes_kernel, other),
        grid=(rank // step,),
        out_shape=like((rank, half), F32),
        in_specs=[
            pl.BlockSpec((tokens, wide), lambda i: (0, 0)),
            pl.BlockSpec((step, wide), lambda i: (i, 0)),
        ],
        out_specs=pl.BlockSpec((step, half), lambda i: (i, 0)),
        scratch_shapes=[pltpu.VMEM((wide, half), BF)],
        compiler_params=pltpu.CompilerParams(vmem_limit_bytes=32 * 1024 * 1024),
        cost_estimate=pl.CostEstimate(
            flops=2 * rank * wide * half, bytes_accessed=2 * rank * wide, transcendentals=0
        ),
    )(acts, proj_b)


def sum_and_copy(blocks, out):
    value = total(blocks).astype(BF)
    for i in range(out.shape[0]):
        out[i] = value


def residual_kernel(codes, near, far, a0, a1, own, message, partial, held):
    rank, outs = codes.shape[0], a0.shape[0]
    step = 256
    for j, (target, a) in enumerate(((near, a0), (far, a1))):
        for at in range(0, outs, step):
            rows = slice(at, at + step)
            left = target[rows].astype(F32) - dot(a[rows], codes[...])
            left = left.astype(BF).T
            held[:, j * outs + at : j * outs + at + step] = left
            if j == 0:
                own[:, rows] = left
            else:
                for c in range(0, step, 256):
                    message[rank + at + c : rank + at + c + 256] = left[:, c : c + 256]
    message[:rank] = codes[...]
    sub = partial.shape[1]
    for at in range(0, rank, 512):
        cols = slice(at, at + 512)
        term = dot(held[:, :outs], a0[:, cols]) + dot(held[:, outs:], a1[:, cols])
        for i in range(partial.shape[0]):
            partial[i, :, cols] = term[i * sub : (i + 1) * sub].astype(BF)


def spread_kernel(blocks, out, held):
    y_lo = lax.axis_index("y_lo")
    held[...] = total(blocks).astype(BF)
    rank = held.shape[1]
    width = rank // 8
    for at, side in ((0, 1 - y_lo), (width, y_lo)):
        for x in range(4):
            start = pl.multiple_of(side * (rank // 2) + x * width, width)
            piece = held[:, pl.ds(start, width)]
            for i in range(out.shape[1]):
                out[x, i, :, at : at + width] = piece


def last_kernel(side, grad_m, grad_o, acts, *refs):
    joined, (out, turned, held, sems) = refs[:-4], refs[-4:]
    core = lax.axis_index("core")
    half, wide, width = grad_m.shape[1], acts.shape[2], out.shape[0]
    step, flight = held.shape[3], 4
    copies = [
        pltpu.make_async_copy(acts.at[:, :, pl.ds(i * step, step)], held.at[i], sems.at[i])
        for i in range(wide // step)
    ]
    for copy in copies[:flight]:
        copy.start()
    at = slice(side * width, (side + 1) * width)
    for k in range(4):
        turned[k, :, pl.ds(pl.multiple_of(core * half, half), half)] = grad_m[k, :, at].T
        turned[k, :, pl.ds(pl.multiple_of((1 - core) * half, half), half)] = grad_o[k, :, at].T
    for ref in joined:
        out[:, wide:] = ref[...]
    for i, copy in enumerate(copies):
        copy.wait()
        if i + flight < len(copies):
            copies[i + flight].start()
        acc = dot(turned[0], held[i, 0])
        for k in range(1, 4):
            acc = acc + dot(turned[k], held[i, k])
        out[:, i * step : (i + 1) * step] = acc.astype(out.dtype)


def last_call(grad_m, grad_o, row, side, dtype, *joined):
    _, tokens, wide = row.shape
    width, step = grad_m.shape[2] // 2, 256
    return pl.pallas_call(
        functools.partial(last_kernel, side),
        out_shape=like((width, wide + sum(j.shape[1] for j in joined)), dtype),
        in_specs=[VMEM, VMEM, ANY] + [VMEM] * len(joined),
        out_specs=VMEM,
        scratch_shapes=[
            pltpu.VMEM((4, width, tokens), BF),
            pltpu.VMEM((wide // step, 4, tokens, step), BF),
            pltpu.SemaphoreType.DMA((wide // step,)),
        ],
        compiler_params=pltpu.CompilerParams(vmem_limit_bytes=48 * 1024 * 1024),
        cost_estimate=pl.CostEstimate(
            flops=8 * tokens * width * wide, bytes_accessed=8 * tokens * wide, transcendentals=0
        ),
    )(grad_m, grad_o, row, *joined)


def term_kernel(codes, own, message, keep, s1, s2, s3):
    x = lax.axis_index("x")
    rank, outs = codes.shape[0], own.shape[1]
    width = rank // 8
    for k, out in enumerate((keep, s1, s2, s3)):
        for side in range(2):
            start = side * (rank // 2) + lax.rem(x + k, 4) * width
            rows = pl.ds(pl.multiple_of(start, width), width)
            left, right = codes[rows, :], message[rows, :]
            for c in range(0, outs, 256):
                acc = dot(left, own[:, c : c + 256])
                acc = acc + dot(right, message[rank + c : rank + c + 256])
                out[side, :, c : c + 256] = acc.astype(out.dtype)


def term_sum_kernel(keep, r1, r2, r3, own, away):
    y_lo = lax.axis_index("y_lo")
    for out, side in ((own, y_lo), (away, 1 - y_lo)):
        value = keep[side]
        for r in (r1, r2, r3):
            value = value + r[side].astype(F32)
        out[...] = value.astype(out.dtype)


def local(acts, target, proj_b, proj_a):
    core = lax.axis_index("core")
    tokens, rank = acts.shape[0], proj_b.shape[0]
    outs, wide = target.shape[1], acts.shape[1]
    half, sub, width = tokens // 2, tokens // 16, rank // 8
    scale = -2.0 / (tokens * 8)

    def part_of(array, which, size, axis):
        return lax.dynamic_slice_in_dim(array, which * size, size, axis)

    row = lax.all_gather(acts, "x")
    pair_a = swap(proj_a, "core")
    target_t = target.T
    near_t = part_of(target_t, core, half, 1)
    pair_t = swap(part_of(target_t, 1 - core, half, 1), "core")

    arrived = swap(codes_call(True, acts, proj_b), "core")
    mine = (codes_call(False, acts, proj_b) + arrived).astype(BF).reshape(8, width, half)
    blocks = lax.all_to_all(mine, ZY, 0, 0)
    codes = call(sum_and_copy, [like((8, width, half))], blocks)
    codes = lax.all_to_all(codes, ZY, 0, 0).reshape(rank, half)

    own, message, partial = call(
        residual_kernel,
        [like((half, outs)), like((rank + outs, half)), like((8, sub, rank))],
        codes, near_t, pair_t, proj_a, pair_a,
        scratch=[pltpu.VMEM((half, 2 * outs), BF)],
        flops=8 * half * rank * outs,
    )
    blocks = lax.all_to_all(partial, ZY, 0, 0)

    piece = like((2, width, outs))
    terms = call(
        term_kernel,
        [like(piece.shape, F32), piece, piece, piece],
        codes, own, swap(message, "core"),
        flops=2 * tokens * rank * outs,
    )
    near = [shift(terms[k], "x", 4, k) for k in (1, 3)]

    barrier = lax.optimization_barrier
    blocks, row, near, later = barrier((blocks, row, near, terms[2]))
    terms = [terms[0], shift(later, "x", 4, 2)] + near
    split = call(spread_kernel, [like((4, 8, sub, 2 * width))], blocks, scratch=[pltpu.VMEM((sub, rank), BF)])
    grad = lax.all_to_all(split.reshape(32, sub, 2 * width), ("x", "z", "y_hi"), 0, 0)
    grad = grad.reshape(4, half, 2 * width)
    grad, *terms = barrier((grad, *terms))
    grad_o = swap(grad, "core")
    term_o, term_a = call(term_sum_kernel, [like((width, outs), F32), like((width, outs))], *terms)
    away = swap(last_call(grad, grad_o, row, 0, BF, term_a), "y_lo").astype(F32)
    here = last_call(grad, grad_o, row, 1, F32)
    here, term_o = barrier((here, term_o))
    return (((term_o + away[:, wide:]) * scale).T, (here + away[:, :wide]) * scale)


def solution(mesh):
    fine = Mesh(np.reshape(mesh.devices, (2, 4, 4, 2, 2)), ("y_lo", "x", "z", "y_hi", "core"))
    return jax.shard_map(
        local,
        mesh=fine,
        in_specs=(P(TOK, CHAN), P(TOK, CHAN), P(None, CHAN), P(CHAN, None)),
        out_specs=(P(CHAN, TOK), P(TOK, CHAN)),
        check_vma=False,
    )
```

```python
import functools

import jax
import jax.numpy as jnp
import numpy as np
from jax import lax
from jax.experimental import pallas as pl
from jax.experimental.pallas import tpu as pltpu
from jax.sharding import Mesh, PartitionSpec as P

BF, F32 = jnp.bfloat16, jnp.float32
TOK, CHAN, ZY = ("y_lo", "x"), ("z", "y_hi", "core"), ("z", "y_hi")
VMEM = pl.BlockSpec(memory_space=pltpu.VMEM)
ANY = pl.BlockSpec(memory_space=pl.ANY)


def dot(left, right, left_dim=1, right_dim=0):
    return lax.dot_general(
        left, right, (((left_dim,), (right_dim,)), ((), ())), preferred_element_type=F32
    )


def shift(array, axis, size, step):
    return lax.ppermute(array, axis, [(i, (i + step) % size) for i in range(size)])


def swap(array, axis):
    return shift(array, axis, 2, 1)


def call(body, outs, *args, scratch=(), flops=0):
    moved = sum(a.size * a.dtype.itemsize for a in list(args) + list(outs))
    return pl.pallas_call(
        body,
        out_shape=outs if len(outs) > 1 else outs[0],
        in_specs=[VMEM] * len(args),
        out_specs=[VMEM] * len(outs) if len(outs) > 1 else VMEM,
        scratch_shapes=scratch,
        compiler_params=pltpu.CompilerParams(vmem_limit_bytes=16 * 1024 * 1024),
        cost_estimate=pl.CostEstimate(flops=flops, bytes_accessed=moved, transcendentals=0),
    )(*args)


def like(shape, dtype=BF):
    return jax.ShapeDtypeStruct(shape, dtype)


def total(ref, at=slice(None)):
    out = ref[0, at].astype(F32)
    for i in range(1, ref.shape[0]):
        out = out + ref[i, at].astype(F32)
    return out


def codes_kernel(other, acts, b, out, turned):
    core, half = lax.axis_index("core"), turned.shape[1]

    @pl.when(pl.program_id(0) == 0)
    def _():
        which = 1 - core if other else core
        turned[...] = acts[pl.ds(pl.multiple_of(which * half, half), half), :].T

    out[...] = dot(b[...], turned[...])


def codes_call(other, acts, proj_b):
    (tokens, wide), rank = acts.shape, proj_b.shape[0]
    half, step = tokens // 2, 512
    return pl.pallas_call(
        functools.partial(codes_kernel, other),
        grid=(rank // step,),
        out_shape=like((rank, half), F32),
        in_specs=[
            pl.BlockSpec((tokens, wide), lambda i: (0, 0)),
            pl.BlockSpec((step, wide), lambda i: (i, 0)),
        ],
        out_specs=pl.BlockSpec((step, half), lambda i: (i, 0)),
        scratch_shapes=[pltpu.VMEM((wide, half), BF)],
        compiler_params=pltpu.CompilerParams(vmem_limit_bytes=32 * 1024 * 1024),
        cost_estimate=pl.CostEstimate(
            flops=2 * rank * wide * half, bytes_accessed=2 * rank * wide, transcendentals=0
        ),
    )(acts, proj_b)


def sum_and_copy(blocks, out):
    value = total(blocks).astype(BF)
    for i in range(out.shape[0]):
        out[i] = value


def residual_kernel(codes, near, far, a0, a1, own, message, partial, held):
    rank, outs = codes.shape[0], a0.shape[0]
    step = 256
    for j, (target, a) in enumerate(((near, a0), (far, a1))):
        for at in range(0, outs, step):
            rows = slice(at, at + step)
            left = target[rows].astype(F32) - dot(a[rows], codes[...])
            left = left.astype(BF).T
            held[:, j * outs + at : j * outs + at + step] = left
            if j == 0:
                own[:, rows] = left
            else:
                for c in range(0, step, 256):
                    message[rank + at + c : rank + at + c + 256] = left[:, c : c + 256]
    message[:rank] = codes[...]
    sub = partial.shape[1]
    for at in range(0, rank, 512):
        cols = slice(at, at + 512)
        term = dot(held[:, :outs], a0[:, cols]) + dot(held[:, outs:], a1[:, cols])
        for i in range(partial.shape[0]):
            partial[i, :, cols] = term[i * sub : (i + 1) * sub].astype(BF)


def spread_kernel(blocks, away, own, held):
    y_lo = lax.axis_index("y_lo")
    held[...] = total(blocks).astype(BF)
    rank = held.shape[1]
    width = rank // 8
    for out, side in ((away, 1 - y_lo), (own, y_lo)):
        for x in range(4):
            start = pl.multiple_of(side * (rank // 2) + x * width, width)
            piece = held[:, pl.ds(start, width)]
            for i in range(out.shape[1]):
                out[x, i] = piece


def last_kernel(grad_m, grad_o, r0, r1, r2, r3, *refs):
    joined, (out, picked, turned) = refs[:-3], refs[-3:]
    core, x = lax.axis_index("core"), lax.axis_index("x")
    half, wide = grad_m.shape[1], r0.shape[1]
    starts = [pl.multiple_of(which * half, half) for which in (core, 1 - core)]
    for h, grad in enumerate((grad_m, grad_o)):
        for k in range(4):
            picked[h, k] = grad[lax.rem(x + 4 - k, 4)]
    for h in range(2):
        for k in range(4):
            turned[h, k] = picked[h, k].T
    for ref in joined:
        out[:, wide:] = ref[...]
    for c in range(0, wide, 256):
        cols = slice(c, c + 256)
        acc = None
        for h in range(2):
            for k, r in enumerate((r0, r1, r2, r3)):
                term = dot(turned[h, k], r[pl.ds(starts[h], half), cols])
                acc = term if acc is None else acc + term
        out[:, cols] = acc.astype(out.dtype)


def last_call(grad_m, grad_o, row, dtype, *joined):
    (tokens, wide), (_, half, width) = row[0].shape, grad_m.shape
    return call(
        last_kernel,
        [like((width, wide + sum(j.shape[1] for j in joined)), dtype)],
        grad_m, grad_o, *row, *joined,
        scratch=[pltpu.VMEM((2, 4, half, width), BF), pltpu.VMEM((2, 4, width, half), BF)],
        flops=8 * tokens * width * wide,
    )


def term_kernel(codes, own, message, keep, s1, s2, s3):
    x = lax.axis_index("x")
    rank, outs = codes.shape[0], own.shape[1]
    width = rank // 8
    for k, out in enumerate((keep, s1, s2, s3)):
        for side in range(2):
            start = side * (rank // 2) + lax.rem(x + k, 4) * width
            rows = pl.ds(pl.multiple_of(start, width), width)
            left, right = codes[rows, :], message[rows, :]
            for c in range(0, outs, 256):
                acc = dot(left, own[:, c : c + 256])
                acc = acc + dot(right, message[rank + c : rank + c + 256])
                out[side, :, c : c + 256] = acc.astype(out.dtype)


def term_sum_kernel(keep, r1, r2, r3, own, away):
    y_lo = lax.axis_index("y_lo")
    for out, side in ((own, y_lo), (away, 1 - y_lo)):
        value = keep[side]
        for r in (r1, r2, r3):
            value = value + r[side].astype(F32)
        value = value.T
        rows = out.shape[0]
        for i in range(value.shape[0] // rows):
            piece = value[i * rows : (i + 1) * rows].astype(out.dtype)
            out[:, i * value.shape[1] : (i + 1) * value.shape[1]] = piece


def local(acts, target, proj_b, proj_a):
    core = lax.axis_index("core")
    tokens, rank = acts.shape[0], proj_b.shape[0]
    outs, wide = target.shape[1], acts.shape[1]
    half, sub, width = tokens // 2, tokens // 16, rank // 8
    scale = -2.0 / (tokens * 8)

    def part_of(array, which, size, axis):
        return lax.dynamic_slice_in_dim(array, which * size, size, axis)

    barrier = lax.optimization_barrier
    plus, minus = shift(acts, "x", 4, 1), shift(acts, "x", 4, 3)
    pair_a = swap(proj_a, "core")
    target_t = target.T
    near_t = part_of(target_t, core, half, 1)
    pair_t = swap(part_of(target_t, 1 - core, half, 1), "core")

    arrived = swap(codes_call(True, acts, proj_b), "core")
    mine = (codes_call(False, acts, proj_b) + arrived).astype(BF).reshape(8, width, half)
    blocks = lax.all_to_all(mine, ZY, 0, 0)
    blocks, plus, minus, later, pair_a, pair_t = barrier((blocks, plus, minus, acts, pair_a, pair_t))
    far = shift(later, "x", 4, 2)
    codes = call(sum_and_copy, [like((8, width, half))], blocks)
    codes = lax.all_to_all(codes, ZY, 0, 0).reshape(rank, half)

    own, message, partial = call(
        residual_kernel,
        [like((half, outs)), like((rank + outs, half)), like((8, sub, rank))],
        codes, near_t, pair_t, proj_a, pair_a,
        scratch=[pltpu.VMEM((half, 2 * outs), BF)],
        flops=8 * half * rank * outs,
    )
    blocks = lax.all_to_all(partial, ZY, 0, 0)

    piece = like((2, width, outs))
    terms = call(
        term_kernel,
        [like(piece.shape, F32), piece, piece, piece],
        codes, own, swap(message, "core"),
        flops=2 * tokens * rank * outs,
    )
    terms = [terms[0]] + [shift(terms[k], "x", 4, k) for k in (1, 2, 3)]

    blocks, far = barrier((blocks, far))
    row = [acts, plus, far, minus]
    spread = like((4, 8, sub, width))
    split_a, split_o = call(spread_kernel, [spread, spread], blocks, scratch=[pltpu.VMEM((sub, rank), BF)])

    def gather(split):
        split = lax.all_to_all(split.reshape(32, sub, width), ("x", "z", "y_hi"), 0, 0)
        return split.reshape(4, half, width)

    grad = gather(split_a)
    term_o, term_a = call(term_sum_kernel, [like((outs, width), F32), like((width, outs))], *terms)
    grad, split_o, term_o, term_a = barrier((grad, split_o, term_o, term_a))
    away = last_call(grad, swap(grad, "core"), row, BF, term_a)
    away, split_o = barrier((away, split_o))
    away = swap(away, "y_lo").astype(F32)
    grad = gather(split_o)
    here = last_call(grad, swap(grad, "core"), row, F32)
    here, term_o = barrier((here, term_o))
    term_a = away[:, wide:].reshape(width, outs // width, width).transpose(1, 0, 2).reshape(outs, width)
    return ((term_o + term_a) * scale, (here + away[:, :wide]) * scale)


def solution(mesh):
    fine = Mesh(np.reshape(mesh.devices, (2, 4, 4, 2, 2)), ("y_lo", "x", "z", "y_hi", "core"))
    return jax.shard_map(
        local,
        mesh=fine,
        in_specs=(P(TOK, CHAN), P(TOK, CHAN), P(None, CHAN), P(CHAN, None)),
        out_specs=(P(CHAN, TOK), P(TOK, CHAN)),
        check_vma=False,
    )
```

```python
import functools

import jax
import jax.numpy as jnp
import numpy as np
from jax import lax
from jax.experimental import pallas as pl
from jax.experimental.pallas import tpu as pltpu
from jax.sharding import Mesh, PartitionSpec as P

BF, F32 = jnp.bfloat16, jnp.float32
TOK, CHAN, ZY = ("y_lo", "x"), ("z", "y_hi", "core"), ("z", "y_hi")
VMEM = pl.BlockSpec(memory_space=pltpu.VMEM)
ANY = pl.BlockSpec(memory_space=pl.ANY)


def dot(left, right, left_dim=1, right_dim=0):
    return lax.dot_general(
        left, right, (((left_dim,), (right_dim,)), ((), ())), preferred_element_type=F32
    )


def shift(array, axis, size, step):
    return lax.ppermute(array, axis, [(i, (i + step) % size) for i in range(size)])


def swap(array, axis):
    return shift(array, axis, 2, 1)


def call(body, outs, *args, scratch=(), flops=0):
    moved = sum(a.size * a.dtype.itemsize for a in list(args) + list(outs))
    return pl.pallas_call(
        body,
        out_shape=outs if len(outs) > 1 else outs[0],
        in_specs=[VMEM] * len(args),
        out_specs=[VMEM] * len(outs) if len(outs) > 1 else VMEM,
        scratch_shapes=scratch,
        compiler_params=pltpu.CompilerParams(vmem_limit_bytes=16 * 1024 * 1024),
        cost_estimate=pl.CostEstimate(flops=flops, bytes_accessed=moved, transcendentals=0),
    )(*args)


def like(shape, dtype=BF):
    return jax.ShapeDtypeStruct(shape, dtype)


def total(ref, at=slice(None)):
    out = ref[0, at].astype(F32)
    for i in range(1, ref.shape[0]):
        out = out + ref[i, at].astype(F32)
    return out


def codes_kernel(other, acts, b, out, turned):
    core, half = lax.axis_index("core"), turned.shape[1]

    @pl.when(pl.program_id(0) == 0)
    def _():
        which = 1 - core if other else core
        turned[...] = acts[pl.ds(pl.multiple_of(which * half, half), half), :].T

    out[...] = dot(b[...], turned[...])


def codes_call(other, acts, proj_b):
    (tokens, wide), rank = acts.shape, proj_b.shape[0]
    half, step = tokens // 2, 512
    return pl.pallas_call(
        functools.partial(codes_kernel, other),
        grid=(rank // step,),
        out_shape=like((rank, half), F32),
        in_specs=[
            pl.BlockSpec((tokens, wide), lambda i: (0, 0)),
            pl.BlockSpec((step, wide), lambda i: (i, 0)),
        ],
        out_specs=pl.BlockSpec((step, half), lambda i: (i, 0)),
        scratch_shapes=[pltpu.VMEM((wide, half), BF)],
        compiler_params=pltpu.CompilerParams(vmem_limit_bytes=32 * 1024 * 1024),
        cost_estimate=pl.CostEstimate(
            flops=2 * rank * wide * half, bytes_accessed=2 * rank * wide, transcendentals=0
        ),
    )(acts, proj_b)


def sum_and_copy(blocks, out):
    value = total(blocks).astype(BF)
    for i in range(out.shape[0]):
        out[i] = value


def residual_kernel(codes, near, far, a0, a1, own, message, partial, held):
    rank, outs = codes.shape[0], a0.shape[0]
    step = 256
    for j, (target, a) in enumerate(((near, a0), (far, a1))):
        for at in range(0, outs, step):
            rows = slice(at, at + step)
            left = target[rows].astype(F32) - dot(a[rows], codes[...])
            left = left.astype(BF).T
            held[:, j * outs + at : j * outs + at + step] = left
            (own if j == 0 else message)[:, rows] = left
    sub = partial.shape[1]
    for at in range(0, rank, 512):
        cols = slice(at, at + 512)
        term = dot(held[:, :outs], a0[:, cols]) + dot(held[:, outs:], a1[:, cols])
        for i in range(partial.shape[0]):
            partial[i, :, cols] = term[i * sub : (i + 1) * sub].astype(BF)


def spread_kernel(blocks, out, held):
    y_lo = lax.axis_index("y_lo")
    held[...] = total(blocks).astype(BF)
    rank = held.shape[1]
    width = rank // 8
    for at, side in ((0, 1 - y_lo), (width, y_lo)):
        for x in range(4):
            start = pl.multiple_of(side * (rank // 2) + x * width, width)
            piece = held[:, pl.ds(start, width)]
            for i in range(out.shape[1]):
                out[x, i, :, at : at + width] = piece


def last_kernel(side, grad_m, grad_o, acts, *refs):
    joined, (out, turned, held, sems) = refs[:-4], refs[-4:]
    core = lax.axis_index("core")
    half, wide, width = grad_m.shape[1], acts.shape[2], out.shape[0]
    step, flight = held.shape[3], 4
    copies = [
        pltpu.make_async_copy(acts.at[:, :, pl.ds(i * step, step)], held.at[i], sems.at[i])
        for i in range(wide // step)
    ]
    for copy in copies[:flight]:
        copy.start()
    at = slice(side * width, (side + 1) * width)
    for k in range(4):
        turned[k, :, pl.ds(pl.multiple_of(core * half, half), half)] = grad_m[k, :, at].T
        turned[k, :, pl.ds(pl.multiple_of((1 - core) * half, half), half)] = grad_o[k, :, at].T
    for ref in joined:
        out[:, wide:] = ref[...]
    for i, copy in enumerate(copies):
        copy.wait()
        if i + flight < len(copies):
            copies[i + flight].start()
        acc = dot(turned[0], held[i, 0])
        for k in range(1, 4):
            acc = acc + dot(turned[k], held[i, k])
        out[:, i * step : (i + 1) * step] = acc.astype(out.dtype)


def last_call(grad_m, grad_o, row, side, dtype, *joined):
    _, tokens, wide = row.shape
    width, step = grad_m.shape[2] // 2, 256
    return pl.pallas_call(
        functools.partial(last_kernel, side),
        out_shape=like((width, wide + sum(j.shape[1] for j in joined)), dtype),
        in_specs=[VMEM, VMEM, ANY] + [VMEM] * len(joined),
        out_specs=VMEM,
        scratch_shapes=[
            pltpu.VMEM((4, width, tokens), BF),
            pltpu.VMEM((wide // step, 4, tokens, step), BF),
            pltpu.SemaphoreType.DMA((wide // step,)),
        ],
        compiler_params=pltpu.CompilerParams(vmem_limit_bytes=48 * 1024 * 1024),
        cost_estimate=pl.CostEstimate(
            flops=8 * tokens * width * wide, bytes_accessed=8 * tokens * wide, transcendentals=0
        ),
    )(grad_m, grad_o, row, *joined)


def term_kernel(codes, own, codes_o, message, keep, s1, s2, s3):
    x = lax.axis_index("x")
    rank, outs = codes.shape[0], own.shape[1]
    width = rank // 8
    for k, out in enumerate((keep, s1, s2, s3)):
        for side in range(2):
            start = side * (rank // 2) + lax.rem(x + k, 4) * width
            rows = pl.ds(pl.multiple_of(start, width), width)
            left, right = codes[rows, :], codes_o[rows, :]
            for c in range(0, outs, 256):
                acc = dot(left, own[:, c : c + 256])
                acc = acc + dot(right, message[:, c : c + 256])
                out[side, :, c : c + 256] = acc.astype(out.dtype)


def term_sum_kernel(keep, r1, r2, r3, own, away):
    y_lo = lax.axis_index("y_lo")
    for out, side in ((own, y_lo), (away, 1 - y_lo)):
        value = keep[side]
        for r in (r1, r2, r3):
            value = value + r[side].astype(F32)
        out[...] = value.astype(out.dtype)


def local(acts, target, proj_b, proj_a):
    core = lax.axis_index("core")
    tokens, rank = acts.shape[0], proj_b.shape[0]
    outs, wide = target.shape[1], acts.shape[1]
    half, sub, width = tokens // 2, tokens // 16, rank // 8
    scale = -2.0 / (tokens * 8)

    def part_of(array, which, size, axis):
        return lax.dynamic_slice_in_dim(array, which * size, size, axis)

    row = lax.all_gather(acts, "x")
    pair_a = swap(proj_a, "core")
    target_t = target.T
    near_t = part_of(target_t, core, half, 1)
    pair_t = swap(part_of(target_t, 1 - core, half, 1), "core")

    arrived = swap(codes_call(True, acts, proj_b), "core")
    mine = (codes_call(False, acts, proj_b) + arrived).astype(BF).reshape(8, width, half)
    blocks = lax.all_to_all(mine, ZY, 0, 0)
    codes = call(sum_and_copy, [like((8, width, half))], blocks)
    codes = lax.all_to_all(codes, ZY, 0, 0).reshape(rank, half)

    codes_o = swap(codes, "core")

    own, message, partial = call(
        residual_kernel,
        [like((half, outs)), like((half, outs)), like((8, sub, rank))],
        codes, near_t, pair_t, proj_a, pair_a,
        scratch=[pltpu.VMEM((half, 2 * outs), BF)],
        flops=8 * half * rank * outs,
    )
    blocks = lax.all_to_all(partial, ZY, 0, 0)

    piece = like((2, width, outs))
    terms = call(
        term_kernel,
        [like(piece.shape, F32), piece, piece, piece],
        codes, own, codes_o, swap(message, "core"),
        flops=2 * tokens * rank * outs,
    )
    terms = [terms[0]] + [shift(terms[k], "x", 4, k) for k in (1, 2, 3)]

    barrier = lax.optimization_barrier
    blocks, row = barrier((blocks, row))
    split = call(spread_kernel, [like((4, 8, sub, 2 * width))], blocks, scratch=[pltpu.VMEM((sub, rank), BF)])
    grad = lax.all_to_all(split.reshape(32, sub, 2 * width), ("x", "z", "y_hi"), 0, 0)
    grad = grad.reshape(4, half, 2 * width)
    grad_o = swap(grad, "core")
    away = last_call(grad, grad_o, row, 0, BF)
    away = swap(away, "y_lo").astype(F32)
    later, *terms = barrier((grad, *terms))
    here = last_call(later, grad_o, row, 1, F32)
    term_o, term_a = call(term_sum_kernel, [like((width, outs), F32), like((width, outs))], *terms)
    term_a = swap(term_a, "y_lo").astype(F32)
    here, term_o = barrier((here, term_o))
    return (((term_o + term_a) * scale).T, (here + away) * scale)


def solution(mesh):
    fine = Mesh(np.reshape(mesh.devices, (2, 4, 4, 2, 2)), ("y_lo", "x", "z", "y_hi", "core"))
    return jax.shard_map(
        local,
        mesh=fine,
        in_specs=(P(TOK, CHAN), P(TOK, CHAN), P(None, CHAN), P(CHAN, None)),
        out_specs=(P(CHAN, TOK), P(TOK, CHAN)),
        check_vma=False,
    )
```

```python
import functools

import jax
import jax.numpy as jnp
import numpy as np
from jax import lax
from jax.experimental import pallas as pl
from jax.experimental.pallas import tpu as pltpu
from jax.sharding import Mesh, PartitionSpec as P

BF, F32 = jnp.bfloat16, jnp.float32
TOK, CHAN, ZY = ("y_lo", "x"), ("z", "y_hi", "core"), ("z", "y_hi")
VMEM = pl.BlockSpec(memory_space=pltpu.VMEM)
ANY = pl.BlockSpec(memory_space=pl.ANY)


def dot(left, right, left_dim=1, right_dim=0):
    return lax.dot_general(
        left, right, (((left_dim,), (right_dim,)), ((), ())), preferred_element_type=F32
    )


def shift(array, axis, size, step):
    return lax.ppermute(array, axis, [(i, (i + step) % size) for i in range(size)])


def swap(array, axis):
    return shift(array, axis, 2, 1)


def call(body, outs, *args, scratch=(), flops=0):
    moved = sum(a.size * a.dtype.itemsize for a in list(args) + list(outs))
    return pl.pallas_call(
        body,
        out_shape=outs if len(outs) > 1 else outs[0],
        in_specs=[VMEM] * len(args),
        out_specs=[VMEM] * len(outs) if len(outs) > 1 else VMEM,
        scratch_shapes=scratch,
        compiler_params=pltpu.CompilerParams(vmem_limit_bytes=16 * 1024 * 1024),
        cost_estimate=pl.CostEstimate(flops=flops, bytes_accessed=moved, transcendentals=0),
    )(*args)


def like(shape, dtype=BF):
    return jax.ShapeDtypeStruct(shape, dtype)


def total(ref, at=slice(None)):
    out = ref[0, at].astype(F32)
    for i in range(1, ref.shape[0]):
        out = out + ref[i, at].astype(F32)
    return out


def codes_kernel(other, acts, b, out, turned):
    core, half = lax.axis_index("core"), turned.shape[1]

    @pl.when(pl.program_id(0) == 0)
    def _():
        which = 1 - core if other else core
        turned[...] = acts[pl.ds(pl.multiple_of(which * half, half), half), :].T

    out[...] = dot(b[...], turned[...])


def codes_call(other, acts, proj_b):
    (tokens, wide), rank = acts.shape, proj_b.shape[0]
    half, step = tokens // 2, 512
    return pl.pallas_call(
        functools.partial(codes_kernel, other),
        grid=(rank // step,),
        out_shape=like((rank, half), F32),
        in_specs=[
            pl.BlockSpec((tokens, wide), lambda i: (0, 0)),
            pl.BlockSpec((step, wide), lambda i: (i, 0)),
        ],
        out_specs=pl.BlockSpec((step, half), lambda i: (i, 0)),
        scratch_shapes=[pltpu.VMEM((wide, half), BF)],
        compiler_params=pltpu.CompilerParams(vmem_limit_bytes=32 * 1024 * 1024),
        cost_estimate=pl.CostEstimate(
            flops=2 * rank * wide * half, bytes_accessed=2 * rank * wide, transcendentals=0
        ),
    )(acts, proj_b)


def sum_and_copy(blocks, out):
    value = total(blocks).astype(BF)
    for i in range(out.shape[0]):
        out[i] = value


def residual_kernel(codes, near, far, a0, a1, own, message, partial, held):
    rank, outs = codes.shape[0], a0.shape[0]
    step = 256
    for j, (target, a) in enumerate(((near, a0), (far, a1))):
        for at in range(0, outs, step):
            rows = slice(at, at + step)
            left = target[rows].astype(F32) - dot(a[rows], codes[...])
            left = left.astype(BF).T
            held[:, j * outs + at : j * outs + at + step] = left
            (own if j == 0 else message)[:, rows] = left
    sub = partial.shape[1]
    for at in range(0, rank, 512):
        cols = slice(at, at + 512)
        term = dot(held[:, :outs], a0[:, cols]) + dot(held[:, outs:], a1[:, cols])
        for i in range(partial.shape[0]):
            partial[i, :, cols] = term[i * sub : (i + 1) * sub].astype(BF)


def spread_kernel(blocks, out, held):
    y_lo = lax.axis_index("y_lo")
    held[...] = total(blocks).astype(BF)
    rank = held.shape[1]
    width = rank // 8
    for at, side in ((0, 1 - y_lo), (width, y_lo)):
        for x in range(4):
            start = pl.multiple_of(side * (rank // 2) + x * width, width)
            piece = held[:, pl.ds(start, width)]
            for i in range(out.shape[1]):
                out[x, i, :, at : at + width] = piece


def last_kernel(side, grad_m, grad_o, acts, *refs):
    joined, (out, turned, held, sems) = refs[:-4], refs[-4:]
    core = lax.axis_index("core")
    half, wide, width = grad_m.shape[1], acts.shape[2], out.shape[0]
    step, flight = held.shape[3], 4
    copies = [
        pltpu.make_async_copy(acts.at[:, :, pl.ds(i * step, step)], held.at[i], sems.at[i])
        for i in range(wide // step)
    ]
    for copy in copies[:flight]:
        copy.start()
    at = slice(side * width, (side + 1) * width)
    for k in range(4):
        turned[k, :, pl.ds(pl.multiple_of(core * half, half), half)] = grad_m[k, :, at].T
        turned[k, :, pl.ds(pl.multiple_of((1 - core) * half, half), half)] = grad_o[k, :, at].T
    for ref in joined:
        out[:, wide:] = ref[...]
    for i, copy in enumerate(copies):
        copy.wait()
        if i + flight < len(copies):
            copies[i + flight].start()
        acc = dot(turned[0], held[i, 0])
        for k in range(1, 4):
            acc = acc + dot(turned[k], held[i, k])
        out[:, i * step : (i + 1) * step] = acc.astype(out.dtype)


def last_call(grad_m, grad_o, row, side, dtype, *joined):
    _, tokens, wide = row.shape
    width, step = grad_m.shape[2] // 2, 256
    return pl.pallas_call(
        functools.partial(last_kernel, side),
        out_shape=like((width, wide + sum(j.shape[1] for j in joined)), dtype),
        in_specs=[VMEM, VMEM, ANY] + [VMEM] * len(joined),
        out_specs=VMEM,
        scratch_shapes=[
            pltpu.VMEM((4, width, tokens), BF),
            pltpu.VMEM((wide // step, 4, tokens, step), BF),
            pltpu.SemaphoreType.DMA((wide // step,)),
        ],
        compiler_params=pltpu.CompilerParams(vmem_limit_bytes=48 * 1024 * 1024),
        cost_estimate=pl.CostEstimate(
            flops=8 * tokens * width * wide, bytes_accessed=8 * tokens * wide, transcendentals=0
        ),
    )(grad_m, grad_o, row, *joined)


def term_kernel(codes, own, codes_o, message, keep, s1, s2, s3):
    x = lax.axis_index("x")
    rank, outs = codes.shape[0], own.shape[1]
    width = rank // 8
    for k, out in enumerate((keep, s1, s2, s3)):
        for side in range(2):
            start = side * (rank // 2) + lax.rem(x + k, 4) * width
            rows = pl.ds(pl.multiple_of(start, width), width)
            left, right = codes[rows, :], codes_o[rows, :]
            for c in range(0, outs, 256):
                acc = dot(left, own[:, c : c + 256])
                acc = acc + dot(right, message[:, c : c + 256])
                out[side, :, c : c + 256] = acc.astype(out.dtype)


def term_sum_kernel(keep, r1, r2, r3, own, away):
    y_lo = lax.axis_index("y_lo")
    for out, side in ((own, y_lo), (away, 1 - y_lo)):
        value = keep[side]
        for r in (r1, r2, r3):
            value = value + r[side].astype(F32)
        out[...] = value.astype(out.dtype)


def local(acts, target, proj_b, proj_a):
    core = lax.axis_index("core")
    tokens, rank = acts.shape[0], proj_b.shape[0]
    outs, wide = target.shape[1], acts.shape[1]
    half, sub, width = tokens // 2, tokens // 16, rank // 8
    scale = -2.0 / (tokens * 8)

    def part_of(array, which, size, axis):
        return lax.dynamic_slice_in_dim(array, which * size, size, axis)

    row = lax.all_gather(acts, "x")
    pair_a = swap(proj_a, "core")
    target_t = target.T
    near_t = part_of(target_t, core, half, 1)
    pair_t = swap(part_of(target_t, 1 - core, half, 1), "core")

    arrived = swap(codes_call(True, acts, proj_b), "core")
    mine = (codes_call(False, acts, proj_b) + arrived).astype(BF).reshape(8, width, half)
    blocks = lax.all_to_all(mine, ZY, 0, 0)
    codes = call(sum_and_copy, [like((8, width, half))], blocks)
    codes = lax.all_to_all(codes, ZY, 0, 0).reshape(rank, half)

    codes_o = swap(codes, "core")

    own, message, partial = call(
        residual_kernel,
        [like((half, outs)), like((half, outs)), like((8, sub, rank))],
        codes, near_t, pair_t, proj_a, pair_a,
        scratch=[pltpu.VMEM((half, 2 * outs), BF)],
        flops=8 * half * rank * outs,
    )
    blocks = lax.all_to_all(partial, ZY, 0, 0)

    piece = like((2, width, outs))
    terms = call(
        term_kernel,
        [like(piece.shape, F32), piece, piece, piece],
        codes, own, codes_o, swap(message, "core"),
        flops=2 * tokens * rank * outs,
    )
    near = [shift(terms[k], "x", 4, k) for k in (1, 3)]

    barrier = lax.optimization_barrier
    blocks, row, near, later = barrier((blocks, row, near, terms[2]))
    terms = [terms[0], shift(later, "x", 4, 2)] + near
    split = call(spread_kernel, [like((4, 8, sub, 2 * width))], blocks, scratch=[pltpu.VMEM((sub, rank), BF)])
    grad = lax.all_to_all(split.reshape(32, sub, 2 * width), ("x", "z", "y_hi"), 0, 0)
    grad = grad.reshape(4, half, 2 * width)
    grad_o = swap(grad, "core")
    away = last_call(grad, grad_o, row, 0, BF)
    away = swap(away, "y_lo").astype(F32)
    later, *terms = barrier((grad, *terms))
    here = last_call(later, grad_o, row, 1, F32)
    term_o, term_a = call(term_sum_kernel, [like((width, outs), F32), like((width, outs))], *terms)
    term_a = swap(term_a, "y_lo").astype(F32)
    here, term_o = barrier((here, term_o))
    return (((term_o + term_a) * scale).T, (here + away) * scale)


def solution(mesh):
    fine = Mesh(np.reshape(mesh.devices, (2, 4, 4, 2, 2)), ("y_lo", "x", "z", "y_hi", "core"))
    return jax.shard_map(
        local,
        mesh=fine,
        in_specs=(P(TOK, CHAN), P(TOK, CHAN), P(None, CHAN), P(CHAN, None)),
        out_specs=(P(CHAN, TOK), P(TOK, CHAN)),
        check_vma=False,
    )
```

```python
import functools

import jax
import jax.numpy as jnp
import numpy as np
from jax import lax
from jax.experimental import pallas as pl
from jax.experimental.pallas import tpu as pltpu
from jax.sharding import Mesh, PartitionSpec as P

BF, F32 = jnp.bfloat16, jnp.float32
TOK, CHAN, ZY = ("y_lo", "x"), ("z", "y_hi", "core"), ("z", "y_hi")
VMEM = pl.BlockSpec(memory_space=pltpu.VMEM)
ANY = pl.BlockSpec(memory_space=pl.ANY)


def dot(left, right, left_dim=1, right_dim=0):
    return lax.dot_general(
        left, right, (((left_dim,), (right_dim,)), ((), ())), preferred_element_type=F32
    )


def shift(array, axis, size, step):
    return lax.ppermute(array, axis, [(i, (i + step) % size) for i in range(size)])


def swap(array, axis):
    return shift(array, axis, 2, 1)


def call(body, outs, *args, scratch=(), flops=0):
    moved = sum(a.size * a.dtype.itemsize for a in list(args) + list(outs))
    return pl.pallas_call(
        body,
        out_shape=outs if len(outs) > 1 else outs[0],
        in_specs=[VMEM] * len(args),
        out_specs=[VMEM] * len(outs) if len(outs) > 1 else VMEM,
        scratch_shapes=scratch,
        compiler_params=pltpu.CompilerParams(vmem_limit_bytes=16 * 1024 * 1024),
        cost_estimate=pl.CostEstimate(flops=flops, bytes_accessed=moved, transcendentals=0),
    )(*args)


def like(shape, dtype=BF):
    return jax.ShapeDtypeStruct(shape, dtype)


def total(ref, at=slice(None)):
    out = ref[0, at].astype(F32)
    for i in range(1, ref.shape[0]):
        out = out + ref[i, at].astype(F32)
    return out


def codes_kernel(other, acts, b, out, turned):
    core, half = lax.axis_index("core"), turned.shape[1]

    @pl.when(pl.program_id(0) == 0)
    def _():
        which = 1 - core if other else core
        turned[...] = acts[pl.ds(pl.multiple_of(which * half, half), half), :].T

    out[...] = dot(b[...], turned[...])


def codes_call(other, acts, proj_b):
    (tokens, wide), rank = acts.shape, proj_b.shape[0]
    half, step = tokens // 2, 512
    return pl.pallas_call(
        functools.partial(codes_kernel, other),
        grid=(rank // step,),
        out_shape=like((rank, half), F32),
        in_specs=[
            pl.BlockSpec((tokens, wide), lambda i: (0, 0)),
            pl.BlockSpec((step, wide), lambda i: (i, 0)),
        ],
        out_specs=pl.BlockSpec((step, half), lambda i: (i, 0)),
        scratch_shapes=[pltpu.VMEM((wide, half), BF)],
        compiler_params=pltpu.CompilerParams(vmem_limit_bytes=32 * 1024 * 1024),
        cost_estimate=pl.CostEstimate(
            flops=2 * rank * wide * half, bytes_accessed=2 * rank * wide, transcendentals=0
        ),
    )(acts, proj_b)


def sum_and_copy(blocks, out):
    value = total(blocks).astype(BF)
    for i in range(out.shape[0]):
        out[i] = value


def residual_kernel(codes, near, far, a0, a1, own, message, partial, held):
    rank, outs = codes.shape[0], a0.shape[0]
    step = 256
    for j, (target, a) in enumerate(((near, a0), (far, a1))):
        for at in range(0, outs, step):
            rows = slice(at, at + step)
            left = target[rows].astype(F32) - dot(a[rows], codes[...])
            left = left.astype(BF).T
            held[:, j * outs + at : j * outs + at + step] = left
            (own if j == 0 else message)[:, rows] = left
    sub = partial.shape[1]
    for at in range(0, rank, 512):
        cols = slice(at, at + 512)
        term = dot(held[:, :outs], a0[:, cols]) + dot(held[:, outs:], a1[:, cols])
        for i in range(partial.shape[0]):
            partial[i, :, cols] = term[i * sub : (i + 1) * sub].astype(BF)


def spread_kernel(blocks, out, held):
    y_lo = lax.axis_index("y_lo")
    held[...] = total(blocks).astype(BF)
    rank = held.shape[1]
    width = rank // 8
    for at, side in ((0, 1 - y_lo), (width, y_lo)):
        for x in range(4):
            start = pl.multiple_of(side * (rank // 2) + x * width, width)
            piece = held[:, pl.ds(start, width)]
            for i in range(out.shape[1]):
                out[x, i, :, at : at + width] = piece


def last_kernel(side, grad_m, grad_o, acts, *refs):
    joined, (out, turned, held, sems) = refs[:-4], refs[-4:]
    core = lax.axis_index("core")
    half, wide, width = grad_m.shape[1], acts.shape[2], out.shape[0]
    step, flight = held.shape[3], 4
    copies = [
        pltpu.make_async_copy(acts.at[:, :, pl.ds(i * step, step)], held.at[i], sems.at[i])
        for i in range(wide // step)
    ]
    for copy in copies[:flight]:
        copy.start()
    at = slice(side * width, (side + 1) * width)
    for k in range(4):
        turned[k, :, pl.ds(pl.multiple_of(core * half, half), half)] = grad_m[k, :, at].T
        turned[k, :, pl.ds(pl.multiple_of((1 - core) * half, half), half)] = grad_o[k, :, at].T
    for ref in joined:
        out[:, wide:] = ref[...]
    for i, copy in enumerate(copies):
        copy.wait()
        if i + flight < len(copies):
            copies[i + flight].start()
        acc = dot(turned[0], held[i, 0])
        for k in range(1, 4):
            acc = acc + dot(turned[k], held[i, k])
        out[:, i * step : (i + 1) * step] = acc.astype(out.dtype)


def last_call(grad_m, grad_o, row, side, dtype, *joined):
    _, tokens, wide = row.shape
    width, step = grad_m.shape[2] // 2, 256
    return pl.pallas_call(
        functools.partial(last_kernel, side),
        out_shape=like((width, wide + sum(j.shape[1] for j in joined)), dtype),
        in_specs=[VMEM, VMEM, ANY] + [VMEM] * len(joined),
        out_specs=VMEM,
        scratch_shapes=[
            pltpu.VMEM((4, width, tokens), BF),
            pltpu.VMEM((wide // step, 4, tokens, step), BF),
            pltpu.SemaphoreType.DMA((wide // step,)),
        ],
        compiler_params=pltpu.CompilerParams(vmem_limit_bytes=48 * 1024 * 1024),
        cost_estimate=pl.CostEstimate(
            flops=8 * tokens * width * wide, bytes_accessed=8 * tokens * wide, transcendentals=0
        ),
    )(grad_m, grad_o, row, *joined)


def term_kernel(codes, own, codes_o, message, keep, s1, s2, s3):
    x = lax.axis_index("x")
    rank, outs = codes.shape[0], own.shape[1]
    width = rank // 8
    for k, out in enumerate((keep, s1, s2, s3)):
        for side in range(2):
            start = side * (rank // 2) + lax.rem(x + k, 4) * width
            rows = pl.ds(pl.multiple_of(start, width), width)
            left, right = codes[rows, :], codes_o[rows, :]
            for c in range(0, outs, 256):
                acc = dot(left, own[:, c : c + 256])
                acc = acc + dot(right, message[:, c : c + 256])
                out[side, :, c : c + 256] = acc.astype(out.dtype)


def term_sum_kernel(keep, r1, r2, r3, own, away):
    y_lo = lax.axis_index("y_lo")
    for out, side in ((own, y_lo), (away, 1 - y_lo)):
        value = keep[side]
        for r in (r1, r2, r3):
            value = value + r[side].astype(F32)
        out[...] = value.astype(out.dtype)


def local(acts, target, proj_b, proj_a):
    core = lax.axis_index("core")
    tokens, rank = acts.shape[0], proj_b.shape[0]
    outs, wide = target.shape[1], acts.shape[1]
    half, sub, width = tokens // 2, tokens // 16, rank // 8
    scale = -2.0 / (tokens * 8)

    def part_of(array, which, size, axis):
        return lax.dynamic_slice_in_dim(array, which * size, size, axis)

    row = lax.all_gather(acts, "x")
    pair_a = swap(proj_a, "core")
    target_t = target.T
    near_t = part_of(target_t, core, half, 1)
    pair_t = swap(part_of(target_t, 1 - core, half, 1), "core")

    arrived = swap(codes_call(True, acts, proj_b), "core")
    mine = (codes_call(False, acts, proj_b) + arrived).astype(BF).reshape(8, width, half)
    blocks = lax.all_to_all(mine, ZY, 0, 0)
    codes = call(sum_and_copy, [like((8, width, half))], blocks)
    codes = lax.all_to_all(codes, ZY, 0, 0).reshape(rank, half)

    codes_o = swap(codes, "core")

    own, message, partial = call(
        residual_kernel,
        [like((half, outs)), like((half, outs)), like((8, sub, rank))],
        codes, near_t, pair_t, proj_a, pair_a,
        scratch=[pltpu.VMEM((half, 2 * outs), BF)],
        flops=8 * half * rank * outs,
    )
    blocks = lax.all_to_all(partial, ZY, 0, 0)

    piece = like((2, width, outs))
    terms = call(
        term_kernel,
        [like(piece.shape, F32), piece, piece, piece],
        codes, own, codes_o, swap(message, "core"),
        flops=2 * tokens * rank * outs,
    )
    terms = [terms[0]] + [shift(terms[k], "x", 4, k) for k in (1, 2, 3)]

    barrier = lax.optimization_barrier
    blocks, row, terms[0] = barrier((blocks, row, terms[0]))
    split = call(spread_kernel, [like((4, 8, sub, 2 * width))], blocks, scratch=[pltpu.VMEM((sub, rank), BF)])
    grad = lax.all_to_all(split.reshape(32, sub, 2 * width), ("x", "z", "y_hi"), 0, 0)
    grad = grad.reshape(4, half, 2 * width)
    grad_o = swap(grad, "core")
    away = last_call(grad, grad_o, row, 0, BF)
    away = swap(away, "y_lo").astype(F32)
    later, *terms = barrier((grad, *terms))
    here = last_call(later, grad_o, row, 1, F32)
    term_o, term_a = call(term_sum_kernel, [like((width, outs), F32), like((width, outs))], *terms)
    term_a = swap(term_a, "y_lo").astype(F32)
    here, term_o = barrier((here, term_o))
    return (((term_o + term_a) * scale).T, (here + away) * scale)


def solution(mesh):
    fine = Mesh(np.reshape(mesh.devices, (2, 4, 4, 2, 2)), ("y_lo", "x", "z", "y_hi", "core"))
    return jax.shard_map(
        local,
        mesh=fine,
        in_specs=(P(TOK, CHAN), P(TOK, CHAN), P(None, CHAN), P(CHAN, None)),
        out_specs=(P(CHAN, TOK), P(TOK, CHAN)),
        check_vma=False,
    )
```

```python
import functools

import jax
import jax.numpy as jnp
import numpy as np
from jax import lax
from jax.experimental import pallas as pl
from jax.experimental.pallas import tpu as pltpu
from jax.sharding import Mesh, PartitionSpec as P

BF, F32 = jnp.bfloat16, jnp.float32
TOK, CHAN, ZY = ("y_lo", "x"), ("z", "y_hi", "core"), ("z", "y_hi")
VMEM = pl.BlockSpec(memory_space=pltpu.VMEM)
ANY = pl.BlockSpec(memory_space=pl.ANY)


def dot(left, right, left_dim=1, right_dim=0):
    return lax.dot_general(
        left, right, (((left_dim,), (right_dim,)), ((), ())), preferred_element_type=F32
    )


def shift(array, axis, size, step):
    return lax.ppermute(array, axis, [(i, (i + step) % size) for i in range(size)])


def swap(array, axis):
    return shift(array, axis, 2, 1)


def call(body, outs, *args, scratch=(), flops=0):
    moved = sum(a.size * a.dtype.itemsize for a in list(args) + list(outs))
    return pl.pallas_call(
        body,
        out_shape=outs if len(outs) > 1 else outs[0],
        in_specs=[VMEM] * len(args),
        out_specs=[VMEM] * len(outs) if len(outs) > 1 else VMEM,
        scratch_shapes=scratch,
        compiler_params=pltpu.CompilerParams(vmem_limit_bytes=16 * 1024 * 1024),
        cost_estimate=pl.CostEstimate(flops=flops, bytes_accessed=moved, transcendentals=0),
    )(*args)


def like(shape, dtype=BF):
    return jax.ShapeDtypeStruct(shape, dtype)


def total(ref, at=slice(None)):
    out = ref[0, at].astype(F32)
    for i in range(1, ref.shape[0]):
        out = out + ref[i, at].astype(F32)
    return out


def codes_kernel(other, acts, b, out, turned):
    core, half = lax.axis_index("core"), turned.shape[1]

    @pl.when(pl.program_id(0) == 0)
    def _():
        which = 1 - core if other else core
        turned[...] = acts[pl.ds(pl.multiple_of(which * half, half), half), :].T

    out[...] = dot(b[...], turned[...])


def codes_call(other, acts, proj_b):
    (tokens, wide), rank = acts.shape, proj_b.shape[0]
    half, step = tokens // 2, 512
    return pl.pallas_call(
        functools.partial(codes_kernel, other),
        grid=(rank // step,),
        out_shape=like((rank, half), F32),
        in_specs=[
            pl.BlockSpec((tokens, wide), lambda i: (0, 0)),
            pl.BlockSpec((step, wide), lambda i: (i, 0)),
        ],
        out_specs=pl.BlockSpec((step, half), lambda i: (i, 0)),
        scratch_shapes=[pltpu.VMEM((wide, half), BF)],
        compiler_params=pltpu.CompilerParams(vmem_limit_bytes=32 * 1024 * 1024),
        cost_estimate=pl.CostEstimate(
            flops=2 * rank * wide * half, bytes_accessed=2 * rank * wide, transcendentals=0
        ),
    )(acts, proj_b)


def sum_and_copy(blocks, out):
    value = total(blocks).astype(BF)
    for i in range(out.shape[0]):
        out[i] = value


def residual_kernel(codes, near, far, a0, a1, own, message, partial, held):
    rank, outs = codes.shape[0], a0.shape[0]
    step = 256
    for j, (target, a) in enumerate(((near, a0), (far, a1))):
        for at in range(0, outs, step):
            rows = slice(at, at + step)
            left = target[rows].astype(F32) - dot(a[rows], codes[...])
            left = left.astype(BF).T
            held[:, j * outs + at : j * outs + at + step] = left
            (own if j == 0 else message)[:, rows] = left
    sub = partial.shape[1]
    for at in range(0, rank, 512):
        cols = slice(at, at + 512)
        term = dot(held[:, :outs], a0[:, cols]) + dot(held[:, outs:], a1[:, cols])
        for i in range(partial.shape[0]):
            partial[i, :, cols] = term[i * sub : (i + 1) * sub].astype(BF)


def spread_kernel(blocks, out, held):
    y_lo = lax.axis_index("y_lo")
    held[...] = total(blocks).astype(BF)
    rank = held.shape[1]
    width = rank // 8
    for at, side in ((0, 1 - y_lo), (width, y_lo)):
        for x in range(4):
            start = pl.multiple_of(side * (rank // 2) + x * width, width)
            piece = held[:, pl.ds(start, width)]
            for i in range(out.shape[1]):
                out[x, i, :, at : at + width] = piece


def last_kernel(side, other, grad, acts, *refs):
    before, (out, turned) = refs[:-2], refs[-2:]
    core = lax.axis_index("core")
    half, wide, width = grad.shape[1], acts.shape[2], out.shape[0]
    rows = pl.ds(pl.multiple_of((1 - core if other else core) * half, half), half)
    for k in range(4):
        turned[k] = grad[k, :, side * width : (side + 1) * width].T
    for ref in before[1:]:
        out[:, wide:] = ref[...]
    for c in range(0, wide, 256):
        cols = slice(c, c + 256)
        acc = dot(turned[0], acts[0, rows, cols])
        for k in range(1, 4):
            acc = acc + dot(turned[k], acts[k, rows, cols])
        if other:
            acc = acc + before[0][:, cols]
        out[:, cols] = acc.astype(out.dtype)


def last_call(grad_m, grad_o, held, side, dtype, *joined):
    _, tokens, wide = held.shape
    half, width = tokens // 2, grad_m.shape[2] // 2
    scratch = [pltpu.VMEM((4, width, half), BF)]
    flops = 4 * tokens * width * wide
    first = call(
        functools.partial(last_kernel, side, False),
        [like((width, wide), F32)],
        grad_m, held, scratch=scratch, flops=flops,
    )
    return call(
        functools.partial(last_kernel, side, True),
        [like((width, wide + sum(j.shape[1] for j in joined)), dtype)],
        grad_o, held, first, *joined, scratch=scratch, flops=flops,
    )


def term_kernel(codes, own, codes_o, message, keep, s1, s2, s3):
    x = lax.axis_index("x")
    rank, outs = codes.shape[0], own.shape[1]
    width = rank // 8
    for k, out in enumerate((keep, s1, s2, s3)):
        for side in range(2):
            start = side * (rank // 2) + lax.rem(x + k, 4) * width
            rows = pl.ds(pl.multiple_of(start, width), width)
            left, right = codes[rows, :], codes_o[rows, :]
            for c in range(0, outs, 256):
                acc = dot(left, own[:, c : c + 256])
                acc = acc + dot(right, message[:, c : c + 256])
                out[side, :, c : c + 256] = acc.astype(out.dtype)


def term_sum_kernel(keep, r1, r2, r3, own, away):
    y_lo = lax.axis_index("y_lo")
    for out, side in ((own, y_lo), (away, 1 - y_lo)):
        value = keep[side]
        for r in (r1, r2, r3):
            value = value + r[side].astype(F32)
        out[...] = value.astype(out.dtype)


def local(acts, target, proj_b, proj_a):
    core = lax.axis_index("core")
    tokens, rank = acts.shape[0], proj_b.shape[0]
    outs, wide = target.shape[1], acts.shape[1]
    half, sub, width = tokens // 2, tokens // 16, rank // 8
    scale = -2.0 / (tokens * 8)

    def part_of(array, which, size, axis):
        return lax.dynamic_slice_in_dim(array, which * size, size, axis)

    row = lax.all_gather(acts, "x")
    pair_a = swap(proj_a, "core")
    target_t = target.T
    near_t = part_of(target_t, core, half, 1)
    pair_t = swap(part_of(target_t, 1 - core, half, 1), "core")

    arrived = swap(codes_call(True, acts, proj_b), "core")
    mine = (codes_call(False, acts, proj_b) + arrived).astype(BF).reshape(8, width, half)
    blocks = lax.all_to_all(mine, ZY, 0, 0)
    codes = call(sum_and_copy, [like((8, width, half))], blocks)
    codes = lax.all_to_all(codes, ZY, 0, 0).reshape(rank, half)

    own, message, partial = call(
        residual_kernel,
        [like((half, outs)), like((half, outs)), like((8, sub, rank))],
        codes, near_t, pair_t, proj_a, pair_a,
        scratch=[pltpu.VMEM((half, 2 * outs), BF)],
        flops=8 * half * rank * outs,
    )
    partial, codes = lax.optimization_barrier((partial, codes))
    codes_o = swap(codes, "core")
    blocks = lax.all_to_all(partial, ZY, 0, 0)

    piece = like((2, width, outs))
    terms = call(
        term_kernel,
        [like(piece.shape, F32), piece, piece, piece],
        codes, own, codes_o, swap(message, "core"),
        flops=2 * tokens * rank * outs,
    )
    terms = [terms[0]] + [shift(terms[k], "x", 4, k) for k in (1, 2, 3)]

    barrier = lax.optimization_barrier
    blocks, row, terms[0] = barrier((blocks, row, terms[0]))
    split = call(spread_kernel, [like((4, 8, sub, 2 * width))], blocks, scratch=[pltpu.VMEM((sub, rank), BF)], flops=15 * 10**9)
    grad = lax.all_to_all(split.reshape(32, sub, 2 * width), ("x", "z", "y_hi"), 0, 0)
    grad = grad.reshape(4, half, 2 * width)
    grad_o = swap(grad, "core")
    away = last_call(grad, grad_o, row, 0, BF)
    away = swap(away, "y_lo").astype(F32)
    here = last_call(grad, grad_o, row, 1, F32)
    term_o, term_a = call(term_sum_kernel, [like((width, outs), F32), like((width, outs))], *terms)
    term_a = swap(term_a, "y_lo").astype(F32)
    here, term_o = barrier((here, term_o))
    return (((term_o + term_a) * scale).T, (here + away) * scale)


def solution(mesh):
    fine = Mesh(np.reshape(mesh.devices, (2, 4, 4, 2, 2)), ("y_lo", "x", "z", "y_hi", "core"))
    return jax.shard_map(
        local,
        mesh=fine,
        in_specs=(P(TOK, CHAN), P(TOK, CHAN), P(None, CHAN), P(CHAN, None)),
        out_specs=(P(CHAN, TOK), P(TOK, CHAN)),
        check_vma=False,
    )
```

```python
import functools

import jax
import jax.numpy as jnp
import numpy as np
from jax import lax
from jax.experimental import pallas as pl
from jax.experimental.pallas import tpu as pltpu
from jax.sharding import Mesh, PartitionSpec as P

BF, F32 = jnp.bfloat16, jnp.float32
TOK, CHAN, ZY = ("y_lo", "x"), ("z", "y_hi", "core"), ("z", "y_hi")
VMEM = pl.BlockSpec(memory_space=pltpu.VMEM)
ANY = pl.BlockSpec(memory_space=pl.ANY)


def dot(left, right, left_dim=1, right_dim=0):
    return lax.dot_general(
        left, right, (((left_dim,), (right_dim,)), ((), ())), preferred_element_type=F32
    )


def shift(array, axis, size, step):
    return lax.ppermute(array, axis, [(i, (i + step) % size) for i in range(size)])


def swap(array, axis):
    return shift(array, axis, 2, 1)


def call(body, outs, *args, scratch=(), flops=0):
    moved = sum(a.size * a.dtype.itemsize for a in list(args) + list(outs))
    return pl.pallas_call(
        body,
        out_shape=outs if len(outs) > 1 else outs[0],
        in_specs=[VMEM] * len(args),
        out_specs=[VMEM] * len(outs) if len(outs) > 1 else VMEM,
        scratch_shapes=scratch,
        compiler_params=pltpu.CompilerParams(vmem_limit_bytes=16 * 1024 * 1024),
        cost_estimate=pl.CostEstimate(flops=flops, bytes_accessed=moved, transcendentals=0),
    )(*args)


def like(shape, dtype=BF):
    return jax.ShapeDtypeStruct(shape, dtype)


def total(ref, at=slice(None)):
    out = ref[0, at].astype(F32)
    for i in range(1, ref.shape[0]):
        out = out + ref[i, at].astype(F32)
    return out


def codes_kernel(other, acts, b, out, turned):
    core, half = lax.axis_index("core"), turned.shape[1]

    @pl.when(pl.program_id(0) == 0)
    def _():
        which = 1 - core if other else core
        turned[...] = acts[pl.ds(pl.multiple_of(which * half, half), half), :].T

    out[...] = dot(b[...], turned[...])


def codes_call(other, acts, proj_b):
    (tokens, wide), rank = acts.shape, proj_b.shape[0]
    half, step = tokens // 2, 512
    return pl.pallas_call(
        functools.partial(codes_kernel, other),
        grid=(rank // step,),
        out_shape=like((rank, half), F32),
        in_specs=[
            pl.BlockSpec((tokens, wide), lambda i: (0, 0)),
            pl.BlockSpec((step, wide), lambda i: (i, 0)),
        ],
        out_specs=pl.BlockSpec((step, half), lambda i: (i, 0)),
        scratch_shapes=[pltpu.VMEM((wide, half), BF)],
        compiler_params=pltpu.CompilerParams(vmem_limit_bytes=32 * 1024 * 1024),
        cost_estimate=pl.CostEstimate(
            flops=2 * rank * wide * half, bytes_accessed=2 * rank * wide, transcendentals=0
        ),
    )(acts, proj_b)


def sum_and_copy(blocks, out):
    value = total(blocks).astype(BF)
    for i in range(out.shape[0]):
        out[i] = value


def residual_kernel(codes, near, far, a0, a1, own, message, partial, held):
    rank, outs = codes.shape[0], a0.shape[0]
    step = 256
    for j, (target, a) in enumerate(((near, a0), (far, a1))):
        for at in range(0, outs, step):
            rows = slice(at, at + step)
            left = target[rows].astype(F32) - dot(a[rows], codes[...])
            left = left.astype(BF).T
            held[:, j * outs + at : j * outs + at + step] = left
            (own if j == 0 else message)[:, rows] = left
    sub = partial.shape[1]
    for at in range(0, rank, 512):
        cols = slice(at, at + 512)
        term = dot(held[:, :outs], a0[:, cols]) + dot(held[:, outs:], a1[:, cols])
        for i in range(partial.shape[0]):
            partial[i, :, cols] = term[i * sub : (i + 1) * sub].astype(BF)


def spread_kernel(blocks, out, held):
    y_lo = lax.axis_index("y_lo")
    held[...] = total(blocks).astype(BF)
    rank = held.shape[1]
    width = rank // 8
    for at, side in ((0, 1 - y_lo), (width, y_lo)):
        for x in range(4):
            start = pl.multiple_of(side * (rank // 2) + x * width, width)
            piece = held[:, pl.ds(start, width)]
            for i in range(out.shape[1]):
                out[x, i, :, at : at + width] = piece


def last_kernel(side, other, grad, acts, *refs):
    before, (out, turned) = refs[:-2], refs[-2:]
    core = lax.axis_index("core")
    half, wide, width = grad.shape[1], acts.shape[2], out.shape[0]
    rows = pl.ds(pl.multiple_of((1 - core if other else core) * half, half), half)
    for k in range(4):
        turned[k] = grad[k, :, side * width : (side + 1) * width].T
    for ref in before[1:]:
        out[:, wide:] = ref[...]
    for c in range(0, wide, 256):
        cols = slice(c, c + 256)
        acc = dot(turned[0], acts[0, rows, cols])
        for k in range(1, 4):
            acc = acc + dot(turned[k], acts[k, rows, cols])
        if other:
            acc = acc + before[0][:, cols]
        out[:, cols] = acc.astype(out.dtype)


def last_call(grad_m, grad_o, held, side, dtype, *joined):
    _, tokens, wide = held.shape
    half, width = tokens // 2, grad_m.shape[2] // 2
    scratch = [pltpu.VMEM((4, width, half), BF)]
    flops = 4 * tokens * width * wide
    first = call(
        functools.partial(last_kernel, side, False),
        [like((width, wide), F32)],
        grad_m, held, scratch=scratch, flops=flops,
    )
    return call(
        functools.partial(last_kernel, side, True),
        [like((width, wide + sum(j.shape[1] for j in joined)), dtype)],
        grad_o, held, first, *joined, scratch=scratch, flops=flops,
    )


def term_kernel(codes, own, codes_o, message, keep, s1, s2, s3):
    x = lax.axis_index("x")
    rank, outs = codes.shape[0], own.shape[1]
    width = rank // 8
    for k, out in enumerate((keep, s1, s2, s3)):
        for side in range(2):
            start = side * (rank // 2) + lax.rem(x + k, 4) * width
            rows = pl.ds(pl.multiple_of(start, width), width)
            left, right = codes[rows, :], codes_o[rows, :]
            for c in range(0, outs, 256):
                acc = dot(left, own[:, c : c + 256])
                acc = acc + dot(right, message[:, c : c + 256])
                out[side, :, c : c + 256] = acc.astype(out.dtype)


def term_sum_kernel(keep, r1, r2, r3, own, away):
    y_lo = lax.axis_index("y_lo")
    for out, side in ((own, y_lo), (away, 1 - y_lo)):
        value = keep[side]
        for r in (r1, r2, r3):
            value = value + r[side].astype(F32)
        out[...] = value.astype(out.dtype)


def local(acts, target, proj_b, proj_a):
    core = lax.axis_index("core")
    tokens, rank = acts.shape[0], proj_b.shape[0]
    outs, wide = target.shape[1], acts.shape[1]
    half, sub, width = tokens // 2, tokens // 16, rank // 8
    scale = -2.0 / (tokens * 8)

    def part_of(array, which, size, axis):
        return lax.dynamic_slice_in_dim(array, which * size, size, axis)

    row = lax.all_gather(acts, "x")
    pair_a = swap(proj_a, "core")
    target_t = target.T
    near_t = part_of(target_t, core, half, 1)
    pair_t = swap(part_of(target_t, 1 - core, half, 1), "core")

    arrived = swap(codes_call(True, acts, proj_b), "core")
    mine = (codes_call(False, acts, proj_b) + arrived).astype(BF).reshape(8, width, half)
    blocks = lax.all_to_all(mine, ZY, 0, 0)
    codes = call(sum_and_copy, [like((8, width, half))], blocks)
    codes = lax.all_to_all(codes, ZY, 0, 0).reshape(rank, half)

    own, message, partial = call(
        residual_kernel,
        [like((half, outs)), like((half, outs)), like((8, sub, rank))],
        codes, near_t, pair_t, proj_a, pair_a,
        scratch=[pltpu.VMEM((half, 2 * outs), BF)],
        flops=8 * half * rank * outs,
    )
    partial, codes = lax.optimization_barrier((partial, codes))
    codes_o = swap(codes, "core")
    blocks = lax.all_to_all(partial, ZY, 0, 0)

    piece = like((2, width, outs))
    terms = call(
        term_kernel,
        [like(piece.shape, F32), piece, piece, piece],
        codes, own, codes_o, swap(message, "core"),
        flops=2 * tokens * rank * outs,
    )
    terms = [terms[0]] + [shift(terms[k], "x", 4, k) for k in (1, 2, 3)]

    barrier = lax.optimization_barrier
    blocks, row, terms[0] = barrier((blocks, row, terms[0]))
    split = call(spread_kernel, [like((4, 8, sub, 2 * width))], blocks, scratch=[pltpu.VMEM((sub, rank), BF)])
    grad = lax.all_to_all(split.reshape(32, sub, 2 * width), ("x", "z", "y_hi"), 0, 0)
    grad = grad.reshape(4, half, 2 * width)
    term_o, term_a = call(
        term_sum_kernel, [like((width, outs), F32), like((width, outs))], *terms, flops=30 * 10**9
    )
    grad, term_o, term_a = barrier((grad, term_o, term_a))
    grad_o = swap(grad, "core")
    away = last_call(grad, grad_o, row, 0, BF)
    away = swap(away, "y_lo").astype(F32)
    here = last_call(grad, grad_o, row, 1, F32)
    term_a = swap(term_a, "y_lo").astype(F32)
    here, term_o = barrier((here, term_o))
    return (((term_o + term_a) * scale).T, (here + away) * scale)


def solution(mesh):
    fine = Mesh(np.reshape(mesh.devices, (2, 4, 4, 2, 2)), ("y_lo", "x", "z", "y_hi", "core"))
    return jax.shard_map(
        local,
        mesh=fine,
        in_specs=(P(TOK, CHAN), P(TOK, CHAN), P(None, CHAN), P(CHAN, None)),
        out_specs=(P(CHAN, TOK), P(TOK, CHAN)),
        check_vma=False,
    )
```

```python
import functools

import jax
import jax.numpy as jnp
import numpy as np
from jax import lax
from jax.experimental import pallas as pl
from jax.experimental.pallas import tpu as pltpu
from jax.sharding import Mesh, PartitionSpec as P

BF, F32 = jnp.bfloat16, jnp.float32
TOK, CHAN, ZY = ("y_lo", "x"), ("z", "y_hi", "core"), ("z", "y_hi")
VMEM = pl.BlockSpec(memory_space=pltpu.VMEM)
ANY = pl.BlockSpec(memory_space=pl.ANY)


def dot(left, right, left_dim=1, right_dim=0):
    return lax.dot_general(
        left, right, (((left_dim,), (right_dim,)), ((), ())), preferred_element_type=F32
    )


def shift(array, axis, size, step):
    return lax.ppermute(array, axis, [(i, (i + step) % size) for i in range(size)])


def swap(array, axis):
    return shift(array, axis, 2, 1)


def call(body, outs, *args, scratch=(), flops=0):
    moved = sum(a.size * a.dtype.itemsize for a in list(args) + list(outs))
    return pl.pallas_call(
        body,
        out_shape=outs if len(outs) > 1 else outs[0],
        in_specs=[VMEM] * len(args),
        out_specs=[VMEM] * len(outs) if len(outs) > 1 else VMEM,
        scratch_shapes=scratch,
        compiler_params=pltpu.CompilerParams(vmem_limit_bytes=16 * 1024 * 1024),
        cost_estimate=pl.CostEstimate(flops=flops, bytes_accessed=moved, transcendentals=0),
    )(*args)


def like(shape, dtype=BF):
    return jax.ShapeDtypeStruct(shape, dtype)


def total(ref, at=slice(None)):
    out = ref[0, at].astype(F32)
    for i in range(1, ref.shape[0]):
        out = out + ref[i, at].astype(F32)
    return out


def codes_kernel(other, acts, b, out, turned):
    core, half = lax.axis_index("core"), turned.shape[1]

    @pl.when(pl.program_id(0) == 0)
    def _():
        which = 1 - core if other else core
        turned[...] = acts[pl.ds(pl.multiple_of(which * half, half), half), :].T

    out[...] = dot(b[...], turned[...])


def codes_call(other, acts, proj_b):
    (tokens, wide), rank = acts.shape, proj_b.shape[0]
    half, step = tokens // 2, 512
    return pl.pallas_call(
        functools.partial(codes_kernel, other),
        grid=(rank // step,),
        out_shape=like((rank, half), F32),
        in_specs=[
            pl.BlockSpec((tokens, wide), lambda i: (0, 0)),
            pl.BlockSpec((step, wide), lambda i: (i, 0)),
        ],
        out_specs=pl.BlockSpec((step, half), lambda i: (i, 0)),
        scratch_shapes=[pltpu.VMEM((wide, half), BF)],
        compiler_params=pltpu.CompilerParams(vmem_limit_bytes=32 * 1024 * 1024),
        cost_estimate=pl.CostEstimate(
            flops=2 * rank * wide * half, bytes_accessed=2 * rank * wide, transcendentals=0
        ),
    )(acts, proj_b)


def sum_and_copy(blocks, out):
    value = total(blocks).astype(BF)
    for i in range(out.shape[0]):
        out[i] = value


def residual_kernel(codes, near, far, a0, a1, own, message, partial, held):
    rank, outs = codes.shape[0], a0.shape[0]
    step = 256
    for j, (target, a) in enumerate(((near, a0), (far, a1))):
        for at in range(0, outs, step):
            rows = slice(at, at + step)
            left = target[rows].astype(F32) - dot(a[rows], codes[...])
            left = left.astype(BF).T
            held[:, j * outs + at : j * outs + at + step] = left
            (own if j == 0 else message)[:, rows] = left
    sub = partial.shape[1]
    for at in range(0, rank, 512):
        cols = slice(at, at + 512)
        term = dot(held[:, :outs], a0[:, cols]) + dot(held[:, outs:], a1[:, cols])
        for i in range(partial.shape[0]):
            partial[i, :, cols] = term[i * sub : (i + 1) * sub].astype(BF)


def spread_kernel(blocks, out, held):
    y_lo = lax.axis_index("y_lo")
    held[...] = total(blocks).astype(BF)
    rank = held.shape[1]
    width = rank // 8
    for at, side in ((0, 1 - y_lo), (width, y_lo)):
        for x in range(4):
            start = pl.multiple_of(side * (rank // 2) + x * width, width)
            piece = held[:, pl.ds(start, width)]
            for i in range(out.shape[1]):
                out[x, i, :, at : at + width] = piece


def last_kernel(side, other, grad, acts, *refs):
    before, (out, turned) = refs[:-2], refs[-2:]
    core = lax.axis_index("core")
    half, wide, width = grad.shape[1], acts.shape[2], out.shape[0]
    rows = pl.ds(pl.multiple_of((1 - core if other else core) * half, half), half)
    for k in range(4):
        turned[k] = grad[k, :, side * width : (side + 1) * width].T
    for ref in before[1:]:
        out[:, wide:] = ref[...]
    for c in range(0, wide, 256):
        cols = slice(c, c + 256)
        acc = dot(turned[0], acts[0, rows, cols])
        for k in range(1, 4):
            acc = acc + dot(turned[k], acts[k, rows, cols])
        if other:
            acc = acc + before[0][:, cols]
        out[:, cols] = acc.astype(out.dtype)


def last_call(grad_m, grad_o, held, side, dtype, *joined):
    _, tokens, wide = held.shape
    half, width = tokens // 2, grad_m.shape[2] // 2
    scratch = [pltpu.VMEM((4, width, half), BF)]
    flops = 4 * tokens * width * wide
    first = call(
        functools.partial(last_kernel, side, False),
        [like((width, wide), F32)],
        grad_m, held, scratch=scratch, flops=flops,
    )
    return call(
        functools.partial(last_kernel, side, True),
        [like((width, wide + sum(j.shape[1] for j in joined)), dtype)],
        grad_o, held, first, *joined, scratch=scratch, flops=flops,
    )


def term_kernel(codes, own, codes_o, message, keep, s1, s2, s3):
    x = lax.axis_index("x")
    rank, outs = codes.shape[0], own.shape[1]
    width = rank // 8
    for k, out in enumerate((keep, s1, s2, s3)):
        for side in range(2):
            start = side * (rank // 2) + lax.rem(x + k, 4) * width
            rows = pl.ds(pl.multiple_of(start, width), width)
            left, right = codes[rows, :], codes_o[rows, :]
            for c in range(0, outs, 256):
                acc = dot(left, own[:, c : c + 256])
                acc = acc + dot(right, message[:, c : c + 256])
                out[side, :, c : c + 256] = acc.astype(out.dtype)


def term_sum_kernel(keep, r1, r2, r3, own, away):
    y_lo = lax.axis_index("y_lo")
    for out, side in ((own, y_lo), (away, 1 - y_lo)):
        value = keep[side]
        for r in (r1, r2, r3):
            value = value + r[side].astype(F32)
        out[...] = value.T.astype(out.dtype)


def local(acts, target, proj_b, proj_a):
    core = lax.axis_index("core")
    tokens, rank = acts.shape[0], proj_b.shape[0]
    outs, wide = target.shape[1], acts.shape[1]
    half, sub, width = tokens // 2, tokens // 16, rank // 8
    scale = -2.0 / (tokens * 8)

    def part_of(array, which, size, axis):
        return lax.dynamic_slice_in_dim(array, which * size, size, axis)

    row = lax.all_gather(acts, "x")
    pair_a = swap(proj_a, "core")
    target_t = target.T
    near_t = part_of(target_t, core, half, 1)
    pair_t = swap(part_of(target_t, 1 - core, half, 1), "core")

    arrived = swap(codes_call(True, acts, proj_b), "core")
    mine = (codes_call(False, acts, proj_b) + arrived).astype(BF).reshape(8, width, half)
    blocks = lax.all_to_all(mine, ZY, 0, 0)
    codes = call(sum_and_copy, [like((8, width, half))], blocks)
    codes = lax.all_to_all(codes, ZY, 0, 0).reshape(rank, half)

    own, message, partial = call(
        residual_kernel,
        [like((half, outs)), like((half, outs)), like((8, sub, rank))],
        codes, near_t, pair_t, proj_a, pair_a,
        scratch=[pltpu.VMEM((half, 2 * outs), BF)],
        flops=8 * half * rank * outs,
    )
    partial, codes = lax.optimization_barrier((partial, codes))
    codes_o = swap(codes, "core")
    blocks = lax.all_to_all(partial, ZY, 0, 0)

    piece = like((2, width, outs))
    terms = call(
        term_kernel,
        [like(piece.shape, F32), piece, piece, piece],
        codes, own, codes_o, swap(message, "core"),
        flops=2 * tokens * rank * outs,
    )
    terms = [terms[0]] + [shift(terms[k], "x", 4, k) for k in (1, 2, 3)]

    barrier = lax.optimization_barrier
    blocks, row, terms[0] = barrier((blocks, row, terms[0]))
    split = call(spread_kernel, [like((4, 8, sub, 2 * width))], blocks, scratch=[pltpu.VMEM((sub, rank), BF)], flops=15 * 10**9)
    grad = lax.all_to_all(split.reshape(32, sub, 2 * width), ("x", "z", "y_hi"), 0, 0)
    grad = grad.reshape(4, half, 2 * width)
    grad_o = swap(grad, "core")
    away = last_call(grad, grad_o, row, 0, BF)
    away = swap(away, "y_lo").astype(F32)
    here = last_call(grad, grad_o, row, 1, F32)
    term_o, term_a = call(term_sum_kernel, [like((outs, width), F32), like((outs, width))], *terms)
    term_a = swap(term_a, "y_lo").astype(F32)
    grad_b = (here + away) * scale
    grad_b, term_o = barrier((grad_b, term_o))
    return ((term_o + term_a) * scale, grad_b)


def solution(mesh):
    fine = Mesh(np.reshape(mesh.devices, (2, 4, 4, 2, 2)), ("y_lo", "x", "z", "y_hi", "core"))
    return jax.shard_map(
        local,
        mesh=fine,
        in_specs=(P(TOK, CHAN), P(TOK, CHAN), P(None, CHAN), P(CHAN, None)),
        out_specs=(P(CHAN, TOK), P(TOK, CHAN)),
        check_vma=False,
    )
```

```python
import functools

import jax
import jax.numpy as jnp
import numpy as np
from jax import lax
from jax.experimental import pallas as pl
from jax.experimental.pallas import tpu as pltpu
from jax.sharding import Mesh, PartitionSpec as P

BF, F32 = jnp.bfloat16, jnp.float32
TOK, CHAN, ZY = ("y_lo", "x"), ("z", "y_hi", "core"), ("z", "y_hi")
VMEM = pl.BlockSpec(memory_space=pltpu.VMEM)
ANY = pl.BlockSpec(memory_space=pl.ANY)


def dot(left, right, left_dim=1, right_dim=0):
    return lax.dot_general(
        left, right, (((left_dim,), (right_dim,)), ((), ())), preferred_element_type=F32
    )


def shift(array, axis, size, step):
    return lax.ppermute(array, axis, [(i, (i + step) % size) for i in range(size)])


def swap(array, axis):
    return shift(array, axis, 2, 1)


def call(body, outs, *args, scratch=(), flops=0):
    moved = sum(a.size * a.dtype.itemsize for a in list(args) + list(outs))
    return pl.pallas_call(
        body,
        out_shape=outs if len(outs) > 1 else outs[0],
        in_specs=[VMEM] * len(args),
        out_specs=[VMEM] * len(outs) if len(outs) > 1 else VMEM,
        scratch_shapes=scratch,
        compiler_params=pltpu.CompilerParams(vmem_limit_bytes=16 * 1024 * 1024),
        cost_estimate=pl.CostEstimate(flops=flops, bytes_accessed=moved, transcendentals=0),
    )(*args)


def like(shape, dtype=BF):
    return jax.ShapeDtypeStruct(shape, dtype)


def total(ref, at=slice(None)):
    out = ref[0, at].astype(F32)
    for i in range(1, ref.shape[0]):
        out = out + ref[i, at].astype(F32)
    return out


def codes_kernel(other, acts, b, out, turned):
    core, half = lax.axis_index("core"), turned.shape[1]

    @pl.when(pl.program_id(0) == 0)
    def _():
        which = 1 - core if other else core
        turned[...] = acts[pl.ds(pl.multiple_of(which * half, half), half), :].T

    out[...] = dot(b[...], turned[...])


def codes_call(other, acts, proj_b):
    (tokens, wide), rank = acts.shape, proj_b.shape[0]
    half, step = tokens // 2, 512
    return pl.pallas_call(
        functools.partial(codes_kernel, other),
        grid=(rank // step,),
        out_shape=like((rank, half), F32),
        in_specs=[
            pl.BlockSpec((tokens, wide), lambda i: (0, 0)),
            pl.BlockSpec((step, wide), lambda i: (i, 0)),
        ],
        out_specs=pl.BlockSpec((step, half), lambda i: (i, 0)),
        scratch_shapes=[pltpu.VMEM((wide, half), BF)],
        compiler_params=pltpu.CompilerParams(vmem_limit_bytes=32 * 1024 * 1024),
        cost_estimate=pl.CostEstimate(
            flops=2 * rank * wide * half, bytes_accessed=2 * rank * wide, transcendentals=0
        ),
    )(acts, proj_b)


def sum_and_copy(blocks, out):
    value = total(blocks).astype(BF)
    for i in range(out.shape[0]):
        out[i] = value


def residual_kernel(codes, near, far, a0, a1, own, message, partial, held):
    rank, outs = codes.shape[0], a0.shape[0]
    step = 256
    for j, (target, a) in enumerate(((near, a0), (far, a1))):
        for at in range(0, outs, step):
            rows = slice(at, at + step)
            left = target[rows].astype(F32) - dot(a[rows], codes[...])
            left = left.astype(BF).T
            held[:, j * outs + at : j * outs + at + step] = left
            (own if j == 0 else message)[:, rows] = left
    sub = partial.shape[1]
    for at in range(0, rank, 512):
        cols = slice(at, at + 512)
        term = dot(held[:, :outs], a0[:, cols]) + dot(held[:, outs:], a1[:, cols])
        for i in range(partial.shape[0]):
            partial[i, :, cols] = term[i * sub : (i + 1) * sub].astype(BF)


def spread_kernel(blocks, out, held):
    y_lo = lax.axis_index("y_lo")
    held[...] = total(blocks).astype(BF)
    rank = held.shape[1]
    width = rank // 8
    for at, side in ((0, 1 - y_lo), (width, y_lo)):
        for x in range(4):
            start = pl.multiple_of(side * (rank // 2) + x * width, width)
            piece = held[:, pl.ds(start, width)]
            for i in range(out.shape[1]):
                out[x, i, :, at : at + width] = piece


def last_kernel(side, other, grad, acts, *refs):
    before, (out, turned) = refs[:-2], refs[-2:]
    core = lax.axis_index("core")
    half, wide, width = grad.shape[1], acts.shape[2], out.shape[0]
    rows = pl.ds(pl.multiple_of((1 - core if other else core) * half, half), half)
    for k in range(4):
        turned[k] = grad[k, :, side * width : (side + 1) * width].T
    for ref in before[1:]:
        out[:, wide:] = ref[...]
    for c in range(0, wide, 256):
        cols = slice(c, c + 256)
        acc = dot(turned[0], acts[0, rows, cols])
        for k in range(1, 4):
            acc = acc + dot(turned[k], acts[k, rows, cols])
        if other:
            acc = acc + before[0][:, cols]
        out[:, cols] = acc.astype(out.dtype)


def last_call(grad_m, grad_o, held, side, dtype, *joined):
    _, tokens, wide = held.shape
    half, width = tokens // 2, grad_m.shape[2] // 2
    scratch = [pltpu.VMEM((4, width, half), BF)]
    flops = 4 * tokens * width * wide
    first = call(
        functools.partial(last_kernel, side, False),
        [like((width, wide), F32)],
        grad_m, held, scratch=scratch, flops=flops,
    )
    return call(
        functools.partial(last_kernel, side, True),
        [like((width, wide + sum(j.shape[1] for j in joined)), dtype)],
        grad_o, held, first, *joined, scratch=scratch, flops=flops,
    )


def term_kernel(codes, own, codes_o, message, keep, s1, s2, s3):
    x = lax.axis_index("x")
    rank, outs = codes.shape[0], own.shape[1]
    width = rank // 8
    for k, out in enumerate((keep, s1, s2, s3)):
        for side in range(2):
            start = side * (rank // 2) + lax.rem(x + k, 4) * width
            rows = pl.ds(pl.multiple_of(start, width), width)
            left, right = codes[rows, :], codes_o[rows, :]
            for c in range(0, outs, 256):
                acc = dot(left, own[:, c : c + 256])
                acc = acc + dot(right, message[:, c : c + 256])
                out[side, :, c : c + 256] = acc.astype(out.dtype)


def term_add_kernel(keep, r2, out):
    for side in range(2):
        out[side] = keep[side] + r2[side].astype(F32)


def term_sum_kernel(keep, r1, r3, own, away):
    y_lo = lax.axis_index("y_lo")
    for out, side in ((own, y_lo), (away, 1 - y_lo)):
        value = keep[side] + r1[side].astype(F32) + r3[side].astype(F32)
        out[...] = value.T.astype(out.dtype)


def local(acts, target, proj_b, proj_a):
    core = lax.axis_index("core")
    tokens, rank = acts.shape[0], proj_b.shape[0]
    outs, wide = target.shape[1], acts.shape[1]
    half, sub, width = tokens // 2, tokens // 16, rank // 8
    scale = -2.0 / (tokens * 8)

    def part_of(array, which, size, axis):
        return lax.dynamic_slice_in_dim(array, which * size, size, axis)

    row = lax.all_gather(acts, "x")
    pair_a = swap(proj_a, "core")
    target_t = target.T
    near_t = part_of(target_t, core, half, 1)
    pair_t = swap(part_of(target_t, 1 - core, half, 1), "core")

    arrived = swap(codes_call(True, acts, proj_b), "core")
    mine = (codes_call(False, acts, proj_b) + arrived).astype(BF).reshape(8, width, half)
    blocks = lax.all_to_all(mine, ZY, 0, 0)
    codes = call(sum_and_copy, [like((8, width, half))], blocks)
    codes = lax.all_to_all(codes, ZY, 0, 0).reshape(rank, half)

    own, message, partial = call(
        residual_kernel,
        [like((half, outs)), like((half, outs)), like((8, sub, rank))],
        codes, near_t, pair_t, proj_a, pair_a,
        scratch=[pltpu.VMEM((half, 2 * outs), BF)],
        flops=8 * half * rank * outs,
    )
    partial, codes = lax.optimization_barrier((partial, codes))
    codes_o = swap(codes, "core")
    blocks = lax.all_to_all(partial, ZY, 0, 0)

    piece = like((2, width, outs))
    terms = call(
        term_kernel,
        [like(piece.shape, F32), piece, piece, piece],
        codes, own, codes_o, swap(message, "core"),
        flops=2 * tokens * rank * outs,
    )
    terms = list(terms)
    far = shift(terms[2], "x", 4, 2)

    barrier = lax.optimization_barrier
    blocks, row, terms[0] = barrier((blocks, row, terms[0]))
    split = call(spread_kernel, [like((4, 8, sub, 2 * width))], blocks, scratch=[pltpu.VMEM((sub, rank), BF)], flops=15 * 10**9)
    grad = lax.all_to_all(split.reshape(32, sub, 2 * width), ("x", "z", "y_hi"), 0, 0)
    grad = grad.reshape(4, half, 2 * width)
    kept = call(term_add_kernel, [like((2, width, outs), F32)], terms[0], far, flops=30 * 10**9)
    grad, kept, plus, minus = barrier((grad, kept, terms[1], terms[3]))
    near = [shift(plus, "x", 4, 1), shift(minus, "x", 4, 3)]
    grad_o = swap(grad, "core")
    away = last_call(grad, grad_o, row, 0, BF)
    away = swap(away, "y_lo").astype(F32)
    here = last_call(grad, grad_o, row, 1, F32)
    term_o, term_a = call(term_sum_kernel, [like((outs, width), F32), like((outs, width))], kept, *near)
    term_a = swap(term_a, "y_lo").astype(F32)
    grad_b = (here + away) * scale
    grad_b, term_o = barrier((grad_b, term_o))
    return ((term_o + term_a) * scale, grad_b)


def solution(mesh):
    fine = Mesh(np.reshape(mesh.devices, (2, 4, 4, 2, 2)), ("y_lo", "x", "z", "y_hi", "core"))
    return jax.shard_map(
        local,
        mesh=fine,
        in_specs=(P(TOK, CHAN), P(TOK, CHAN), P(None, CHAN), P(CHAN, None)),
        out_specs=(P(CHAN, TOK), P(TOK, CHAN)),
        check_vma=False,
    )
```

```python
import functools

import jax
import jax.numpy as jnp
import numpy as np
from jax import lax
from jax.experimental import pallas as pl
from jax.experimental.pallas import tpu as pltpu
from jax.sharding import Mesh, PartitionSpec as P

BF, F32 = jnp.bfloat16, jnp.float32
TOK, CHAN, ZY = ("y_lo", "x"), ("z", "y_hi", "core"), ("z", "y_hi")
VMEM = pl.BlockSpec(memory_space=pltpu.VMEM)
ANY = pl.BlockSpec(memory_space=pl.ANY)


def dot(left, right, left_dim=1, right_dim=0):
    return lax.dot_general(
        left, right, (((left_dim,), (right_dim,)), ((), ())), preferred_element_type=F32
    )


def shift(array, axis, size, step):
    return lax.ppermute(array, axis, [(i, (i + step) % size) for i in range(size)])


def swap(array, axis):
    return shift(array, axis, 2, 1)


def call(body, outs, *args, scratch=(), flops=0):
    moved = sum(a.size * a.dtype.itemsize for a in list(args) + list(outs))
    return pl.pallas_call(
        body,
        out_shape=outs if len(outs) > 1 else outs[0],
        in_specs=[VMEM] * len(args),
        out_specs=[VMEM] * len(outs) if len(outs) > 1 else VMEM,
        scratch_shapes=scratch,
        compiler_params=pltpu.CompilerParams(vmem_limit_bytes=16 * 1024 * 1024),
        cost_estimate=pl.CostEstimate(flops=flops, bytes_accessed=moved, transcendentals=0),
    )(*args)


def like(shape, dtype=BF):
    return jax.ShapeDtypeStruct(shape, dtype)


def total(ref, at=slice(None)):
    out = ref[0, at].astype(F32)
    for i in range(1, ref.shape[0]):
        out = out + ref[i, at].astype(F32)
    return out


def codes_kernel(other, acts, b, out, turned):
    core, half = lax.axis_index("core"), turned.shape[1]

    @pl.when(pl.program_id(0) == 0)
    def _():
        which = 1 - core if other else core
        turned[...] = acts[pl.ds(pl.multiple_of(which * half, half), half), :].T

    out[...] = dot(b[...], turned[...])


def codes_call(other, acts, proj_b):
    (tokens, wide), rank = acts.shape, proj_b.shape[0]
    half, step = tokens // 2, 512
    return pl.pallas_call(
        functools.partial(codes_kernel, other),
        grid=(rank // step,),
        out_shape=like((rank, half), F32),
        in_specs=[
            pl.BlockSpec((tokens, wide), lambda i: (0, 0)),
            pl.BlockSpec((step, wide), lambda i: (i, 0)),
        ],
        out_specs=pl.BlockSpec((step, half), lambda i: (i, 0)),
        scratch_shapes=[pltpu.VMEM((wide, half), BF)],
        compiler_params=pltpu.CompilerParams(vmem_limit_bytes=32 * 1024 * 1024),
        cost_estimate=pl.CostEstimate(
            flops=2 * rank * wide * half, bytes_accessed=2 * rank * wide, transcendentals=0
        ),
    )(acts, proj_b)


def sum_and_copy(blocks, out):
    value = total(blocks).astype(BF)
    for i in range(out.shape[0]):
        out[i] = value


def residual_kernel(codes, near, far, a0, a1, own, message, partial, held):
    rank, outs = codes.shape[0], a0.shape[0]
    step = 256
    for j, (target, a) in enumerate(((near, a0), (far, a1))):
        for at in range(0, outs, step):
            rows = slice(at, at + step)
            left = target[rows].astype(F32) - dot(a[rows], codes[...])
            left = left.astype(BF).T
            held[:, j * outs + at : j * outs + at + step] = left
            (own if j == 0 else message)[:, rows] = left
    sub = partial.shape[1]
    for at in range(0, rank, 512):
        cols = slice(at, at + 512)
        term = dot(held[:, :outs], a0[:, cols]) + dot(held[:, outs:], a1[:, cols])
        for i in range(partial.shape[0]):
            partial[i, :, cols] = term[i * sub : (i + 1) * sub].astype(BF)


def spread_kernel(blocks, out, held):
    y_lo = lax.axis_index("y_lo")
    held[...] = total(blocks).astype(BF)
    rank = held.shape[1]
    width = rank // 8
    for at, side in ((0, 1 - y_lo), (width, y_lo)):
        for x in range(4):
            start = pl.multiple_of(side * (rank // 2) + x * width, width)
            piece = held[:, pl.ds(start, width)]
            for i in range(out.shape[1]):
                out[x, i, :, at : at + width] = piece


def last_kernel(side, other, grad, acts, *refs):
    before, (out, turned) = refs[:-2], refs[-2:]
    core = lax.axis_index("core")
    half, wide, width = grad.shape[1], acts.shape[2], out.shape[0]
    rows = pl.ds(pl.multiple_of((1 - core if other else core) * half, half), half)
    for k in range(4):
        turned[k] = grad[k, :, side * width : (side + 1) * width].T
    for ref in before[1:]:
        out[:, wide:] = ref[...]
    for c in range(0, wide, 256):
        cols = slice(c, c + 256)
        acc = dot(turned[0], acts[0, rows, cols])
        for k in range(1, 4):
            acc = acc + dot(turned[k], acts[k, rows, cols])
        if other:
            acc = acc + before[0][:, cols]
        out[:, cols] = acc.astype(out.dtype)


def last_call(grad_m, grad_o, held, side, dtype, *joined):
    _, tokens, wide = held.shape
    half, width = tokens // 2, grad_m.shape[2] // 2
    scratch = [pltpu.VMEM((4, width, half), BF)]
    flops = 4 * tokens * width * wide
    first = call(
        functools.partial(last_kernel, side, False),
        [like((width, wide), F32)],
        grad_m, held, scratch=scratch, flops=flops,
    )
    return call(
        functools.partial(last_kernel, side, True),
        [like((width, wide + sum(j.shape[1] for j in joined)), dtype)],
        grad_o, held, first, *joined, scratch=scratch, flops=flops,
    )


def term_kernel(codes, own, codes_o, message, keep, s1, s2, s3):
    x = lax.axis_index("x")
    rank, outs = codes.shape[0], own.shape[1]
    width = rank // 8
    for k, out in enumerate((keep, s1, s2, s3)):
        for side in range(2):
            start = side * (rank // 2) + lax.rem(x + k, 4) * width
            rows = pl.ds(pl.multiple_of(start, width), width)
            left, right = codes[rows, :], codes_o[rows, :]
            for c in range(0, outs, 256):
                acc = dot(left, own[:, c : c + 256])
                acc = acc + dot(right, message[:, c : c + 256])
                out[side, :, c : c + 256] = acc.astype(out.dtype)


def term_add_kernel(keep, r2, out):
    for side in range(2):
        out[side] = keep[side] + r2[side].astype(F32)


def term_sum_kernel(keep, r1, r3, own, away):
    y_lo = lax.axis_index("y_lo")
    for out, side in ((own, y_lo), (away, 1 - y_lo)):
        value = keep[side] + r1[side].astype(F32) + r3[side].astype(F32)
        out[...] = value.T.astype(out.dtype)


def local(acts, target, proj_b, proj_a):
    core = lax.axis_index("core")
    tokens, rank = acts.shape[0], proj_b.shape[0]
    outs, wide = target.shape[1], acts.shape[1]
    half, sub, width = tokens // 2, tokens // 16, rank // 8
    scale = -2.0 / (tokens * 8)

    def part_of(array, which, size, axis):
        return lax.dynamic_slice_in_dim(array, which * size, size, axis)

    row = lax.all_gather(acts, "x")
    pair_a = swap(proj_a, "core")
    target_t = target.T
    near_t = part_of(target_t, core, half, 1)
    pair_t = swap(part_of(target_t, 1 - core, half, 1), "core")

    arrived = swap(codes_call(True, acts, proj_b), "core")
    mine = (codes_call(False, acts, proj_b) + arrived).astype(BF).reshape(8, width, half)
    blocks = lax.all_to_all(mine, ZY, 0, 0)
    codes = call(sum_and_copy, [like((8, width, half))], blocks)
    codes = lax.all_to_all(codes, ZY, 0, 0).reshape(rank, half)

    own, message, partial = call(
        residual_kernel,
        [like((half, outs)), like((half, outs)), like((8, sub, rank))],
        codes, near_t, pair_t, proj_a, pair_a,
        scratch=[pltpu.VMEM((half, 2 * outs), BF)],
        flops=8 * half * rank * outs,
    )
    partial, codes = lax.optimization_barrier((partial, codes))
    codes_o = swap(codes, "core")
    blocks = lax.all_to_all(partial, ZY, 0, 0)

    piece = like((2, width, outs))
    terms = call(
        term_kernel,
        [like(piece.shape, F32), piece, piece, piece],
        codes, own, codes_o, swap(message, "core"),
        flops=2 * tokens * rank * outs,
    )
    terms = list(terms)
    far = shift(terms[2], "x", 4, 2)

    barrier = lax.optimization_barrier
    blocks, row, terms[0] = barrier((blocks, row, terms[0]))
    split = call(spread_kernel, [like((4, 8, sub, 2 * width))], blocks, scratch=[pltpu.VMEM((sub, rank), BF)], flops=15 * 10**9)
    grad = lax.all_to_all(split.reshape(32, sub, 2 * width), ("x", "z", "y_hi"), 0, 0)
    grad = grad.reshape(4, half, 2 * width)
    kept = call(term_add_kernel, [like((2, width, outs), F32)], terms[0], far, flops=7 * 10**9)
    grad, kept, plus, minus = barrier((grad, kept, terms[1], terms[3]))
    near = [shift(plus, "x", 4, 1), shift(minus, "x", 4, 3)]
    grad_o = swap(grad, "core")
    away = last_call(grad, grad_o, row, 0, BF)
    away = swap(away, "y_lo").astype(F32)
    here = last_call(grad, grad_o, row, 1, F32)
    term_o, term_a = call(term_sum_kernel, [like((outs, width), F32), like((outs, width))], kept, *near)
    term_a = swap(term_a, "y_lo").astype(F32)
    grad_b = (here + away) * scale
    grad_b, term_o = barrier((grad_b, term_o))
    return ((term_o + term_a) * scale, grad_b)


def solution(mesh):
    fine = Mesh(np.reshape(mesh.devices, (2, 4, 4, 2, 2)), ("y_lo", "x", "z", "y_hi", "core"))
    return jax.shard_map(
        local,
        mesh=fine,
        in_specs=(P(TOK, CHAN), P(TOK, CHAN), P(None, CHAN), P(CHAN, None)),
        out_specs=(P(CHAN, TOK), P(TOK, CHAN)),
        check_vma=False,
    )
```

```python
import functools

import jax
import jax.numpy as jnp
import numpy as np
from jax import lax
from jax.experimental import pallas as pl
from jax.experimental.pallas import tpu as pltpu
from jax.sharding import Mesh, PartitionSpec as P

BF, F32 = jnp.bfloat16, jnp.float32
TOK, CHAN, ZY = ("y_lo", "x"), ("z", "y_hi", "core"), ("z", "y_hi")
VMEM = pl.BlockSpec(memory_space=pltpu.VMEM)
ANY = pl.BlockSpec(memory_space=pl.ANY)


def dot(left, right, left_dim=1, right_dim=0):
    return lax.dot_general(
        left, right, (((left_dim,), (right_dim,)), ((), ())), preferred_element_type=F32
    )


def shift(array, axis, size, step):
    return lax.ppermute(array, axis, [(i, (i + step) % size) for i in range(size)])


def swap(array, axis):
    return shift(array, axis, 2, 1)


def call(body, outs, *args, scratch=(), flops=0):
    moved = sum(a.size * a.dtype.itemsize for a in list(args) + list(outs))
    return pl.pallas_call(
        body,
        out_shape=outs if len(outs) > 1 else outs[0],
        in_specs=[VMEM] * len(args),
        out_specs=[VMEM] * len(outs) if len(outs) > 1 else VMEM,
        scratch_shapes=scratch,
        compiler_params=pltpu.CompilerParams(vmem_limit_bytes=16 * 1024 * 1024),
        cost_estimate=pl.CostEstimate(flops=flops, bytes_accessed=moved, transcendentals=0),
    )(*args)


def like(shape, dtype=BF):
    return jax.ShapeDtypeStruct(shape, dtype)


def total(ref, at=slice(None)):
    out = ref[0, at].astype(F32)
    for i in range(1, ref.shape[0]):
        out = out + ref[i, at].astype(F32)
    return out


def codes_kernel(other, acts, b, out, turned):
    core, half = lax.axis_index("core"), turned.shape[1]

    @pl.when(pl.program_id(0) == 0)
    def _():
        which = 1 - core if other else core
        turned[...] = acts[pl.ds(pl.multiple_of(which * half, half), half), :].T

    out[...] = dot(b[...], turned[...])


def codes_call(other, acts, proj_b):
    (tokens, wide), rank = acts.shape, proj_b.shape[0]
    half, step = tokens // 2, 512
    return pl.pallas_call(
        functools.partial(codes_kernel, other),
        grid=(rank // step,),
        out_shape=like((rank, half), F32),
        in_specs=[
            pl.BlockSpec((tokens, wide), lambda i: (0, 0)),
            pl.BlockSpec((step, wide), lambda i: (i, 0)),
        ],
        out_specs=pl.BlockSpec((step, half), lambda i: (i, 0)),
        scratch_shapes=[pltpu.VMEM((wide, half), BF)],
        compiler_params=pltpu.CompilerParams(vmem_limit_bytes=32 * 1024 * 1024),
        cost_estimate=pl.CostEstimate(
            flops=2 * rank * wide * half, bytes_accessed=2 * rank * wide, transcendentals=0
        ),
    )(acts, proj_b)


def sum_and_copy(blocks, out):
    value = total(blocks).astype(BF)
    for i in range(out.shape[0]):
        out[i] = value


def residual_kernel(codes, near, far, a0, a1, own, message, partial, held):
    rank, outs = codes.shape[0], a0.shape[0]
    step = 256
    for j, (target, a) in enumerate(((near, a0), (far, a1))):
        for at in range(0, outs, step):
            rows = slice(at, at + step)
            left = target[rows].astype(F32) - dot(a[rows], codes[...])
            left = left.astype(BF).T
            held[:, j * outs + at : j * outs + at + step] = left
            (own if j == 0 else message)[:, rows] = left
    sub = partial.shape[1]
    for at in range(0, rank, 512):
        cols = slice(at, at + 512)
        term = dot(held[:, :outs], a0[:, cols]) + dot(held[:, outs:], a1[:, cols])
        for i in range(partial.shape[0]):
            partial[i, :, cols] = term[i * sub : (i + 1) * sub].astype(BF)


def spread_kernel(blocks, out, held):
    y_lo = lax.axis_index("y_lo")
    held[...] = total(blocks).astype(BF)
    rank = held.shape[1]
    width = rank // 8
    for at, side in ((0, 1 - y_lo), (width, y_lo)):
        for x in range(4):
            start = pl.multiple_of(side * (rank // 2) + x * width, width)
            piece = held[:, pl.ds(start, width)]
            for i in range(out.shape[1]):
                out[x, i, :, at : at + width] = piece


def last_kernel(side, other, grad, acts, *refs):
    before, (out, turned) = refs[:-2], refs[-2:]
    core = lax.axis_index("core")
    half, wide, width = grad.shape[1], acts.shape[2], out.shape[0]
    rows = pl.ds(pl.multiple_of((1 - core if other else core) * half, half), half)
    for k in range(4):
        turned[k] = grad[k, :, side * width : (side + 1) * width].T
    for ref in before[1:]:
        out[:, wide:] = ref[...]
    for c in range(0, wide, 256):
        cols = slice(c, c + 256)
        acc = dot(turned[0], acts[0, rows, cols])
        for k in range(1, 4):
            acc = acc + dot(turned[k], acts[k, rows, cols])
        if other:
            acc = acc + before[0][:, cols]
        out[:, cols] = acc.astype(out.dtype)


def last_call(grad_m, grad_o, held, side, dtype, *joined):
    _, tokens, wide = held.shape
    half, width = tokens // 2, grad_m.shape[2] // 2
    scratch = [pltpu.VMEM((4, width, half), BF)]
    flops = 4 * tokens * width * wide
    first = call(
        functools.partial(last_kernel, side, False),
        [like((width, wide), F32)],
        grad_m, held, scratch=scratch, flops=flops,
    )
    return call(
        functools.partial(last_kernel, side, True),
        [like((width, wide + sum(j.shape[1] for j in joined)), dtype)],
        grad_o, held, first, *joined, scratch=scratch, flops=flops,
    )


def term_kernel(codes, own, codes_o, message, keep, s1, s2, s3):
    x = lax.axis_index("x")
    rank, outs = codes.shape[0], own.shape[1]
    width = rank // 8
    for k, out in enumerate((keep, s1, s2, s3)):
        for side in range(2):
            start = side * (rank // 2) + lax.rem(x + k, 4) * width
            rows = pl.ds(pl.multiple_of(start, width), width)
            left, right = codes[rows, :], codes_o[rows, :]
            for c in range(0, outs, 256):
                acc = dot(left, own[:, c : c + 256])
                acc = acc + dot(right, message[:, c : c + 256])
                out[side, :, c : c + 256] = acc.astype(out.dtype)


def term_sum_kernel(keep, r1, r2, r3, own, away):
    y_lo = lax.axis_index("y_lo")
    for out, side in ((own, y_lo), (away, 1 - y_lo)):
        value = keep[side]
        for r in (r1, r2, r3):
            value = value + r[side].astype(F32)
        out[...] = value.T.astype(out.dtype)


def local(acts, target, proj_b, proj_a):
    core = lax.axis_index("core")
    tokens, rank = acts.shape[0], proj_b.shape[0]
    outs, wide = target.shape[1], acts.shape[1]
    half, sub, width = tokens // 2, tokens // 16, rank // 8
    scale = -2.0 / (tokens * 8)

    def part_of(array, which, size, axis):
        return lax.dynamic_slice_in_dim(array, which * size, size, axis)

    row = lax.all_gather(acts, "x")
    pair_a = swap(proj_a, "core")
    target_t = target.T
    near_t = part_of(target_t, core, half, 1)
    pair_t = swap(part_of(target_t, 1 - core, half, 1), "core")

    arrived = swap(codes_call(True, acts, proj_b), "core")
    mine = (codes_call(False, acts, proj_b) + arrived).astype(BF).reshape(8, width, half)
    blocks = lax.all_to_all(mine, ZY, 0, 0)
    codes = call(sum_and_copy, [like((8, width, half))], blocks)
    codes = lax.all_to_all(codes, ZY, 0, 0).reshape(rank, half)

    own, message, partial = call(
        residual_kernel,
        [like((half, outs)), like((half, outs)), like((8, sub, rank))],
        codes, near_t, pair_t, proj_a, pair_a,
        scratch=[pltpu.VMEM((half, 2 * outs), BF)],
        flops=8 * half * rank * outs,
    )
    partial, codes = lax.optimization_barrier((partial, codes))
    codes_o = swap(codes, "core")
    blocks = lax.all_to_all(partial, ZY, 0, 0)

    piece = like((2, width, outs))
    terms = call(
        term_kernel,
        [like(piece.shape, F32), piece, piece, piece],
        codes, own, codes_o, swap(message, "core"),
        flops=2 * tokens * rank * outs,
    )
    terms = list(terms)
    far = shift(terms[2], "x", 4, 2)

    barrier = lax.optimization_barrier
    blocks, row, terms[0] = barrier((blocks, row, terms[0]))
    split = call(spread_kernel, [like((4, 8, sub, 2 * width))], blocks, scratch=[pltpu.VMEM((sub, rank), BF)], flops=15 * 10**9)
    grad = lax.all_to_all(split.reshape(32, sub, 2 * width), ("x", "z", "y_hi"), 0, 0)
    grad = grad.reshape(4, half, 2 * width)
    grad, far, plus, minus = barrier((grad, far, terms[1], terms[3]))
    terms = [terms[0], shift(plus, "x", 4, 1), far, shift(minus, "x", 4, 3)]
    grad_o = swap(grad, "core")
    away = last_call(grad, grad_o, row, 0, BF)
    away = swap(away, "y_lo").astype(F32)
    here = last_call(grad, grad_o, row, 1, F32)
    term_o, term_a = call(term_sum_kernel, [like((outs, width), F32), like((outs, width))], *terms)
    term_a = swap(term_a, "y_lo").astype(F32)
    grad_b = (here + away) * scale
    grad_b, term_o = barrier((grad_b, term_o))
    return ((term_o + term_a) * scale, grad_b)


def solution(mesh):
    fine = Mesh(np.reshape(mesh.devices, (2, 4, 4, 2, 2)), ("y_lo", "x", "z", "y_hi", "core"))
    return jax.shard_map(
        local,
        mesh=fine,
        in_specs=(P(TOK, CHAN), P(TOK, CHAN), P(None, CHAN), P(CHAN, None)),
        out_specs=(P(CHAN, TOK), P(TOK, CHAN)),
        check_vma=False,
    )
```

```python
import functools

import jax
import jax.numpy as jnp
import numpy as np
from jax import lax
from jax.experimental import pallas as pl
from jax.experimental.pallas import tpu as pltpu
from jax.sharding import Mesh, PartitionSpec as P

BF, F32 = jnp.bfloat16, jnp.float32
TOK, CHAN, ZY = ("y_lo", "x"), ("z", "y_hi", "core"), ("z", "y_hi")
VMEM = pl.BlockSpec(memory_space=pltpu.VMEM)
ANY = pl.BlockSpec(memory_space=pl.ANY)


def dot(left, right, left_dim=1, right_dim=0):
    return lax.dot_general(
        left, right, (((left_dim,), (right_dim,)), ((), ())), preferred_element_type=F32
    )


def shift(array, axis, size, step):
    return lax.ppermute(array, axis, [(i, (i + step) % size) for i in range(size)])


def swap(array, axis):
    return shift(array, axis, 2, 1)


def call(body, outs, *args, scratch=(), flops=0):
    moved = sum(a.size * a.dtype.itemsize for a in list(args) + list(outs))
    return pl.pallas_call(
        body,
        out_shape=outs if len(outs) > 1 else outs[0],
        in_specs=[VMEM] * len(args),
        out_specs=[VMEM] * len(outs) if len(outs) > 1 else VMEM,
        scratch_shapes=scratch,
        compiler_params=pltpu.CompilerParams(vmem_limit_bytes=16 * 1024 * 1024),
        cost_estimate=pl.CostEstimate(flops=flops, bytes_accessed=moved, transcendentals=0),
    )(*args)


def like(shape, dtype=BF):
    return jax.ShapeDtypeStruct(shape, dtype)


def total(ref, at=slice(None)):
    out = ref[0, at].astype(F32)
    for i in range(1, ref.shape[0]):
        out = out + ref[i, at].astype(F32)
    return out


def codes_kernel(other, acts, b, out, turned):
    core, half = lax.axis_index("core"), turned.shape[1]

    @pl.when(pl.program_id(0) == 0)
    def _():
        which = 1 - core if other else core
        turned[...] = acts[pl.ds(pl.multiple_of(which * half, half), half), :].T

    out[...] = dot(b[...], turned[...])


def codes_call(other, acts, proj_b):
    (tokens, wide), rank = acts.shape, proj_b.shape[0]
    half, step = tokens // 2, 512
    return pl.pallas_call(
        functools.partial(codes_kernel, other),
        grid=(rank // step,),
        out_shape=like((rank, half), F32),
        in_specs=[
            pl.BlockSpec((tokens, wide), lambda i: (0, 0)),
            pl.BlockSpec((step, wide), lambda i: (i, 0)),
        ],
        out_specs=pl.BlockSpec((step, half), lambda i: (i, 0)),
        scratch_shapes=[pltpu.VMEM((wide, half), BF)],
        compiler_params=pltpu.CompilerParams(vmem_limit_bytes=32 * 1024 * 1024),
        cost_estimate=pl.CostEstimate(
            flops=2 * rank * wide * half, bytes_accessed=2 * rank * wide, transcendentals=0
        ),
    )(acts, proj_b)


def sum_and_copy(blocks, out):
    value = total(blocks).astype(BF)
    for i in range(out.shape[0]):
        out[i] = value


def residual_kernel(codes, near, far, a0, a1, own, message, partial, held):
    rank, outs = codes.shape[0], a0.shape[0]
    step = 256
    for j, (target, a) in enumerate(((near, a0), (far, a1))):
        for at in range(0, outs, step):
            rows = slice(at, at + step)
            left = target[rows].astype(F32) - dot(a[rows], codes[...])
            left = left.astype(BF).T
            held[:, j * outs + at : j * outs + at + step] = left
            (own if j == 0 else message)[:, rows] = left
    sub = partial.shape[1]
    for at in range(0, rank, 512):
        cols = slice(at, at + 512)
        term = dot(held[:, :outs], a0[:, cols]) + dot(held[:, outs:], a1[:, cols])
        for i in range(partial.shape[0]):
            partial[i, :, cols] = term[i * sub : (i + 1) * sub].astype(BF)


def spread_kernel(blocks, out, held):
    y_lo = lax.axis_index("y_lo")
    held[...] = total(blocks).astype(BF)
    rank = held.shape[1]
    width = rank // 8
    for at, side in ((0, 1 - y_lo), (width, y_lo)):
        for x in range(4):
            start = pl.multiple_of(side * (rank // 2) + x * width, width)
            piece = held[:, pl.ds(start, width)]
            for i in range(out.shape[1]):
                out[x, i, :, at : at + width] = piece


def last_kernel(side, other, grad, acts, *refs):
    before, (out, turned) = refs[:-2], refs[-2:]
    core = lax.axis_index("core")
    half, wide, width = grad.shape[1], acts.shape[2], out.shape[0]
    rows = pl.ds(pl.multiple_of((1 - core if other else core) * half, half), half)
    for k in range(4):
        turned[k] = grad[k, :, side * width : (side + 1) * width].T
    for ref in before[1:]:
        out[:, wide:] = ref[...]
    for c in range(0, wide, 256):
        cols = slice(c, c + 256)
        acc = dot(turned[0], acts[0, rows, cols])
        for k in range(1, 4):
            acc = acc + dot(turned[k], acts[k, rows, cols])
        if other:
            acc = acc + before[0][:, cols]
        out[:, cols] = acc.astype(out.dtype)


def last_call(grad_m, grad_o, held, side, dtype, *joined):
    _, tokens, wide = held.shape
    half, width = tokens // 2, grad_m.shape[2] // 2
    scratch = [pltpu.VMEM((4, width, half), BF)]
    flops = 4 * tokens * width * wide
    first = call(
        functools.partial(last_kernel, side, False),
        [like((width, wide), F32)],
        grad_m, held, scratch=scratch, flops=flops,
    )
    return call(
        functools.partial(last_kernel, side, True),
        [like((width, wide + sum(j.shape[1] for j in joined)), dtype)],
        grad_o, held, first, *joined, scratch=scratch, flops=flops,
    )


def term_kernel(codes, own, codes_o, message, keep, s1, s2, s3):
    x = lax.axis_index("x")
    rank, outs = codes.shape[0], own.shape[1]
    width = rank // 8
    for k, out in enumerate((keep, s1, s2, s3)):
        for side in range(2):
            start = side * (rank // 2) + lax.rem(x + k, 4) * width
            rows = pl.ds(pl.multiple_of(start, width), width)
            left, right = codes[rows, :], codes_o[rows, :]
            for c in range(0, outs, 256):
                acc = dot(left, own[:, c : c + 256])
                acc = acc + dot(right, message[:, c : c + 256])
                out[side, :, c : c + 256] = acc.astype(out.dtype)


def term_sum_kernel(keep, r1, r2, r3, own, away):
    y_lo = lax.axis_index("y_lo")
    for out, side in ((own, y_lo), (away, 1 - y_lo)):
        value = keep[side]
        for r in (r1, r2, r3):
            value = value + r[side].astype(F32)
        out[...] = value.astype(out.dtype)


def local(acts, target, proj_b, proj_a):
    core = lax.axis_index("core")
    tokens, rank = acts.shape[0], proj_b.shape[0]
    outs, wide = target.shape[1], acts.shape[1]
    half, sub, width = tokens // 2, tokens // 16, rank // 8
    scale = -2.0 / (tokens * 8)

    def part_of(array, which, size, axis):
        return lax.dynamic_slice_in_dim(array, which * size, size, axis)

    row = lax.all_gather(acts, "x")
    pair_a = swap(proj_a, "core")
    target_t = target.T
    near_t = part_of(target_t, core, half, 1)
    pair_t = swap(part_of(target_t, 1 - core, half, 1), "core")

    arrived = swap(codes_call(True, acts, proj_b), "core")
    mine = (codes_call(False, acts, proj_b) + arrived).astype(BF).reshape(8, width, half)
    blocks = lax.all_to_all(mine, ZY, 0, 0)
    codes = call(sum_and_copy, [like((8, width, half))], blocks)
    codes = lax.all_to_all(codes, ZY, 0, 0).reshape(rank, half)

    own, message, partial = call(
        residual_kernel,
        [like((half, outs)), like((half, outs)), like((8, sub, rank))],
        codes, near_t, pair_t, proj_a, pair_a,
        scratch=[pltpu.VMEM((half, 2 * outs), BF)],
        flops=8 * half * rank * outs,
    )
    partial, codes = lax.optimization_barrier((partial, codes))
    codes_o = swap(codes, "core")
    blocks = lax.all_to_all(partial, ZY, 0, 0)

    piece = like((2, width, outs))
    terms = call(
        term_kernel,
        [like(piece.shape, F32), piece, piece, piece],
        codes, own, codes_o, swap(message, "core"),
        flops=2 * tokens * rank * outs,
    )
    terms = [terms[0]] + [shift(terms[k], "x", 4, k) for k in (1, 2, 3)]

    barrier = lax.optimization_barrier
    blocks, row, terms[0] = barrier((blocks, row, terms[0]))
    split = call(spread_kernel, [like((4, 8, sub, 2 * width))], blocks, scratch=[pltpu.VMEM((sub, rank), BF)], flops=15 * 10**9)
    grad = lax.all_to_all(split.reshape(32, sub, 2 * width), ("x", "z", "y_hi"), 0, 0)
    grad = grad.reshape(4, half, 2 * width)
    grad_o = swap(grad, "core")
    away = last_call(grad, grad_o, row, 0, BF)
    away = swap(away, "y_lo").astype(F32)
    here = last_call(grad, grad_o, row, 1, F32)
    term_o, term_a = call(term_sum_kernel, [like((width, outs), F32), like((width, outs))], *terms)
    term_a = swap(term_a, "y_lo").astype(F32)
    grad_b, term_o = barrier(((here + away) * scale, term_o))
    return (((term_o + term_a) * scale).T, grad_b)


def solution(mesh):
    fine = Mesh(np.reshape(mesh.devices, (2, 4, 4, 2, 2)), ("y_lo", "x", "z", "y_hi", "core"))
    return jax.shard_map(
        local,
        mesh=fine,
        in_specs=(P(TOK, CHAN), P(TOK, CHAN), P(None, CHAN), P(CHAN, None)),
        out_specs=(P(CHAN, TOK), P(TOK, CHAN)),
        check_vma=False,
    )
```
